32 devices in a mesh: dp: 8 (over y, x, core), tensor: 4 (over z).
Axes of the slice: x: 2, y: 2, z: 4, core: 2. Of those that a mesh axis runs over, the one named last changes fastest.
Arguments:
- queries: bfloat16 [2048, 6144], P(('dp', 'tensor')), may hold values from -24 to 24
- key_vectors: bfloat16 [2048, 6144], P(('dp', 'tensor')), may hold values from -24 to 24
- value_vectors: bfloat16 [2048, 6144], P(('dp', 'tensor')), may hold values from -6 to 6
- grad_output: bfloat16 [2048, 6144], P(('dp', 'tensor')), may hold values from -6 to 6
- image_ids: int32 [2048], replicated, may hold values from 0 to 31, as said below
Outputs:
- attended: bfloat16 [2048, 6144], P('dp', 'tensor')
- grad_queries: bfloat16 [2048, 6144], P('dp', 'tensor')
- grad_keys: bfloat16 [2048, 6144], P('dp', 'tensor')
- grad_values: bfloat16 [2048, 6144], P('dp', 'tensor')
The draws below stay inside these ranges and needn't reach their ends.
Inputs may be any that keep to these rules, and one draw needn't show every extreme that they name: `image_ids`: A patch's id is the index of its image's last block of 64 rows, so ids never fall along the rows; every image covers whole blocks of 64 rows and lies within one aligned block of 256 rows or two consecutive ones; images have 64 to 384 rows, and both ends are reached in every draw.
All inputs are finite; a program needn't handle non-finite values.
Results may differ from the reference program's by a relative error of at most 0.0068.
Values may be sent and summed in bfloat16 or wider, within the bound.
No kernel may reach another device: no remote copies, remote signals or barrier semaphores. Data moves between devices by JAX's collectives and lax.ppermute only.
A program may use at most 64 MiB of HBM per device.

```python
import math
import jax
import jax.numpy as jnp
from jax import lax

HEADS = 48
HD = 128
BLOCK = 64
ROWS_DEV = 256
TOKENS = 2048
WIDTH = 6144
N_DP = 8


def draw_queries(key, part):
    own_key = jax.random.fold_in(key, 1)
    full_shape = (TOKENS, HEADS * HD)
    result = jax.random.normal(own_key, full_shape, jnp.float32)
    return jnp.clip(result, -24.0, 24.0).astype(jnp.bfloat16)


def draw_key_vectors(key, part):
    own_key = jax.random.fold_in(key, 2)
    full_shape = (TOKENS, HEADS * HD)
    result = jax.random.normal(own_key, full_shape, jnp.float32)
    return jnp.clip(result, -24.0, 24.0).astype(jnp.bfloat16)


def draw_image_ids(key, part):
    key = jax.random.fold_in(key, 7)
    shard_total = TOKENS // ROWS_DEV
    per_shard = ROWS_DEV // BLOCK
    cuts = (jax.random.randint(key, (shard_total, per_shard), 0, 3) == 0).astype(jnp.int32)
    column = jnp.arange(per_shard, dtype=jnp.int32)[None, :]
    shard_number = jnp.arange(shard_total, dtype=jnp.int32)[:, None]
    cuts = jnp.maximum(cuts, (column == 1).astype(jnp.int32))
    first_pattern = (column <= 1).astype(jnp.int32) + 0 * shard_number
    second_pattern = (column == per_shard - 1).astype(jnp.int32) + 0 * shard_number
    cuts = jnp.where(shard_number == 0, first_pattern, jnp.where(shard_number == 1, second_pattern, jnp.where(shard_number == 2, 1, cuts)))
    middle = shard_total // 2
    joined = ((shard_number == middle) | (shard_number == middle + 1)) & (column == 0)
    cuts = jnp.where(joined, 0, cuts)
    flat_cuts = cuts.reshape(-1)
    block_total = shard_total * per_shard
    block_number = jnp.arange(block_total, dtype=jnp.int32)
    next_cut = jnp.concatenate((flat_cuts[1:], jnp.ones((1,), jnp.int32)))
    candidate = jnp.where(next_cut == 1, block_number, block_total)
    last_block = lax.cummin(candidate, axis=0, reverse=True)
    return jnp.repeat(last_block, BLOCK, total_repeat_length=TOKENS).astype(jnp.int32)


def levels(key, extent, split, least, largest):
    loudness, own = 1.0, jax.random.fold_in(key, 6)
    for dim, shards_of in split:
        draws = jnp.exp(jax.random.uniform(jax.random.fold_in(own, dim), (shards_of,), jnp.float32, least / len(split), largest / len(split)))
        loudness = loudness * jnp.repeat(draws, extent[dim] // shards_of).reshape([-1 if axis == dim else 1 for axis in range(len(extent))])
    return loudness


def centred(stream_key, dims, width, most, split=(), held_as=jnp.bfloat16):
    loudness = levels(stream_key, dims, split, -0.22, 0.18) if split else 1.0
    values = jax.random.normal(stream_key, dims, jnp.float32) * width * loudness
    return jnp.minimum(jnp.maximum(values, -most), most).astype(held_as)


def setup_inputs(seed: int = 0) -> dict:
    key_of = jax.random.split(jax.random.key(seed), 6)
    return {
        "queries": draw_queries(jax.random.fold_in(key_of[5], 71), 0),
        "key_vectors": draw_key_vectors(jax.random.fold_in(key_of[5], 71), 0),
        "value_vectors": centred(key_of[2], (TOKENS, WIDTH), 1.0, 6.0, ((0, 32),)),
        "grad_output": centred(key_of[3], (TOKENS, WIDTH), 1.0, 6.0, ((0, 32),)),
        "image_ids": draw_image_ids(jax.random.fold_in(key_of[5], 71), 0),
    }


def shard_rows(array, start, length):
    return lax.dynamic_slice_in_dim(array, start, length, 0)

def split_heads(array):
    return array.astype(jnp.float32).reshape(array.shape[0], HEADS, HD)

def rounded(array):
    low = array.astype(jnp.bfloat16)
    low = lax.optimization_barrier(low)
    return low.astype(jnp.float32)

def reference(queries, key_vectors, value_vectors, grad_output, image_ids):
    row_count = ROWS_DEV
    score_scale = 1.0 / math.sqrt(HD)
    margin = ((row_count, row_count), (0, 0))
    query_pad = jnp.pad(queries, margin)
    key_pad = jnp.pad(key_vectors, margin)
    value_pad = jnp.pad(value_vectors, margin)
    grad_pad = jnp.pad(grad_output, margin)
    id_pad = jnp.pad(image_ids, (row_count, row_count), constant_values=-1)
    shard_list = jnp.arange(N_DP, dtype=jnp.int32)

    def forward_shard(shard):
        here = (shard + 1) * row_count
        nearby = shard * row_count
        query_part = split_heads(shard_rows(query_pad, here, row_count))
        grad_part = split_heads(shard_rows(grad_pad, here, row_count))
        key_part = split_heads(shard_rows(key_pad, nearby, 3 * row_count))
        value_part = split_heads(shard_rows(value_pad, nearby, 3 * row_count))
        same_image = shard_rows(id_pad, here, row_count)[:, None] == shard_rows(id_pad, nearby, 3 * row_count)[None, :]
        scores = jnp.einsum('qhd,khd->hqk', query_part, key_part) * score_scale
        scores = jnp.where(same_image[None], scores, -1e+30)
        row_max = lax.optimization_barrier(jnp.max(scores, axis=2, keepdims=True))
        weights = jnp.exp(scores - row_max)
        row_total = lax.optimization_barrier(jnp.sum(weights, axis=2, keepdims=True))
        probs = weights / row_total
        probs_low = rounded(probs)
        attended = jnp.einsum('hqk,khd->qhd', probs_low, value_part)
        grad_probs = jnp.einsum('qhd,khd->hqk', grad_part, value_part)
        inner = lax.optimization_barrier(jnp.sum(probs * grad_probs, axis=2, keepdims=True))
        grad_scores = rounded(probs * (grad_probs - inner))
        grad_query = jnp.einsum('hqk,khd->qhd', grad_scores, key_part) * score_scale
        return (attended.reshape(row_count, WIDTH).astype(jnp.bfloat16), grad_query.reshape(row_count, WIDTH).astype(jnp.bfloat16), row_max[:, :, 0], row_total[:, :, 0], inner[:, :, 0])
    attended, grad_queries, maxima, totals, inners = lax.map(forward_shard, shard_list)
    shard_margin = ((1, 1), (0, 0), (0, 0))
    max_pad = jnp.pad(maxima, shard_margin, constant_values=0.0)
    total_pad = jnp.pad(totals, shard_margin, constant_values=1.0)
    inner_pad = jnp.pad(inners, shard_margin, constant_values=0.0)

    def gather_stat(padded, shard):
        window = lax.dynamic_slice_in_dim(padded, shard, 3, 0)
        return jnp.transpose(window, (1, 0, 2)).reshape(HEADS, 3 * row_count)

    def backward_shard(shard):
        here = (shard + 1) * row_count
        nearby = shard * row_count
        key_part = split_heads(shard_rows(key_pad, here, row_count))
        value_part = split_heads(shard_rows(value_pad, here, row_count))
        query_part = split_heads(shard_rows(query_pad, nearby, 3 * row_count))
        grad_part = split_heads(shard_rows(grad_pad, nearby, 3 * row_count))
        same_image = shard_rows(id_pad, nearby, 3 * row_count)[:, None] == shard_rows(id_pad, here, row_count)[None, :]
        row_max = gather_stat(max_pad, shard)[:, :, None]
        row_total = gather_stat(total_pad, shard)[:, :, None]
        inner = gather_stat(inner_pad, shard)[:, :, None]
        scores = jnp.einsum('qhd,khd->hqk', query_part, key_part) * score_scale
        scores = jnp.where(same_image[None], scores, -1e+30)
        probs = jnp.exp(scores - row_max) / row_total
        probs_low = rounded(probs)
        grad_probs = jnp.einsum('qhd,khd->hqk', grad_part, value_part)
        grad_scores = rounded(probs * (grad_probs - inner))
        grad_key = jnp.einsum('hqk,qhd->khd', grad_scores, query_part) * score_scale
        grad_value = jnp.einsum('hqk,qhd->khd', probs_low, grad_part)
        return (grad_key.reshape(row_count, WIDTH).astype(jnp.bfloat16), grad_value.reshape(row_count, WIDTH).astype(jnp.bfloat16))
    grad_keys, grad_values = lax.map(backward_shard, shard_list)
    return (attended.reshape(TOKENS, WIDTH), grad_queries.reshape(TOKENS, WIDTH), grad_keys.reshape(TOKENS, WIDTH), grad_values.reshape(TOKENS, WIDTH))
```

```python
import functools
import math

import jax
import jax.numpy as jnp
from jax import lax
from jax.experimental import pallas as pl
from jax.experimental.pallas import tpu as pltpu
from jax.sharding import PartitionSpec as P

HD = 128
SCALE = 1.0 / math.sqrt(HD)
EXP2_SCALE = SCALE * math.log2(math.e)
MASKED = -1e30
CHUNK_SHARES = (4, 4, 4)
VMEM_LIMIT = 48 * 1024 * 1024


def split_counts(total, shares):
    whole = sum(shares)
    edges = [round(total * sum(shares[:i]) / whole) for i in range(len(shares) + 1)]
    return [(a, b - a) for a, b in zip(edges[:-1], edges[1:]) if b > a]


def shift(block, axis, distance):
    count = lax.axis_size(axis)
    route = [(i, i + distance) for i in range(count) if 0 <= i + distance < count]
    return lax.ppermute(block, axis, route)


def pack_kernel(parts, first, width, stride, *refs):
    arrays, packed, sems = refs[:4], refs[4], refs[5]
    copies = []
    for part in range(parts):
        for index, array in enumerate(arrays):
            copy = pltpu.make_async_copy(
                array.at[:, pl.ds(part * stride + first, width)],
                packed.at[part, index],
                sems.at[part * 4 + index],
            )
            copy.start()
            copies.append(copy)
    for copy in copies:
        copy.wait()


def pack(arrays, parts, first, width):
    rows, total = arrays[0].shape
    return pl.pallas_call(
        functools.partial(pack_kernel, parts, first, width, total // parts),
        out_shape=jax.ShapeDtypeStruct((parts, 4, rows, width), jnp.bfloat16),
        in_specs=[pl.BlockSpec(memory_space=pl.ANY)] * 4,
        out_specs=pl.BlockSpec(memory_space=pl.ANY),
        scratch_shapes=[pltpu.SemaphoreType.DMA((parts * 4,))],
        cost_estimate=pl.CostEstimate(
            flops=0, bytes_accessed=parts * 16 * rows * width, transcendentals=0
        ),
    )(*arrays)


def dot_nt(a, b):
    return lax.dot_general(a, b, (((1,), (1,)), ((), ())), preferred_element_type=jnp.float32)


def dot_tn(a, b):
    return lax.dot_general(a, b, (((0,), (0,)), ((), ())), preferred_element_type=jnp.float32)


def dot_nn(a, b):
    return jnp.dot(a, b, preferred_element_type=jnp.float32)


def probs_and_grads(queries, grads, keys, values, bias):
    scores = dot_nt(queries, keys) + bias
    row_max = jnp.max(scores, axis=1, keepdims=True)
    weights = jnp.exp2((scores - row_max) * EXP2_SCALE)
    probs = weights * (1.0 / jnp.sum(weights, axis=1, keepdims=True))
    grad_probs = dot_nt(grads, values)
    inner = jnp.sum(probs * grad_probs, axis=1, keepdims=True)
    grad_scores = probs * (grad_probs - inner)
    return probs.astype(jnp.bfloat16), grad_scores.astype(jnp.bfloat16)


def attend_kernel(rows, has_outs, *refs):
    row_ids, col_ids, own, left, right = refs[:5]
    refs = refs[5 + (4 if has_outs else 0) :]
    attended, grad_q, grad_k, grad_v, bias_own, bias_left, bias_right = refs

    @pl.when(pl.program_id(0) == 0)
    def _():
        def bias(row_start, col_start, col_count):
            same = (
                row_ids[row_start : row_start + rows, :]
                == col_ids[:, col_start : col_start + col_count]
            )
            return jnp.where(same, 0.0, MASKED)

        bias_own[...] = bias(rows, 0, 3 * rows)
        bias_left[...] = bias(0, 0, 2 * rows)
        bias_right[...] = bias(2 * rows, rows, 2 * rows)

    def load(ref, index):
        return ref[:, index].reshape(rows, HD)

    q_l, k_l, v_l, g_l = (load(left, i) for i in range(4))
    q_o, k_o, v_o, g_o = (load(own, i) for i in range(4))
    q_r, k_r, v_r, g_r = (load(right, i) for i in range(4))

    k_all = jnp.concatenate((k_l, k_o, k_r))
    v_all = jnp.concatenate((v_l, v_o, v_r))
    p, s = probs_and_grads(q_o, g_o, k_all, v_all, bias_own[...])
    attended[...] = dot_nn(p, v_all).astype(jnp.bfloat16)
    grad_q[...] = (dot_nn(s, k_all) * SCALE).astype(jnp.bfloat16)
    p_o, s_o = p[:, rows : 2 * rows], s[:, rows : 2 * rows]
    p_l, s_l = probs_and_grads(
        q_l, g_l, k_all[: 2 * rows], v_all[: 2 * rows], bias_left[...]
    )
    p_r, s_r = probs_and_grads(q_r, g_r, k_all[rows:], v_all[rows:], bias_right[...])
    p_l, s_l = p_l[:, rows:], s_l[:, rows:]
    p_r, s_r = p_r[:, :rows], s_r[:, :rows]
    grad_v[...] = (dot_tn(p_l, g_l) + dot_tn(p_o, g_o) + dot_tn(p_r, g_r)).astype(jnp.bfloat16)
    grad_k[...] = (
        (dot_tn(s_l, q_l) + dot_tn(s_o, q_o) + dot_tn(s_r, q_r)) * SCALE
    ).astype(jnp.bfloat16)


def attend(ids, own, left, right, outs, first_head, head_total):
    parts, _, part_rows, width = own.shape
    rows = parts * part_rows
    heads = width // HD
    block = pl.BlockSpec((parts, 4, part_rows, HD), lambda h: (0, 0, 0, h))
    whole = pl.BlockSpec(memory_space=pltpu.VMEM)
    out_spec = pl.BlockSpec((rows, HD), lambda h: (0, h + first_head))
    has_outs = outs is not None
    aliases = {5 + i: i for i in range(4)} if has_outs else {}
    return pl.pallas_call(
        functools.partial(attend_kernel, rows, has_outs),
        grid=(heads,),
        out_shape=[jax.ShapeDtypeStruct((rows, head_total * HD), jnp.bfloat16)] * 4,
        in_specs=[whole, whole, block, block, block]
        + ([pl.BlockSpec(memory_space=pl.ANY)] * 4 if has_outs else []),
        out_specs=[out_spec] * 4,
        scratch_shapes=[
            pltpu.VMEM((rows, 3 * rows), jnp.float32),
            pltpu.VMEM((rows, 2 * rows), jnp.float32),
            pltpu.VMEM((rows, 2 * rows), jnp.float32),
        ],
        input_output_aliases=aliases,
        compiler_params=pltpu.CompilerParams(
            dimension_semantics=("arbitrary",), vmem_limit_bytes=VMEM_LIMIT
        ),
        cost_estimate=pl.CostEstimate(
            flops=heads * 26 * 2 * rows * rows * HD,
            bytes_accessed=heads * 16 * 2 * rows * HD,
            transcendentals=heads * 7 * rows * rows,
        ),
    )(ids[:, None], ids[None, :], own, left, right, *(outs or ()))


def shards(queries, key_vectors, value_vectors, grad_output, image_ids):
    arrays = (queries, key_vectors, value_vectors, grad_output)
    parts = lax.axis_size("tensor")
    rows = queries.shape[0] * parts
    head_total = queries.shape[1] // HD // parts
    padded_ids = jnp.pad(image_ids, (rows, rows), constant_values=-1)
    ids = lax.dynamic_slice_in_dim(padded_ids, lax.axis_index("dp") * rows, 3 * rows)
    outs = None
    for first, count in split_counts(head_total, CHUNK_SHARES):
        packed = pack(arrays, parts, first * HD, count * HD)
        own = lax.all_to_all(packed, "tensor", split_axis=0, concat_axis=0, tiled=True)
        left = shift(own, "dp", 1)
        right = shift(own, "dp", -1)
        outs = attend(ids, own, left, right, outs, first, head_total)
    return tuple(outs)


def solution(mesh):
    return jax.shard_map(
        shards,
        mesh=mesh,
        in_specs=(
            P(("dp", "tensor"), None),
            P(("dp", "tensor"), None),
            P(("dp", "tensor"), None),
            P(("dp", "tensor"), None),
            P(),
        ),
        out_specs=(P("dp", "tensor"), P("dp", "tensor"), P("dp", "tensor"), P("dp", "tensor")),
        check_vma=False,
    )
```

```python
import functools
import math

import jax
import jax.numpy as jnp
from jax import lax
from jax.experimental import pallas as pl
from jax.experimental.pallas import tpu as pltpu
from jax.sharding import PartitionSpec as P

HD = 128
SCALE = 1.0 / math.sqrt(HD)
EXP2_SCALE = SCALE * math.log2(math.e)
MASKED = -1e30
CHUNK_SHARES = (4, 4, 4)
VMEM_LIMIT = 48 * 1024 * 1024


def split_counts(total, shares):
    whole = sum(shares)
    edges = [round(total * sum(shares[:i]) / whole) for i in range(len(shares) + 1)]
    return [(a, b - a) for a, b in zip(edges[:-1], edges[1:]) if b > a]


def shift(block, axis, distance):
    count = lax.axis_size(axis)
    route = [(i, i + distance) for i in range(count) if 0 <= i + distance < count]
    return lax.ppermute(block, axis, route)


def pack_kernel(*refs):
    packed = refs[4]
    for index, array in enumerate(refs[:4]):
        packed[0, index] = array[...]


def pack(arrays, parts, first, count):
    rows, total = arrays[0].shape
    heads = total // parts // HD
    width = math.gcd(first, math.gcd(count, heads)) * HD
    steps = count * HD // width
    in_spec = pl.BlockSpec(
        (rows, width), lambda p, s: (0, p * (heads * HD // width) + first * HD // width + s)
    )
    return pl.pallas_call(
        pack_kernel,
        grid=(parts, steps),
        out_shape=jax.ShapeDtypeStruct((parts, 4, rows, count * HD), jnp.bfloat16),
        in_specs=[in_spec] * 4,
        out_specs=pl.BlockSpec((1, 4, rows, width), lambda p, s: (p, 0, 0, s)),
        compiler_params=pltpu.CompilerParams(
            dimension_semantics=("arbitrary", "arbitrary"), vmem_limit_bytes=VMEM_LIMIT
        ),
        cost_estimate=pl.CostEstimate(
            flops=0, bytes_accessed=parts * 16 * rows * count * HD, transcendentals=0
        ),
    )(*arrays)


def dot_nt(a, b):
    return lax.dot_general(a, b, (((1,), (1,)), ((), ())), preferred_element_type=jnp.float32)


def dot_tn(a, b):
    return lax.dot_general(a, b, (((0,), (0,)), ((), ())), preferred_element_type=jnp.float32)


def dot_nn(a, b):
    return jnp.dot(a, b, preferred_element_type=jnp.float32)


def probs_and_grads(queries, grads, keys, values, bias):
    scores = dot_nt(queries, keys) + bias
    row_max = jnp.max(scores, axis=1, keepdims=True)
    weights = jnp.exp2((scores - row_max) * EXP2_SCALE)
    probs = weights * (1.0 / jnp.sum(weights, axis=1, keepdims=True))
    grad_probs = dot_nt(grads, values)
    inner = jnp.sum(probs * grad_probs, axis=1, keepdims=True)
    grad_scores = probs * (grad_probs - inner)
    return probs.astype(jnp.bfloat16), grad_scores.astype(jnp.bfloat16)


def attend_kernel(rows, has_outs, *refs):
    row_ids, col_ids, own, left, right = refs[:5]
    refs = refs[5 + (4 if has_outs else 0) :]
    attended, grad_q, grad_k, grad_v, bias_own, bias_left, bias_right = refs

    @pl.when(pl.program_id(0) == 0)
    def _():
        def bias(row_start, col_start, col_count):
            same = (
                row_ids[row_start : row_start + rows, :]
                == col_ids[:, col_start : col_start + col_count]
            )
            return jnp.where(same, 0.0, MASKED)

        bias_own[...] = bias(rows, 0, 3 * rows)
        bias_left[...] = bias(0, 0, 2 * rows)
        bias_right[...] = bias(2 * rows, rows, 2 * rows)

    def load(ref, index):
        return ref[:, index].reshape(rows, HD)

    q_l, k_l, v_l, g_l = (load(left, i) for i in range(4))
    q_o, k_o, v_o, g_o = (load(own, i) for i in range(4))
    q_r, k_r, v_r, g_r = (load(right, i) for i in range(4))

    k_all = jnp.concatenate((k_l, k_o, k_r))
    v_all = jnp.concatenate((v_l, v_o, v_r))
    p, s = probs_and_grads(q_o, g_o, k_all, v_all, bias_own[...])
    attended[...] = dot_nn(p, v_all).astype(jnp.bfloat16)
    grad_q[...] = (dot_nn(s, k_all) * SCALE).astype(jnp.bfloat16)
    p_o, s_o = p[:, rows : 2 * rows], s[:, rows : 2 * rows]
    p_l, s_l = probs_and_grads(
        q_l, g_l, k_all[: 2 * rows], v_all[: 2 * rows], bias_left[...]
    )
    p_r, s_r = probs_and_grads(q_r, g_r, k_all[rows:], v_all[rows:], bias_right[...])
    p_l, s_l = p_l[:, rows:], s_l[:, rows:]
    p_r, s_r = p_r[:, :rows], s_r[:, :rows]
    grad_v[...] = (dot_tn(p_l, g_l) + dot_tn(p_o, g_o) + dot_tn(p_r, g_r)).astype(jnp.bfloat16)
    grad_k[...] = (
        (dot_tn(s_l, q_l) + dot_tn(s_o, q_o) + dot_tn(s_r, q_r)) * SCALE
    ).astype(jnp.bfloat16)


def attend(ids, own, left, right, outs, first_head, head_total):
    parts, _, part_rows, width = own.shape
    rows = parts * part_rows
    heads = width // HD
    block = pl.BlockSpec((parts, 4, part_rows, HD), lambda h: (0, 0, 0, h))
    whole = pl.BlockSpec(memory_space=pltpu.VMEM)
    out_spec = pl.BlockSpec((rows, HD), lambda h: (0, h + first_head))
    has_outs = outs is not None
    aliases = {5 + i: i for i in range(4)} if has_outs else {}
    return pl.pallas_call(
        functools.partial(attend_kernel, rows, has_outs),
        grid=(heads,),
        out_shape=[jax.ShapeDtypeStruct((rows, head_total * HD), jnp.bfloat16)] * 4,
        in_specs=[whole, whole, block, block, block]
        + ([pl.BlockSpec(memory_space=pl.ANY)] * 4 if has_outs else []),
        out_specs=[out_spec] * 4,
        scratch_shapes=[
            pltpu.VMEM((rows, 3 * rows), jnp.float32),
            pltpu.VMEM((rows, 2 * rows), jnp.float32),
            pltpu.VMEM((rows, 2 * rows), jnp.float32),
        ],
        input_output_aliases=aliases,
        compiler_params=pltpu.CompilerParams(
            dimension_semantics=("arbitrary",), vmem_limit_bytes=VMEM_LIMIT
        ),
        cost_estimate=pl.CostEstimate(
            flops=heads * 26 * 2 * rows * rows * HD,
            bytes_accessed=heads * 16 * 2 * rows * HD,
            transcendentals=heads * 7 * rows * rows,
        ),
    )(ids[:, None], ids[None, :], own, left, right, *(outs or ()))


def shards(queries, key_vectors, value_vectors, grad_output, image_ids):
    arrays = (queries, key_vectors, value_vectors, grad_output)
    parts = lax.axis_size("tensor")
    rows = queries.shape[0] * parts
    head_total = queries.shape[1] // HD // parts
    padded_ids = jnp.pad(image_ids, (rows, rows), constant_values=-1)
    ids = lax.dynamic_slice_in_dim(padded_ids, lax.axis_index("dp") * rows, 3 * rows)
    outs = None
    for first, count in split_counts(head_total, CHUNK_SHARES):
        packed = pack(arrays, parts, first, count)
        own = lax.all_to_all(packed, "tensor", split_axis=0, concat_axis=0, tiled=True)
        left = shift(own, "dp", 1)
        right = shift(own, "dp", -1)
        outs = attend(ids, own, left, right, outs, first, head_total)
    return tuple(outs)


def solution(mesh):
    return jax.shard_map(
        shards,
        mesh=mesh,
        in_specs=(
            P(("dp", "tensor"), None),
            P(("dp", "tensor"), None),
            P(("dp", "tensor"), None),
            P(("dp", "tensor"), None),
            P(),
        ),
        out_specs=(P("dp", "tensor"), P("dp", "tensor"), P("dp", "tensor"), P("dp", "tensor")),
        check_vma=False,
    )
```

```python
import functools
import math

import jax
import jax.numpy as jnp
from jax import lax
from jax.experimental import pallas as pl
from jax.experimental.pallas import tpu as pltpu
from jax.sharding import PartitionSpec as P

HD = 128
SCALE = 1.0 / math.sqrt(HD)
EXP2_SCALE = SCALE * math.log2(math.e)
MASKED = -1e30
CHUNKS = (("all", 4), ("pairs", 2), ("all", 4), ("pairs", 2))
VMEM_LIMIT = 60 * 1024 * 1024
SMALL_COST = pl.CostEstimate(flops=1, bytes_accessed=1, transcendentals=0)


def split_counts(total, shares):
    whole = sum(shares)
    edges = [round(total * sum(shares[:i]) / whole) for i in range(len(shares) + 1)]
    return [(a, b - a) for a, b in zip(edges[:-1], edges[1:]) if b > a]


def shift(block, axis, distance):
    count = lax.axis_size(axis)
    route = [(i, i + distance) for i in range(count) if 0 <= i + distance < count]
    return lax.ppermute(block, axis, route)


def swap(block, axis, flip):
    route = [(i, i ^ flip) for i in range(lax.axis_size(axis))]
    return lax.ppermute(block, axis, route)


def columns(array, part, stride, first, width):
    start = pl.multiple_of(part * stride + first, HD)
    return array.at[:, pl.ds(start, width)]


def pack_kernel(parts, stride, first, width, deps, *refs):
    arrays, refs = refs[:4], refs[4 + deps :]
    packed, (stage, in_sems, out_sems) = refs[: parts - 1], refs[parts - 1 :]
    me = lax.axis_index("tensor")
    loads, stores = [], []
    for flip in range(1, parts):
        for index, array in enumerate(arrays):
            load = pltpu.make_async_copy(
                columns(array, me ^ flip, stride, first, width),
                stage.at[flip - 1, index],
                in_sems.at[(flip - 1) * 4 + index],
            )
            load.start()
            loads.append(load)
    for flip in range(1, parts):
        for load in loads[(flip - 1) * 4 : flip * 4]:
            load.wait()
        store = pltpu.make_async_copy(
            stage.at[flip - 1], packed[flip - 1], out_sems.at[flip - 1]
        )
        store.start()
        stores.append(store)
    for store in stores:
        store.wait()


def pack(arrays, parts, first, count, after):
    rows, total = arrays[0].shape
    width = count * HD
    return pl.pallas_call(
        functools.partial(
            pack_kernel, parts, total // parts, first * HD, width, len(after)
        ),
        out_shape=[jax.ShapeDtypeStruct((4, rows, width), jnp.bfloat16)] * (parts - 1),
        in_specs=[pl.BlockSpec(memory_space=pl.ANY)] * (4 + len(after)),
        out_specs=[pl.BlockSpec(memory_space=pl.ANY)] * (parts - 1),
        scratch_shapes=[
            pltpu.VMEM((parts - 1, 4, rows, width), jnp.bfloat16),
            pltpu.SemaphoreType.DMA(((parts - 1) * 4,)),
            pltpu.SemaphoreType.DMA((parts - 1,)),
        ],
        compiler_params=pltpu.CompilerParams(vmem_limit_bytes=VMEM_LIMIT),
        cost_estimate=SMALL_COST,
    )(*arrays, *after)


def pack_all_kernel(parts, stride, first, width, deps, *refs):
    arrays, (packed, stage, in_sems, out_sems) = refs[:4], refs[4 + deps :]
    loads, stores = [], []
    for part in range(parts):
        for index, array in enumerate(arrays):
            load = pltpu.make_async_copy(
                columns(array, part, stride, first, width),
                stage.at[part, index],
                in_sems.at[part * 4 + index],
            )
            load.start()
            loads.append(load)
    for part in range(parts):
        for load in loads[part * 4 : part * 4 + 4]:
            load.wait()
        store = pltpu.make_async_copy(stage.at[part], packed.at[part], out_sems.at[part])
        store.start()
        stores.append(store)
    for store in stores:
        store.wait()


def pack_all(arrays, parts, first, count, after):
    rows, total = arrays[0].shape
    width = count * HD
    return pl.pallas_call(
        functools.partial(
            pack_all_kernel, parts, total // parts, first * HD, width, len(after)
        ),
        out_shape=jax.ShapeDtypeStruct((parts, 4, rows, width), jnp.bfloat16),
        in_specs=[pl.BlockSpec(memory_space=pl.ANY)] * (4 + len(after)),
        out_specs=pl.BlockSpec(memory_space=pl.ANY),
        scratch_shapes=[
            pltpu.VMEM((parts, 4, rows, width), jnp.bfloat16),
            pltpu.SemaphoreType.DMA((parts * 4,)),
            pltpu.SemaphoreType.DMA((parts,)),
        ],
        compiler_params=pltpu.CompilerParams(vmem_limit_bytes=VMEM_LIMIT),
        cost_estimate=SMALL_COST,
    )(*arrays, *after)


def join_kernel(parts, stride, first, width, deps, *refs):
    arrays, received, refs = refs[:4], refs[4 : 3 + parts], refs[3 + parts + deps :]
    joined, stage, in_sems, out_sems = refs
    me = lax.axis_index("tensor")
    loads, stores = [], []
    for flip in range(1, parts):
        load = pltpu.make_async_copy(received[flip - 1], stage.at[flip], in_sems.at[3 + flip])
        load.start()
        loads.append([load])
    own = []
    for index, array in enumerate(arrays):
        load = pltpu.make_async_copy(
            columns(array, me, stride, first, width), stage.at[0, index], in_sems.at[index]
        )
        load.start()
        own.append(load)
    loads = [own] + loads
    for flip in range(parts):
        for load in loads[flip]:
            load.wait()
        store = pltpu.make_async_copy(stage.at[flip], joined.at[me ^ flip], out_sems.at[flip])
        store.start()
        stores.append(store)
    for store in stores:
        store.wait()


def join(arrays, received, first, after):
    parts = len(received) + 1
    rows, total = arrays[0].shape
    width = received[0].shape[2]
    return pl.pallas_call(
        functools.partial(
            join_kernel, parts, total // parts, first * HD, width, len(after)
        ),
        out_shape=jax.ShapeDtypeStruct((parts, 4, rows, width), jnp.bfloat16),
        in_specs=[pl.BlockSpec(memory_space=pl.ANY)] * (3 + parts + len(after)),
        out_specs=pl.BlockSpec(memory_space=pl.ANY),
        scratch_shapes=[
            pltpu.VMEM((parts, 4, rows, width), jnp.bfloat16),
            pltpu.SemaphoreType.DMA((parts + 3,)),
            pltpu.SemaphoreType.DMA((parts,)),
        ],
        compiler_params=pltpu.CompilerParams(vmem_limit_bytes=VMEM_LIMIT),
        cost_estimate=SMALL_COST,
    )(*arrays, *received, *after)


def dot_nt(a, b):
    return lax.dot_general(a, b, (((1,), (1,)), ((), ())), preferred_element_type=jnp.float32)


def dot_tn(a, b):
    return lax.dot_general(a, b, (((0,), (0,)), ((), ())), preferred_element_type=jnp.float32)


def dot_nn(a, b):
    return jnp.dot(a, b, preferred_element_type=jnp.float32)


def probs_and_grads(queries, grads, keys, values, bias):
    scores = dot_nt(queries, keys) + bias
    row_max = jnp.max(scores, axis=1, keepdims=True)
    weights = jnp.exp2((scores - row_max) * EXP2_SCALE)
    probs = weights * (1.0 / jnp.sum(weights, axis=1, keepdims=True))
    grad_probs = dot_nt(grads, values)
    inner = jnp.sum(probs * grad_probs, axis=1, keepdims=True)
    grad_scores = probs * (grad_probs - inner)
    return probs.astype(jnp.bfloat16), grad_scores.astype(jnp.bfloat16)


def attend_kernel(rows, has_outs, *refs):
    row_ids, col_ids, own, left, right = refs[:5]
    refs = refs[5 + (4 if has_outs else 0) :]
    attended, grad_q, grad_k, grad_v, bias_own, bias_left, bias_right = refs

    @pl.when(pl.program_id(0) == 0)
    def _():
        def bias(row_start, col_start, col_count):
            same = (
                row_ids[row_start : row_start + rows, :]
                == col_ids[:, col_start : col_start + col_count]
            )
            return jnp.where(same, 0.0, MASKED)

        bias_own[...] = bias(rows, 0, 3 * rows)
        bias_left[...] = bias(0, 0, 2 * rows)
        bias_right[...] = bias(2 * rows, rows, 2 * rows)

    def load(ref, index):
        return ref[:, index].reshape(rows, HD)

    q_l, k_l, v_l, g_l = (load(left, i) for i in range(4))
    q_o, k_o, v_o, g_o = (load(own, i) for i in range(4))
    q_r, k_r, v_r, g_r = (load(right, i) for i in range(4))

    k_all = jnp.concatenate((k_l, k_o, k_r))
    v_all = jnp.concatenate((v_l, v_o, v_r))
    p, s = probs_and_grads(q_o, g_o, k_all, v_all, bias_own[...])
    attended[...] = dot_nn(p, v_all).astype(jnp.bfloat16)
    grad_q[...] = (dot_nn(s, k_all) * SCALE).astype(jnp.bfloat16)
    p_o, s_o = p[:, rows : 2 * rows], s[:, rows : 2 * rows]
    p_l, s_l = probs_and_grads(
        q_l, g_l, k_all[: 2 * rows], v_all[: 2 * rows], bias_left[...]
    )
    p_r, s_r = probs_and_grads(q_r, g_r, k_all[rows:], v_all[rows:], bias_right[...])
    p_l, s_l = p_l[:, rows:], s_l[:, rows:]
    p_r, s_r = p_r[:, :rows], s_r[:, :rows]
    grad_v[...] = (dot_tn(p_l, g_l) + dot_tn(p_o, g_o) + dot_tn(p_r, g_r)).astype(jnp.bfloat16)
    grad_k[...] = (
        (dot_tn(s_l, q_l) + dot_tn(s_o, q_o) + dot_tn(s_r, q_r)) * SCALE
    ).astype(jnp.bfloat16)


def attend(ids, own, left, right, outs, first_head, head_total):
    parts, _, part_rows, width = own.shape
    rows = parts * part_rows
    heads = width // HD
    block = pl.BlockSpec((parts, 4, part_rows, HD), lambda h: (0, 0, 0, h))
    whole = pl.BlockSpec(memory_space=pltpu.VMEM)
    out_spec = pl.BlockSpec((rows, HD), lambda h: (0, h + first_head))
    has_outs = outs is not None
    aliases = {5 + i: i for i in range(4)} if has_outs else {}
    return pl.pallas_call(
        functools.partial(attend_kernel, rows, has_outs),
        grid=(heads,),
        out_shape=[jax.ShapeDtypeStruct((rows, head_total * HD), jnp.bfloat16)] * 4,
        in_specs=[whole, whole, block, block, block]
        + ([pl.BlockSpec(memory_space=pl.ANY)] * 4 if has_outs else []),
        out_specs=[out_spec] * 4,
        scratch_shapes=[
            pltpu.VMEM((rows, 3 * rows), jnp.float32),
            pltpu.VMEM((rows, 2 * rows), jnp.float32),
            pltpu.VMEM((rows, 2 * rows), jnp.float32),
        ],
        input_output_aliases=aliases,
        compiler_params=pltpu.CompilerParams(
            dimension_semantics=("arbitrary",), vmem_limit_bytes=VMEM_LIMIT
        ),
        cost_estimate=SMALL_COST,
    )(ids[:, None], ids[None, :], own, left, right, *(outs or ()))


def shards(queries, key_vectors, value_vectors, grad_output, image_ids):
    arrays = (queries, key_vectors, value_vectors, grad_output)
    parts = lax.axis_size("tensor")
    rows = queries.shape[0] * parts
    head_total = queries.shape[1] // HD // parts
    padded_ids = jnp.pad(image_ids, (rows, rows), constant_values=-1)
    ids = lax.dynamic_slice_in_dim(padded_ids, lax.axis_index("dp") * rows, 3 * rows)
    chunks = split_counts(head_total, [share for _, share in CHUNKS])
    outs, owns, out_history, sent = None, [], [], []

    def send(number):
        first, count = chunks[number]
        after = owns[number - 2 : number - 1] if number >= 2 else []
        if CHUNKS[number][0] == "all":
            sent.append([pack_all(arrays, parts, first, count, after)])
        else:
            sent.append(pack(arrays, parts, first, count, after))

    send(0)
    send(1)
    for number, (first, count) in enumerate(chunks):
        packed = sent[number]
        if CHUNKS[number][0] == "all":
            own = lax.all_to_all(packed[0], "tensor", split_axis=0, concat_axis=0, tiled=True)
        else:
            received = [swap(packed[flip - 1], "tensor", flip) for flip in range(1, parts)]
            after = [later[0] for later in sent[number + 1 : number + 2]]
            own = join(arrays, received, first, after)
        owns.append(own)
        if number + 2 < len(chunks):
            send(number + 2)
        left = shift(own, "dp", 1)
        right = shift(own, "dp", -1)
        outs = attend(ids, own, left, right, outs, first, head_total)
        out_history.append(outs)
    return tuple(outs)


def solution(mesh):
    return jax.shard_map(
        shards,
        mesh=mesh,
        in_specs=(
            P(("dp", "tensor"), None),
            P(("dp", "tensor"), None),
            P(("dp", "tensor"), None),
            P(("dp", "tensor"), None),
            P(),
        ),
        out_specs=(P("dp", "tensor"), P("dp", "tensor"), P("dp", "tensor"), P("dp", "tensor")),
        check_vma=False,
    )
```

```python
import functools
import math

import jax
import jax.numpy as jnp
from jax import lax
from jax.experimental import pallas as pl
from jax.experimental.pallas import tpu as pltpu
from jax.sharding import PartitionSpec as P

HD = 128
SCALE = 1.0 / math.sqrt(HD)
EXP2_SCALE = SCALE * math.log2(math.e)
MASKED = -1e30
CHUNK_SHARES = (4, 4, 3, 1)
VMEM_LIMIT = 60 * 1024 * 1024
ATTEND_FLOPS = 2_500_000_000
SMALL_COST = pl.CostEstimate(flops=1, bytes_accessed=1, transcendentals=0)


def split_counts(total, shares):
    whole = sum(shares)
    edges = [round(total * sum(shares[:i]) / whole) for i in range(len(shares) + 1)]
    return [(a, b - a) for a, b in zip(edges[:-1], edges[1:]) if b > a]


def swap_pairs(block, axis, first):
    count = lax.axis_size(axis)
    route = []
    for low in range(first, count - 1, 2):
        route += [(low, low + 1), (low + 1, low)]
    return lax.ppermute(block, axis, route)


def nearby_ids(image_ids, rows):
    shard = lax.axis_index("dp")
    padded = jnp.pad(image_ids, (rows, rows), constant_values=-1)
    odd = lax.rem(shard, 2)

    def ids_of(other):
        return lax.dynamic_slice_in_dim(padded, (other + 1) * rows, rows)

    return jnp.concatenate(
        (ids_of(shard + 1 - 2 * odd), ids_of(shard), ids_of(shard - 1 + 2 * odd))
    )


def columns(array, part, stride, first, width):
    start = pl.multiple_of(part * stride + first, HD)
    return array.at[:, pl.ds(start, width)]


def pack_kernel(parts, stride, first, width, deps, *refs):
    arrays, (packed, stage, in_sems, out_sems) = refs[:4], refs[4 + deps :]
    loads, stores = [], []
    for part in range(parts):
        for index, array in enumerate(arrays):
            load = pltpu.make_async_copy(
                columns(array, part, stride, first, width),
                stage.at[part, index],
                in_sems.at[part * 4 + index],
            )
            load.start()
            loads.append(load)
    for part in range(parts):
        for load in loads[part * 4 : part * 4 + 4]:
            load.wait()
        store = pltpu.make_async_copy(stage.at[part], packed.at[part], out_sems.at[part])
        store.start()
        stores.append(store)
    for store in stores:
        store.wait()


def pack(arrays, parts, first, count, after):
    rows, total = arrays[0].shape
    width = count * HD
    return pl.pallas_call(
        functools.partial(
            pack_kernel, parts, total // parts, first * HD, width, len(after)
        ),
        out_shape=jax.ShapeDtypeStruct((parts, 4, rows, width), jnp.bfloat16),
        in_specs=[pl.BlockSpec(memory_space=pl.ANY)] * (4 + len(after)),
        out_specs=pl.BlockSpec(memory_space=pl.ANY),
        scratch_shapes=[
            pltpu.VMEM((parts, 4, rows, width), jnp.bfloat16),
            pltpu.SemaphoreType.DMA((parts * 4,)),
            pltpu.SemaphoreType.DMA((parts,)),
        ],
        compiler_params=pltpu.CompilerParams(vmem_limit_bytes=VMEM_LIMIT),
        cost_estimate=SMALL_COST,
    )(*arrays, *after)


def join_kernel(parts, stride, first, width, deps, *refs):
    arrays, received, refs = refs[:4], refs[4 : 3 + parts], refs[3 + parts + deps :]
    joined, stage, in_sems, out_sems = refs
    me = lax.axis_index("tensor")
    loads, stores = [], []
    for flip in range(1, parts):
        load = pltpu.make_async_copy(received[flip - 1], stage.at[flip], in_sems.at[3 + flip])
        load.start()
        loads.append([load])
    own = []
    for index, array in enumerate(arrays):
        load = pltpu.make_async_copy(
            columns(array, me, stride, first, width), stage.at[0, index], in_sems.at[index]
        )
        load.start()
        own.append(load)
    loads = [own] + loads
    for flip in range(parts):
        for load in loads[flip]:
            load.wait()
        store = pltpu.make_async_copy(stage.at[flip], joined.at[me ^ flip], out_sems.at[flip])
        store.start()
        stores.append(store)
    for store in stores:
        store.wait()


def join(arrays, received, first, after):
    parts = len(received) + 1
    rows, total = arrays[0].shape
    width = received[0].shape[2]
    return pl.pallas_call(
        functools.partial(
            join_kernel, parts, total // parts, first * HD, width, len(after)
        ),
        out_shape=jax.ShapeDtypeStruct((parts, 4, rows, width), jnp.bfloat16),
        in_specs=[pl.BlockSpec(memory_space=pl.ANY)] * (3 + parts + len(after)),
        out_specs=pl.BlockSpec(memory_space=pl.ANY),
        scratch_shapes=[
            pltpu.VMEM((parts, 4, rows, width), jnp.bfloat16),
            pltpu.SemaphoreType.DMA((parts + 3,)),
            pltpu.SemaphoreType.DMA((parts,)),
        ],
        compiler_params=pltpu.CompilerParams(vmem_limit_bytes=VMEM_LIMIT),
        cost_estimate=SMALL_COST,
    )(*arrays, *received, *after)


def hold(array, after):
    return pl.pallas_call(
        lambda *refs: None,
        out_shape=jax.ShapeDtypeStruct(array.shape, array.dtype),
        in_specs=[pl.BlockSpec(memory_space=pl.ANY)] * (1 + len(after)),
        out_specs=pl.BlockSpec(memory_space=pl.ANY),
        input_output_aliases={0: 0},
        compiler_params=pltpu.CompilerParams(vmem_limit_bytes=VMEM_LIMIT),
        cost_estimate=SMALL_COST,
    )(array, *after)


def dot_nt(a, b):
    return lax.dot_general(a, b, (((1,), (1,)), ((), ())), preferred_element_type=jnp.float32)


def dot_tn(a, b):
    return lax.dot_general(a, b, (((0,), (0,)), ((), ())), preferred_element_type=jnp.float32)


def dot_nn(a, b):
    return jnp.dot(a, b, preferred_element_type=jnp.float32)


def probs_and_grads(queries, grads, keys, values, bias):
    scores = dot_nt(queries, keys) + bias
    row_max = jnp.max(scores, axis=1, keepdims=True)
    weights = jnp.exp2((scores - row_max) * EXP2_SCALE)
    probs = weights * (1.0 / jnp.sum(weights, axis=1, keepdims=True))
    grad_probs = dot_nt(grads, values)
    inner = jnp.sum(probs * grad_probs, axis=1, keepdims=True)
    grad_scores = probs * (grad_probs - inner)
    return probs.astype(jnp.bfloat16), grad_scores.astype(jnp.bfloat16)


def attend_kernel(rows, has_outs, *refs):
    row_ids, col_ids, own, left, right = refs[:5]
    refs = refs[5 + (4 if has_outs else 0) :]
    attended, grad_q, grad_k, grad_v, bias_own, bias_left, bias_right = refs

    @pl.when(pl.program_id(0) == 0)
    def _():
        def bias(row_start, col_start, col_count):
            same = (
                row_ids[row_start : row_start + rows, :]
                == col_ids[:, col_start : col_start + col_count]
            )
            return jnp.where(same, 0.0, MASKED)

        bias_own[...] = bias(rows, 0, 3 * rows)
        bias_left[...] = bias(0, 0, 2 * rows)
        bias_right[...] = bias(2 * rows, rows, 2 * rows)

    def load(ref, index):
        return ref[:, index].reshape(rows, HD)

    q_l, k_l, v_l, g_l = (load(left, i) for i in range(4))
    q_o, k_o, v_o, g_o = (load(own, i) for i in range(4))
    q_r, k_r, v_r, g_r = (load(right, i) for i in range(4))

    k_all = jnp.concatenate((k_l, k_o, k_r))
    v_all = jnp.concatenate((v_l, v_o, v_r))
    p, s = probs_and_grads(q_o, g_o, k_all, v_all, bias_own[...])
    attended[...] = dot_nn(p, v_all).astype(jnp.bfloat16)
    grad_q[...] = (dot_nn(s, k_all) * SCALE).astype(jnp.bfloat16)
    p_o, s_o = p[:, rows : 2 * rows], s[:, rows : 2 * rows]
    p_l, s_l = probs_and_grads(
        q_l, g_l, k_all[: 2 * rows], v_all[: 2 * rows], bias_left[...]
    )
    p_r, s_r = probs_and_grads(q_r, g_r, k_all[rows:], v_all[rows:], bias_right[...])
    p_l, s_l = p_l[:, rows:], s_l[:, rows:]
    p_r, s_r = p_r[:, :rows], s_r[:, :rows]
    grad_v[...] = (dot_tn(p_l, g_l) + dot_tn(p_o, g_o) + dot_tn(p_r, g_r)).astype(jnp.bfloat16)
    grad_k[...] = (
        (dot_tn(s_l, q_l) + dot_tn(s_o, q_o) + dot_tn(s_r, q_r)) * SCALE
    ).astype(jnp.bfloat16)


def attend(ids, own, left, right, outs, first_head, head_total):
    parts, _, part_rows, width = own.shape
    rows = parts * part_rows
    heads = width // HD
    block = pl.BlockSpec((parts, 4, part_rows, HD), lambda h: (0, 0, 0, h))
    whole = pl.BlockSpec(memory_space=pltpu.VMEM)
    out_spec = pl.BlockSpec((rows, HD), lambda h: (0, h + first_head))
    has_outs = outs is not None
    aliases = {5 + i: i for i in range(4)} if has_outs else {}
    return pl.pallas_call(
        functools.partial(attend_kernel, rows, has_outs),
        grid=(heads,),
        out_shape=[jax.ShapeDtypeStruct((rows, head_total * HD), jnp.bfloat16)] * 4,
        in_specs=[whole, whole, block, block, block]
        + ([pl.BlockSpec(memory_space=pl.ANY)] * 4 if has_outs else []),
        out_specs=[out_spec] * 4,
        scratch_shapes=[
            pltpu.VMEM((rows, 3 * rows), jnp.float32),
            pltpu.VMEM((rows, 2 * rows), jnp.float32),
            pltpu.VMEM((rows, 2 * rows), jnp.float32),
        ],
        input_output_aliases=aliases,
        compiler_params=pltpu.CompilerParams(
            dimension_semantics=("arbitrary",), vmem_limit_bytes=VMEM_LIMIT
        ),
        cost_estimate=pl.CostEstimate(
            flops=heads * ATTEND_FLOPS, bytes_accessed=1, transcendentals=0
        ),
    )(ids[:, None], ids[None, :], own, left, right, *(outs or ()))


def shards(queries, key_vectors, value_vectors, grad_output, image_ids):
    arrays = (queries, key_vectors, value_vectors, grad_output)
    parts = lax.axis_size("tensor")
    rows = queries.shape[0] * parts
    head_total = queries.shape[1] // HD // parts
    ids = nearby_ids(image_ids, rows)
    chunks = split_counts(head_total, CHUNK_SHARES)
    outs, out_history, packed = None, [], []
    for first, count in chunks[:2]:
        packed.append(pack(arrays, parts, first, count, []))
    for number, (first, count) in enumerate(chunks):
        own = lax.all_to_all(packed[number], "tensor", split_axis=0, concat_axis=0, tiled=True)
        after = packed[number + 1 : number + 2]
        if number >= 2:
            after.append(out_history[number - 2][0])
        own = hold(own, after)
        if number + 2 < len(chunks):
            packed.append(pack(arrays, parts, *chunks[number + 2], [own]))
        near = swap_pairs(own, "dp", 0)
        far = swap_pairs(own, "dp", 1)
        outs = attend(ids, own, near, far, outs, first, head_total)
        out_history.append(outs)
    return tuple(outs)


def solution(mesh):
    return jax.shard_map(
        shards,
        mesh=mesh,
        in_specs=(
            P(("dp", "tensor"), None),
            P(("dp", "tensor"), None),
            P(("dp", "tensor"), None),
            P(("dp", "tensor"), None),
            P(),
        ),
        out_specs=(P("dp", "tensor"), P("dp", "tensor"), P("dp", "tensor"), P("dp", "tensor")),
        check_vma=False,
    )
```

```python
import functools
import math

import jax
import jax.numpy as jnp
from jax import lax
from jax.experimental import pallas as pl
from jax.experimental.pallas import tpu as pltpu
from jax.sharding import PartitionSpec as P

HD = 128
BLOCK = 64
WINDOW = 384
SCALE = 1.0 / math.sqrt(HD)
EXP2_SCALE = SCALE * math.log2(math.e)
MASKED = -1e30
CHUNK_SHARES = (4, 4, 3, 1)
VMEM_LIMIT = 60 * 1024 * 1024
ATTEND_FLOPS = 1_500_000_000
SMALL_COST = pl.CostEstimate(flops=1, bytes_accessed=1, transcendentals=0)


def split_counts(total, shares):
    whole = sum(shares)
    edges = [round(total * sum(shares[:i]) / whole) for i in range(len(shares) + 1)]
    return [(a, b - a) for a, b in zip(edges[:-1], edges[1:]) if b > a]


def swap_pairs(block, axis, first):
    count = lax.axis_size(axis)
    route = []
    for low in range(first, count - 1, 2):
        route += [(low, low + 1), (low + 1, low)]
    return lax.ppermute(block, axis, route)


def nearby_ids(image_ids, rows):
    shard = lax.axis_index("dp")
    padded = jnp.pad(image_ids, (rows, rows), constant_values=-1)
    odd = lax.rem(shard, 2)

    def ids_of(other):
        return lax.dynamic_slice_in_dim(padded, (other + 1) * rows, rows)

    return ids_of(shard), ids_of(shard + 1 - 2 * odd), ids_of(shard - 1 + 2 * odd)


def columns(array, part, stride, first, width):
    start = pl.multiple_of(part * stride + first, HD)
    return array.at[:, pl.ds(start, width)]


def pack_kernel(parts, stride, first, width, deps, *refs):
    arrays, (packed, stage, in_sems, out_sems) = refs[:4], refs[4 + deps :]
    loads, stores = [], []
    for part in range(parts):
        for index, array in enumerate(arrays):
            load = pltpu.make_async_copy(
                columns(array, part, stride, first, width),
                stage.at[part, index],
                in_sems.at[part * 4 + index],
            )
            load.start()
            loads.append(load)
    for part in range(parts):
        for load in loads[part * 4 : part * 4 + 4]:
            load.wait()
        store = pltpu.make_async_copy(stage.at[part], packed.at[part], out_sems.at[part])
        store.start()
        stores.append(store)
    for store in stores:
        store.wait()


def pack(arrays, parts, first, count, after):
    rows, total = arrays[0].shape
    width = count * HD
    return pl.pallas_call(
        functools.partial(
            pack_kernel, parts, total // parts, first * HD, width, len(after)
        ),
        out_shape=jax.ShapeDtypeStruct((parts, 4, rows, width), jnp.bfloat16),
        in_specs=[pl.BlockSpec(memory_space=pl.ANY)] * (4 + len(after)),
        out_specs=pl.BlockSpec(memory_space=pl.ANY),
        scratch_shapes=[
            pltpu.VMEM((parts, 4, rows, width), jnp.bfloat16),
            pltpu.SemaphoreType.DMA((parts * 4,)),
            pltpu.SemaphoreType.DMA((parts,)),
        ],
        compiler_params=pltpu.CompilerParams(vmem_limit_bytes=VMEM_LIMIT),
        cost_estimate=SMALL_COST,
    )(*arrays, *after)


def join_kernel(parts, stride, first, width, deps, *refs):
    arrays, received, refs = refs[:4], refs[4 : 3 + parts], refs[3 + parts + deps :]
    joined, stage, in_sems, out_sems = refs
    me = lax.axis_index("tensor")
    loads, stores = [], []
    for flip in range(1, parts):
        load = pltpu.make_async_copy(received[flip - 1], stage.at[flip], in_sems.at[3 + flip])
        load.start()
        loads.append([load])
    own = []
    for index, array in enumerate(arrays):
        load = pltpu.make_async_copy(
            columns(array, me, stride, first, width), stage.at[0, index], in_sems.at[index]
        )
        load.start()
        own.append(load)
    loads = [own] + loads
    for flip in range(parts):
        for load in loads[flip]:
            load.wait()
        store = pltpu.make_async_copy(stage.at[flip], joined.at[me ^ flip], out_sems.at[flip])
        store.start()
        stores.append(store)
    for store in stores:
        store.wait()


def join(arrays, received, first, after):
    parts = len(received) + 1
    rows, total = arrays[0].shape
    width = received[0].shape[2]
    return pl.pallas_call(
        functools.partial(
            join_kernel, parts, total // parts, first * HD, width, len(after)
        ),
        out_shape=jax.ShapeDtypeStruct((parts, 4, rows, width), jnp.bfloat16),
        in_specs=[pl.BlockSpec(memory_space=pl.ANY)] * (3 + parts + len(after)),
        out_specs=pl.BlockSpec(memory_space=pl.ANY),
        scratch_shapes=[
            pltpu.VMEM((parts, 4, rows, width), jnp.bfloat16),
            pltpu.SemaphoreType.DMA((parts + 3,)),
            pltpu.SemaphoreType.DMA((parts,)),
        ],
        compiler_params=pltpu.CompilerParams(vmem_limit_bytes=VMEM_LIMIT),
        cost_estimate=SMALL_COST,
    )(*arrays, *received, *after)


def hold(array, after):
    return pl.pallas_call(
        lambda *refs: None,
        out_shape=jax.ShapeDtypeStruct(array.shape, array.dtype),
        in_specs=[pl.BlockSpec(memory_space=pl.ANY)] * (1 + len(after)),
        out_specs=pl.BlockSpec(memory_space=pl.ANY),
        input_output_aliases={0: 0},
        compiler_params=pltpu.CompilerParams(vmem_limit_bytes=VMEM_LIMIT),
        cost_estimate=SMALL_COST,
    )(array, *after)


def dot_nt(a, b):
    return lax.dot_general(a, b, (((1,), (1,)), ((), ())), preferred_element_type=jnp.float32)


def dot_tn(a, b):
    return lax.dot_general(a, b, (((0,), (0,)), ((), ())), preferred_element_type=jnp.float32)


def dot_nn(a, b):
    return jnp.dot(a, b, preferred_element_type=jnp.float32)


def attention(queries, keys, values, grads, bias, count):
    scores = dot_nt(queries, keys) + bias
    row_max = jnp.max(scores, axis=1, keepdims=True)
    weights = jnp.exp2((scores - row_max) * EXP2_SCALE)
    probs = weights * (1.0 / jnp.sum(weights, axis=1, keepdims=True))
    grad_probs = dot_nt(grads, values)
    inner = jnp.sum(probs * grad_probs, axis=1, keepdims=True)
    low = probs.astype(jnp.bfloat16)
    grad_scores = (probs * (grad_probs - inner)).astype(jnp.bfloat16)
    results = (
        dot_nn(low[:count], values),
        dot_nn(grad_scores[:count], keys) * SCALE,
        dot_tn(grad_scores[:, :count], queries) * SCALE,
        dot_tn(low[:, :count], grads),
    )
    return [result.astype(jnp.bfloat16) for result in results]


def attend_kernel(rows, has_outs, *refs):
    row_ids, col_ids, sides, own, near, far = refs[:6]
    refs = refs[6 + (4 if has_outs else 0) :]
    outs, (bias, gathered, results) = refs[:4], refs[4:]
    parts_per_block = own.shape[0] * BLOCK // rows
    most = WINDOW // BLOCK

    @pl.when(pl.program_id(0) == 0)
    def _():
        bias[...] = jnp.where(row_ids[...] == col_ids[...], 0.0, MASKED)

    whole = [own[:, index].reshape(rows, HD) for index in range(4)]
    for out, result in zip(outs, attention(*whole, bias[...], rows)):
        out[...] = result

    def block_of(ref, block, index):
        block = jnp.clip(block, 0, rows // BLOCK - 1)
        taken = ref[pl.ds(block * parts_per_block, parts_per_block), index]
        return taken.reshape(BLOCK, HD)

    def one_side(side, other):
        own_first, own_count = sides[side, 0], sides[side, 1]
        other_first, other_count = sides[side, 2], sides[side, 3]
        total = own_count + other_count

        @pl.when(own_count > 0)
        def _():
            for slot in range(most):
                for index in range(4):
                    block = jnp.where(
                        slot < own_count,
                        block_of(own, own_first + slot, index),
                        block_of(other, other_first + slot - own_count, index),
                    )
                    if index == 3:
                        block = jnp.where(slot < total, block, jnp.zeros_like(block))
                    gathered[index, slot * BLOCK : (slot + 1) * BLOCK] = block

        for size in range(2 * BLOCK, WINDOW + 1, 2 * BLOCK):
            blocks = size // BLOCK

            @pl.when((own_count > 0) & (total > blocks - 2) & (total <= blocks))
            def _():
                lane = lax.broadcasted_iota(jnp.int32, (1, size), 1)
                tail = jnp.where(lane < total * BLOCK, 0.0, MASKED)
                count = min(size, rows)
                image = [gathered[index, :size] for index in range(4)]
                for index, result in enumerate(attention(*image, tail, count)):
                    results[index, :count] = result

        for slot in range(rows // BLOCK):

            @pl.when(slot < own_count)
            def _():
                target = pl.ds(pl.multiple_of((own_first + slot) * BLOCK, BLOCK), BLOCK)
                for index, out in enumerate(outs):
                    out[target, :] = results[index, slot * BLOCK : (slot + 1) * BLOCK]

    one_side(0, near)
    one_side(1, far)


def attend(ids, sides, own, near, far, outs, first_head, head_total):
    parts, _, part_rows, width = own.shape
    rows = parts * part_rows
    heads = width // HD
    block = pl.BlockSpec((parts, 4, part_rows, HD), lambda h: (0, 0, 0, h))
    whole = pl.BlockSpec(memory_space=pltpu.VMEM)
    out_spec = pl.BlockSpec((rows, HD), lambda h: (0, h + first_head))
    has_outs = outs is not None
    aliases = {6 + i: i for i in range(4)} if has_outs else {}
    return pl.pallas_call(
        functools.partial(attend_kernel, rows, has_outs),
        grid=(heads,),
        out_shape=[jax.ShapeDtypeStruct((rows, head_total * HD), jnp.bfloat16)] * 4,
        in_specs=[whole, whole, pl.BlockSpec(memory_space=pltpu.SMEM), block, block, block]
        + ([pl.BlockSpec(memory_space=pl.ANY)] * 4 if has_outs else []),
        out_specs=[out_spec] * 4,
        scratch_shapes=[
            pltpu.VMEM((rows, rows), jnp.float32),
            pltpu.VMEM((4, WINDOW, HD), jnp.bfloat16),
            pltpu.VMEM((4, rows, HD), jnp.bfloat16),
        ],
        input_output_aliases=aliases,
        compiler_params=pltpu.CompilerParams(
            dimension_semantics=("arbitrary",), vmem_limit_bytes=VMEM_LIMIT
        ),
        cost_estimate=pl.CostEstimate(
            flops=heads * ATTEND_FLOPS, bytes_accessed=1, transcendentals=0
        ),
    )(ids[:, None], ids[None, :], sides, own, near, far, *(outs or ()))


def side_blocks(own_ids, other_ids):
    same = own_ids[:, None] == other_ids[None, :]

    def span(shared):
        return jnp.argmax(shared).astype(jnp.int32), jnp.sum(shared, dtype=jnp.int32)

    return jnp.stack(span(jnp.any(same, axis=1)) + span(jnp.any(same, axis=0)))


def shards(queries, key_vectors, value_vectors, grad_output, image_ids):
    arrays = (queries, key_vectors, value_vectors, grad_output)
    parts = lax.axis_size("tensor")
    rows = queries.shape[0] * parts
    head_total = queries.shape[1] // HD // parts
    ids, *others = nearby_ids(image_ids, rows)
    sides = jnp.stack([side_blocks(ids[::BLOCK], other[::BLOCK]) for other in others])
    chunks = split_counts(head_total, CHUNK_SHARES)
    outs, out_history, packed = None, [], []
    for first, count in chunks[:2]:
        packed.append(pack(arrays, parts, first, count, []))
    for number, (first, count) in enumerate(chunks):
        own = lax.all_to_all(packed[number], "tensor", split_axis=0, concat_axis=0, tiled=True)
        after = packed[number + 1 : number + 2]
        if number >= 2:
            after.append(out_history[number - 2][0])
        own = hold(own, after)
        if number + 2 < len(chunks):
            packed.append(pack(arrays, parts, *chunks[number + 2], [own]))
        near = swap_pairs(own, "dp", 0)
        far = swap_pairs(own, "dp", 1)
        outs = attend(ids, sides, own, near, far, outs, first, head_total)
        out_history.append(outs)
    return tuple(outs)


def solution(mesh):
    return jax.shard_map(
        shards,
        mesh=mesh,
        in_specs=(
            P(("dp", "tensor"), None),
            P(("dp", "tensor"), None),
            P(("dp", "tensor"), None),
            P(("dp", "tensor"), None),
            P(),
        ),
        out_specs=(P("dp", "tensor"), P("dp", "tensor"), P("dp", "tensor"), P("dp", "tensor")),
        check_vma=False,
    )
```

```python
import functools
import math

import jax
import jax.numpy as jnp
from jax import lax
from jax.experimental import pallas as pl
from jax.experimental.pallas import tpu as pltpu
from jax.sharding import PartitionSpec as P

HD = 128
BLOCK = 64
SCALE = 1.0 / math.sqrt(HD)
EXP2_SCALE = SCALE * math.log2(math.e)
MASKED = -1e30
CHUNK_SHARES = (4, 4, 3, 1)
VMEM_LIMIT = 60 * 1024 * 1024
ATTEND_FLOPS = 1_500_000_000
SMALL_COST = pl.CostEstimate(flops=1, bytes_accessed=1, transcendentals=0)


def split_counts(total, shares):
    whole = sum(shares)
    edges = [round(total * sum(shares[:i]) / whole) for i in range(len(shares) + 1)]
    return [(a, b - a) for a, b in zip(edges[:-1], edges[1:]) if b > a]


def swap_pairs(block, axis, first):
    count = lax.axis_size(axis)
    route = []
    for low in range(first, count - 1, 2):
        route += [(low, low + 1), (low + 1, low)]
    return lax.ppermute(block, axis, route)


def nearby_block_ids(image_ids, rows):
    shard = lax.axis_index("dp")
    blocks = rows // BLOCK
    padded = jnp.pad(image_ids[::BLOCK], (blocks, blocks), constant_values=-1)
    odd = lax.rem(shard, 2)

    def ids_of(other):
        return lax.dynamic_slice_in_dim(padded, (other + 1) * blocks, blocks)

    return jnp.stack((ids_of(shard), ids_of(shard + 1 - 2 * odd), ids_of(shard - 1 + 2 * odd)))


def columns(array, part, stride, first, width):
    start = pl.multiple_of(part * stride + first, HD)
    return array.at[:, pl.ds(start, width)]


def pack_kernel(parts, stride, first, width, deps, *refs):
    arrays, (packed, stage, in_sems, out_sems) = refs[:4], refs[4 + deps :]
    loads, stores = [], []
    for part in range(parts):
        for index, array in enumerate(arrays):
            load = pltpu.make_async_copy(
                columns(array, part, stride, first, width),
                stage.at[part, index],
                in_sems.at[part * 4 + index],
            )
            load.start()
            loads.append(load)
    for part in range(parts):
        for load in loads[part * 4 : part * 4 + 4]:
            load.wait()
        store = pltpu.make_async_copy(stage.at[part], packed.at[part], out_sems.at[part])
        store.start()
        stores.append(store)
    for store in stores:
        store.wait()


def pack(arrays, parts, first, count, after):
    rows, total = arrays[0].shape
    width = count * HD
    return pl.pallas_call(
        functools.partial(
            pack_kernel, parts, total // parts, first * HD, width, len(after)
        ),
        out_shape=jax.ShapeDtypeStruct((parts, 4, rows, width), jnp.bfloat16),
        in_specs=[pl.BlockSpec(memory_space=pl.ANY)] * (4 + len(after)),
        out_specs=pl.BlockSpec(memory_space=pl.ANY),
        scratch_shapes=[
            pltpu.VMEM((parts, 4, rows, width), jnp.bfloat16),
            pltpu.SemaphoreType.DMA((parts * 4,)),
            pltpu.SemaphoreType.DMA((parts,)),
        ],
        compiler_params=pltpu.CompilerParams(vmem_limit_bytes=VMEM_LIMIT),
        cost_estimate=SMALL_COST,
    )(*arrays, *after)


def join_kernel(parts, stride, first, width, deps, *refs):
    arrays, received, refs = refs[:4], refs[4 : 3 + parts], refs[3 + parts + deps :]
    joined, stage, in_sems, out_sems = refs
    me = lax.axis_index("tensor")
    loads, stores = [], []
    for flip in range(1, parts):
        load = pltpu.make_async_copy(received[flip - 1], stage.at[flip], in_sems.at[3 + flip])
        load.start()
        loads.append([load])
    own = []
    for index, array in enumerate(arrays):
        load = pltpu.make_async_copy(
            columns(array, me, stride, first, width), stage.at[0, index], in_sems.at[index]
        )
        load.start()
        own.append(load)
    loads = [own] + loads
    for flip in range(parts):
        for load in loads[flip]:
            load.wait()
        store = pltpu.make_async_copy(stage.at[flip], joined.at[me ^ flip], out_sems.at[flip])
        store.start()
        stores.append(store)
    for store in stores:
        store.wait()


def join(arrays, received, first, after):
    parts = len(received) + 1
    rows, total = arrays[0].shape
    width = received[0].shape[2]
    return pl.pallas_call(
        functools.partial(
            join_kernel, parts, total // parts, first * HD, width, len(after)
        ),
        out_shape=jax.ShapeDtypeStruct((parts, 4, rows, width), jnp.bfloat16),
        in_specs=[pl.BlockSpec(memory_space=pl.ANY)] * (3 + parts + len(after)),
        out_specs=pl.BlockSpec(memory_space=pl.ANY),
        scratch_shapes=[
            pltpu.VMEM((parts, 4, rows, width), jnp.bfloat16),
            pltpu.SemaphoreType.DMA((parts + 3,)),
            pltpu.SemaphoreType.DMA((parts,)),
        ],
        compiler_params=pltpu.CompilerParams(vmem_limit_bytes=VMEM_LIMIT),
        cost_estimate=SMALL_COST,
    )(*arrays, *received, *after)


def hold(array, after):
    return pl.pallas_call(
        lambda *refs: None,
        out_shape=jax.ShapeDtypeStruct(array.shape, array.dtype),
        in_specs=[pl.BlockSpec(memory_space=pl.ANY)] * (1 + len(after)),
        out_specs=pl.BlockSpec(memory_space=pl.ANY),
        input_output_aliases={0: 0},
        compiler_params=pltpu.CompilerParams(vmem_limit_bytes=VMEM_LIMIT),
        cost_estimate=SMALL_COST,
    )(array, *after)


def dot_nt(a, b):
    return lax.dot_general(a, b, (((1,), (1,)), ((), ())), preferred_element_type=jnp.float32)


def dot_tn(a, b):
    return lax.dot_general(a, b, (((0,), (0,)), ((), ())), preferred_element_type=jnp.float32)


def dot_nn(a, b):
    return jnp.dot(a, b, preferred_element_type=jnp.float32)


def attend_head(values_of, bias, size, rows):
    queries, keys, values, grads = values_of
    grad_k = grad_v = None
    for start in range(0, size, rows):
        tile = slice(start, start + rows)
        scores = dot_nt(keys, queries[tile]) + bias[:size, tile]
        weights = jnp.exp2((scores - jnp.max(scores, axis=0, keepdims=True)) * EXP2_SCALE)
        probs = weights * (1.0 / jnp.sum(weights, axis=0, keepdims=True))
        grad_probs = dot_nt(values, grads[tile])
        inner = jnp.sum(probs * grad_probs, axis=0, keepdims=True)
        low = probs.astype(jnp.bfloat16)
        grad_scores = (probs * (grad_probs - inner)).astype(jnp.bfloat16)
        tile_v = dot_nn(low[:rows], grads[tile])
        tile_k = dot_nn(grad_scores[:rows], queries[tile])
        if start == 0:
            attended = dot_tn(low, values)
            grad_q = dot_tn(grad_scores, keys)
            grad_k, grad_v = tile_k, tile_v
        else:
            grad_k, grad_v = grad_k + tile_k, grad_v + tile_v
    return attended, grad_q * SCALE, grad_k * SCALE, grad_v


def attend_kernel(rows, has_outs, *refs):
    block_ids, own, near, far = refs[:4]
    refs = refs[4 + (4 if has_outs else 0) :]
    outs, (bias, gathered, table) = refs[:4], refs[4:]
    blocks = rows // BLOCK
    parts_per_block = own.shape[0] * BLOCK // rows
    most = 3 * rows

    @pl.when(pl.program_id(0) == 0)
    def _():
        count = jnp.int32(0)
        for other in range(2 * blocks):
            other_id = block_ids[1 + other // blocks, other % blocks]
            shared = other_id == block_ids[0, 0]
            for block in range(1, blocks):
                shared = shared | (other_id == block_ids[0, block])
            table[count] = other
            count = count + shared.astype(jnp.int32)
        table[2 * blocks] = count

        def ids_along(axis):
            shape = (most, 1) if axis == 0 else (1, most)
            place = lax.broadcasted_iota(jnp.int32, shape, axis)
            ids = jnp.full(shape, -2, jnp.int32)
            for block in range(3 * blocks):
                if block < blocks:
                    block_id = block_ids[0, block]
                else:
                    source = table[jnp.minimum(block - blocks, 2 * blocks - 1)]
                    source = jnp.clip(source, 0, 2 * blocks - 1)
                    block_id = block_ids[1 + source // blocks, lax.rem(source, blocks)]
                    block_id = jnp.where(block - blocks < count, block_id, -2)
                inside = (place >= block * BLOCK) & (place < (block + 1) * BLOCK)
                ids = jnp.where(inside, block_id, ids)
            return ids

        bias[...] = jnp.where(ids_along(0) == ids_along(1), 0.0, MASKED)

    count = table[2 * blocks]

    def other_block(slot, index):
        source = jnp.where(slot < count, table[slot], 0)
        place = lax.rem(source, blocks) * parts_per_block
        taken = [ref[pl.ds(place, parts_per_block), index] for ref in (near, far)]
        return jnp.where(source < blocks, *taken).reshape(BLOCK, HD)

    for size in range(rows, most + 1, rows):
        slots = size // BLOCK - blocks

        @pl.when((count <= slots) & (count > slots - blocks))
        def _():
            for slot in range(slots):
                for index in range(4):
                    gathered[index, slot * BLOCK : (slot + 1) * BLOCK] = other_block(slot, index)
            values_of = []
            for index in range(4):
                mine = own[:, index].reshape(rows, HD)
                if slots:
                    mine = jnp.concatenate((mine, gathered[index, : slots * BLOCK]))
                values_of.append(mine)
            for out, result in zip(outs, attend_head(values_of, bias, size, rows)):
                out[...] = result.astype(jnp.bfloat16)


def attend(block_ids, own, near, far, outs, first_head, head_total):
    parts, _, part_rows, width = own.shape
    rows = parts * part_rows
    heads = width // HD
    block = pl.BlockSpec((parts, 4, part_rows, HD), lambda h: (0, 0, 0, h))
    out_spec = pl.BlockSpec((rows, HD), lambda h: (0, h + first_head))
    has_outs = outs is not None
    aliases = {4 + i: i for i in range(4)} if has_outs else {}
    return pl.pallas_call(
        functools.partial(attend_kernel, rows, has_outs),
        grid=(heads,),
        out_shape=[jax.ShapeDtypeStruct((rows, head_total * HD), jnp.bfloat16)] * 4,
        in_specs=[pl.BlockSpec(memory_space=pltpu.SMEM), block, block, block]
        + ([pl.BlockSpec(memory_space=pl.ANY)] * 4 if has_outs else []),
        out_specs=[out_spec] * 4,
        scratch_shapes=[
            pltpu.VMEM((3 * rows, 3 * rows), jnp.float32),
            pltpu.VMEM((4, 2 * rows, HD), jnp.bfloat16),
            pltpu.SMEM((2 * rows // BLOCK + 1,), jnp.int32),
        ],
        input_output_aliases=aliases,
        compiler_params=pltpu.CompilerParams(
            dimension_semantics=("arbitrary",), vmem_limit_bytes=VMEM_LIMIT
        ),
        cost_estimate=pl.CostEstimate(
            flops=heads * ATTEND_FLOPS, bytes_accessed=1, transcendentals=0
        ),
    )(block_ids, own, near, far, *(outs or ()))


def shards(queries, key_vectors, value_vectors, grad_output, image_ids):
    arrays = (queries, key_vectors, value_vectors, grad_output)
    parts = lax.axis_size("tensor")
    rows = queries.shape[0] * parts
    head_total = queries.shape[1] // HD // parts
    block_ids = nearby_block_ids(image_ids, rows)
    chunks = split_counts(head_total, CHUNK_SHARES)
    outs, out_history, packed = None, [], []
    for first, count in chunks[:2]:
        packed.append(pack(arrays, parts, first, count, []))
    for number, (first, count) in enumerate(chunks):
        own = lax.all_to_all(packed[number], "tensor", split_axis=0, concat_axis=0, tiled=True)
        after = packed[number + 1 : number + 2]
        if number >= 2:
            after.append(out_history[number - 2][0])
        own = hold(own, after)
        if number + 2 < len(chunks):
            packed.append(pack(arrays, parts, *chunks[number + 2], [own]))
        near = swap_pairs(own, "dp", 0)
        far = swap_pairs(own, "dp", 1)
        outs = attend(block_ids, own, near, far, outs, first, head_total)
        out_history.append(outs)
    return tuple(outs)


def solution(mesh):
    return jax.shard_map(
        shards,
        mesh=mesh,
        in_specs=(
            P(("dp", "tensor"), None),
            P(("dp", "tensor"), None),
            P(("dp", "tensor"), None),
            P(("dp", "tensor"), None),
            P(),
        ),
        out_specs=(P("dp", "tensor"), P("dp", "tensor"), P("dp", "tensor"), P("dp", "tensor")),
        check_vma=False,
    )
```

```python
import functools
import math

import jax
import jax.numpy as jnp
from jax import lax
from jax.experimental import pallas as pl
from jax.experimental.pallas import tpu as pltpu
from jax.sharding import PartitionSpec as P

HD = 128
SCALE = 1.0 / math.sqrt(HD)
EXP2_SCALE = SCALE * math.log2(math.e)
MASKED = -1e30
CHUNK_SHARES = (6, 4, 2)
VMEM_LIMIT = 63 * 1024 * 1024
ATTEND_FLOPS = 1_500_000_000
SMALL_COST = pl.CostEstimate(flops=1, bytes_accessed=1, transcendentals=0)


def split_counts(total, shares):
    whole = sum(shares)
    edges = [round(total * sum(shares[:i]) / whole) for i in range(len(shares) + 1)]
    return [(a, b - a) for a, b in zip(edges[:-1], edges[1:]) if b > a]


def swap_pairs(block, axis, first):
    count = lax.axis_size(axis)
    route = []
    for low in range(first, count - 1, 2):
        route += [(low, low + 1), (low + 1, low)]
    return lax.ppermute(block, axis, route)


def swap_flipped(block, axis, flip):
    return lax.ppermute(block, axis, [(i, i ^ flip) for i in range(lax.axis_size(axis))])


def nearby_ids(image_ids, parts, part_rows):
    shard = lax.axis_index("dp")
    padded = jnp.pad(image_ids[::part_rows], (parts, parts), constant_values=-1)
    odd = lax.rem(shard, 2)

    def ids_of(other):
        return lax.dynamic_slice_in_dim(padded, (other + 1) * parts, parts)

    return jnp.stack((ids_of(shard), ids_of(shard + 1 - 2 * odd), ids_of(shard - 1 + 2 * odd)))


def columns(array, part, stride, first, width):
    start = pl.multiple_of(part * stride + first, HD)
    return array.at[:, pl.ds(start, width)]


def pack_kernel(parts, stride, chunks, *refs):
    arrays, refs = refs[:4], refs[4:]
    own, packed, (stage, in_sems, out_sems) = refs[0], refs[1:-3], refs[-3:]
    me = lax.axis_index("tensor")
    jobs = [(0, 0, stride, own)]
    for number, (first, count) in enumerate(chunks):
        for flip in range(1, parts):
            target = packed[number * (parts - 1) + flip - 1]
            jobs.append((flip, first * HD, count * HD, target))
    jobs = jobs[1:parts] + jobs[:1] + jobs[parts:]
    loads, stores = [], []
    for number, (flip, first, width, _) in enumerate(jobs):
        for index, array in enumerate(arrays):
            load = pltpu.make_async_copy(
                columns(array, me ^ flip, stride, first, width),
                stage.at[flip, index, :, pl.ds(first, width)],
                in_sems.at[number * 4 + index],
            )
            load.start()
            loads.append(load)
    for number, (flip, first, width, target) in enumerate(jobs):
        for load in loads[number * 4 : number * 4 + 4]:
            load.wait()
        store = pltpu.make_async_copy(
            stage.at[flip, :, :, pl.ds(first, width)], target, out_sems.at[number]
        )
        store.start()
        stores.append(store)
    for store in stores:
        store.wait()


def pack(arrays, parts, chunks):
    rows, total = arrays[0].shape
    stride = total // parts
    widths = [stride] + [count * HD for _, count in chunks for _ in range(1, parts)]
    results = pl.pallas_call(
        functools.partial(pack_kernel, parts, stride, chunks),
        out_shape=[jax.ShapeDtypeStruct((4, rows, width), jnp.bfloat16) for width in widths],
        in_specs=[pl.BlockSpec(memory_space=pl.ANY)] * 4,
        out_specs=[pl.BlockSpec(memory_space=pl.ANY)] * len(widths),
        scratch_shapes=[
            pltpu.VMEM((parts, 4, rows, stride), jnp.bfloat16),
            pltpu.SemaphoreType.DMA((4 * len(widths),)),
            pltpu.SemaphoreType.DMA((len(widths),)),
        ],
        compiler_params=pltpu.CompilerParams(vmem_limit_bytes=VMEM_LIMIT),
        cost_estimate=SMALL_COST,
    )(*arrays)
    pieces = results[1:]
    return results[0], [
        pieces[start : start + parts - 1] for start in range(0, len(pieces), parts - 1)
    ]


def join_kernel(pieces, *refs):
    received, (joined, stage, in_sems, out_sems) = refs[:pieces], refs[-4:]
    loads, stores = [], []
    for piece in range(pieces):
        load = pltpu.make_async_copy(received[piece], stage.at[piece], in_sems.at[piece])
        load.start()
        loads.append(load)
    for piece in range(pieces):
        loads[piece].wait()
        store = pltpu.make_async_copy(stage.at[piece], joined.at[piece], out_sems.at[piece])
        store.start()
        stores.append(store)
    for store in stores:
        store.wait()


def join(received, after):
    pieces = len(received)
    shape = (pieces,) + received[0].shape
    return pl.pallas_call(
        functools.partial(join_kernel, pieces),
        out_shape=jax.ShapeDtypeStruct(shape, jnp.bfloat16),
        in_specs=[pl.BlockSpec(memory_space=pl.ANY)] * (pieces + len(after)),
        out_specs=pl.BlockSpec(memory_space=pl.ANY),
        scratch_shapes=[
            pltpu.VMEM(shape, jnp.bfloat16),
            pltpu.SemaphoreType.DMA((pieces,)),
            pltpu.SemaphoreType.DMA((pieces,)),
        ],
        compiler_params=pltpu.CompilerParams(vmem_limit_bytes=VMEM_LIMIT),
        cost_estimate=SMALL_COST,
    )(*received, *after)


def hold(array, after):
    return pl.pallas_call(
        lambda *refs: None,
        out_shape=jax.ShapeDtypeStruct(array.shape, array.dtype),
        in_specs=[pl.BlockSpec(memory_space=pl.ANY)] * (1 + len(after)),
        out_specs=pl.BlockSpec(memory_space=pl.ANY),
        input_output_aliases={0: 0},
        compiler_params=pltpu.CompilerParams(vmem_limit_bytes=VMEM_LIMIT),
        cost_estimate=SMALL_COST,
    )(array, *after)


def dot_nt(a, b):
    return lax.dot_general(a, b, (((1,), (1,)), ((), ())), preferred_element_type=jnp.float32)


def dot_tn(a, b):
    return lax.dot_general(a, b, (((0,), (0,)), ((), ())), preferred_element_type=jnp.float32)


def dot_nn(a, b):
    return jnp.dot(a, b, preferred_element_type=jnp.float32)


def attend_head(values_of, bias, size, rows):
    queries, keys, values, grads = values_of
    grad_k = grad_v = None
    for start in range(0, size, rows):
        tile = slice(start, start + rows)
        scores = dot_nt(keys, queries[tile]) + bias[:size, tile]
        weights = jnp.exp2((scores - jnp.max(scores, axis=0, keepdims=True)) * EXP2_SCALE)
        probs = weights * (1.0 / jnp.sum(weights, axis=0, keepdims=True))
        grad_probs = dot_nt(values, grads[tile])
        inner = jnp.sum(probs * grad_probs, axis=0, keepdims=True)
        low = probs.astype(jnp.bfloat16)
        grad_scores = (probs * (grad_probs - inner)).astype(jnp.bfloat16)
        tile_v = dot_nn(low[:rows], grads[tile])
        tile_k = dot_nn(grad_scores[:rows], queries[tile])
        if start == 0:
            attended = dot_tn(low, values)
            grad_q = dot_tn(grad_scores, keys)
            grad_k, grad_v = tile_k, tile_v
        else:
            grad_k, grad_v = grad_k + tile_k, grad_v + tile_v
    return attended, grad_q * SCALE, grad_k * SCALE, grad_v


def attend_kernel(parts, has_outs, *refs):
    image_ids, groups = refs[0], (refs[1:3], refs[3:5], refs[5:7])
    refs = refs[7 + (4 if has_outs else 0) :]
    outs, (bias, gathered, table) = refs[:4], refs[4:]
    part_rows = groups[0][0].shape[1]
    rows = parts * part_rows
    most = 3 * rows
    me = lax.axis_index("tensor")

    def id_of(group, slot):
        return image_ids[group, me ^ slot]

    @pl.when(pl.program_id(0) == 0)
    def _():
        count = jnp.int32(0)
        for other in range(2 * parts):
            other_id = id_of(1 + other // parts, other % parts)
            shared = other_id == id_of(0, 0)
            for slot in range(1, parts):
                shared = shared | (other_id == id_of(0, slot))
            table[count] = other
            count = count + shared.astype(jnp.int32)
        table[2 * parts] = count

        def ids_along(axis):
            shape = (most, 1) if axis == 0 else (1, most)
            place = lax.broadcasted_iota(jnp.int32, shape, axis)
            ids = jnp.full(shape, -2, jnp.int32)
            for slot in range(3 * parts):
                if slot < parts:
                    slot_id = id_of(0, slot)
                else:
                    used = slot - parts < count
                    source = jnp.where(used, table[slot - parts], 0)
                    slot_id = id_of(1 + source // parts, lax.rem(source, parts))
                    slot_id = jnp.where(used, slot_id, -2)
                inside = (place >= slot * part_rows) & (place < (slot + 1) * part_rows)
                ids = jnp.where(inside, slot_id, ids)
            return ids

        bias[...] = jnp.where(ids_along(0) == ids_along(1), 0.0, MASKED)

    count = table[2 * parts]

    def other_part(slot, index):
        source = jnp.where(slot < count, table[slot], 0)
        place = lax.rem(source, parts)
        taken = [
            jnp.where(place == 0, first[index], rest[jnp.maximum(place - 1, 0), index])
            for first, rest in groups[1:]
        ]
        return jnp.where(source < parts, *taken)

    for size in range(rows, most + 1, rows):
        slots = (size - rows) // part_rows

        @pl.when((count <= slots) & (count > slots - parts))
        def _():
            for slot in range(slots):
                for index in range(4):
                    place = slice(slot * part_rows, (slot + 1) * part_rows)
                    gathered[index, place] = other_part(slot, index)
            values_of = []
            for index in range(4):
                first, rest = groups[0]
                mine = [first[index], rest[:, index].reshape(rows - part_rows, HD)]
                if slots:
                    mine.append(gathered[index, : size - rows])
                values_of.append(jnp.concatenate(mine))
            for out, result in zip(outs, attend_head(values_of, bias, size, rows)):
                result = result.astype(jnp.bfloat16)
                for slot in range(parts):
                    target = pl.multiple_of((me ^ slot) * part_rows, part_rows)
                    out[pl.ds(target, part_rows), :] = result[
                        slot * part_rows : (slot + 1) * part_rows
                    ]


def attend(image_ids, groups, outs, first_head):
    (first, rest) = groups[0]
    others, _, part_rows, width = rest.shape
    parts = others + 1
    rows = parts * part_rows
    heads = width // HD
    first_block = pl.BlockSpec((4, part_rows, HD), lambda h: (0, 0, h + first_head))
    rest_block = pl.BlockSpec((others, 4, part_rows, HD), lambda h: (0, 0, 0, h))
    out_spec = pl.BlockSpec((rows, HD), lambda h: (0, h + first_head))
    has_outs = outs is not None
    aliases = {7 + i: i for i in range(4)} if has_outs else {}
    return pl.pallas_call(
        functools.partial(attend_kernel, parts, has_outs),
        grid=(heads,),
        out_shape=[jax.ShapeDtypeStruct((rows, first.shape[2]), jnp.bfloat16)] * 4,
        in_specs=[pl.BlockSpec(memory_space=pltpu.SMEM)]
        + [first_block, rest_block] * 3
        + ([pl.BlockSpec(memory_space=pl.ANY)] * 4 if has_outs else []),
        out_specs=[out_spec] * 4,
        scratch_shapes=[
            pltpu.VMEM((3 * rows, 3 * rows), jnp.float32),
            pltpu.VMEM((4, 2 * rows, HD), jnp.bfloat16),
            pltpu.SMEM((2 * parts + 1,), jnp.int32),
        ],
        input_output_aliases=aliases,
        compiler_params=pltpu.CompilerParams(
            dimension_semantics=("arbitrary",), vmem_limit_bytes=VMEM_LIMIT
        ),
        cost_estimate=pl.CostEstimate(
            flops=heads * ATTEND_FLOPS, bytes_accessed=1, transcendentals=0
        ),
    )(image_ids, *groups[0], *groups[1], *groups[2], *(outs or ()))


def shards(queries, key_vectors, value_vectors, grad_output, image_ids):
    arrays = (queries, key_vectors, value_vectors, grad_output)
    parts = lax.axis_size("tensor")
    part_rows = queries.shape[0]
    head_total = queries.shape[1] // HD // parts
    near_ids = nearby_ids(image_ids, parts, part_rows)
    chunks = split_counts(head_total, CHUNK_SHARES)

    def cross(packed):
        return [
            swap_flipped(piece, "tensor", flip) for flip, piece in enumerate(packed, start=1)
        ]

    first, packed = pack(arrays, parts, chunks)
    received = [cross(packed[0])]
    near_first = swap_pairs(first, "dp", 0)
    far_first = swap_pairs(first, "dp", 1)
    firsts = [near_first, far_first]
    outs, out_history = None, []
    for number, (first_head, _) in enumerate(chunks):
        if number + 1 < len(chunks):
            held = [
                hold(piece, [done] + (firsts if number == 0 else []))
                for piece, done in zip(packed[number + 1], received[number])
            ]
            received.append(cross(held))
        after = [out_history[number - 2][0]] if number >= 2 else []
        after += firsts if number == 0 else []
        rest = join(received[number], after)
        near_rest = swap_pairs(rest, "dp", 0)
        far_rest = swap_pairs(rest, "dp", 1)
        groups = ((first, rest), (near_first, near_rest), (far_first, far_rest))
        outs = attend(near_ids, groups, outs, first_head)
        out_history.append(outs)
    return tuple(outs)


def solution(mesh):
    return jax.shard_map(
        shards,
        mesh=mesh,
        in_specs=(
            P(("dp", "tensor"), None),
            P(("dp", "tensor"), None),
            P(("dp", "tensor"), None),
            P(("dp", "tensor"), None),
            P(),
        ),
        out_specs=(P("dp", "tensor"), P("dp", "tensor"), P("dp", "tensor"), P("dp", "tensor")),
        check_vma=False,
    )
```

```python
import functools
import math

import jax
import jax.numpy as jnp
from jax import lax
from jax.experimental import pallas as pl
from jax.experimental.pallas import tpu as pltpu
from jax.sharding import PartitionSpec as P

HD = 128
SCALE = 1.0 / math.sqrt(HD)
EXP2_SCALE = SCALE * math.log2(math.e)
MASKED = -1e30
CHUNK_SHARES = (5, 4, 2, 1)
VMEM_LIMIT = 63 * 1024 * 1024
ATTEND_FLOPS = 2_500_000_000
SMALL_COST = pl.CostEstimate(flops=1, bytes_accessed=1, transcendentals=0)


def split_counts(total, shares):
    whole = sum(shares)
    edges = [round(total * sum(shares[:i]) / whole) for i in range(len(shares) + 1)]
    return [(a, b - a) for a, b in zip(edges[:-1], edges[1:]) if b > a]


def swap_pairs(block, axis, first):
    count = lax.axis_size(axis)
    route = []
    for low in range(first, count - 1, 2):
        route += [(low, low + 1), (low + 1, low)]
    return lax.ppermute(block, axis, route)


def nearby_ids(image_ids, parts, part_rows):
    shard = lax.axis_index("dp")
    padded = jnp.pad(image_ids[::part_rows], (parts, parts), constant_values=-1)
    odd = lax.rem(shard, 2)

    def ids_of(other):
        return lax.dynamic_slice_in_dim(padded, (other + 1) * parts, parts)

    return jnp.stack((ids_of(shard), ids_of(shard + 1 - 2 * odd), ids_of(shard - 1 + 2 * odd)))


def columns(array, part, stride, first, width):
    start = pl.multiple_of(part * stride + first, HD)
    return array.at[:, pl.ds(start, width)]


def pack_kernel(parts, stride, first, width, deps, *refs):
    arrays, (packed, stage, in_sems, out_sems) = refs[:4], refs[4 + deps :]
    loads, stores = [], []
    for part in range(parts):
        for index, array in enumerate(arrays):
            load = pltpu.make_async_copy(
                columns(array, part, stride, first, width),
                stage.at[part, index],
                in_sems.at[part * 4 + index],
            )
            load.start()
            loads.append(load)
    for part in range(parts):
        for load in loads[part * 4 : part * 4 + 4]:
            load.wait()
        store = pltpu.make_async_copy(stage.at[part], packed.at[part], out_sems.at[part])
        store.start()
        stores.append(store)
    for store in stores:
        store.wait()


def pack(arrays, parts, first, count, after):
    rows, total = arrays[0].shape
    width = count * HD
    return pl.pallas_call(
        functools.partial(
            pack_kernel, parts, total // parts, first * HD, width, len(after)
        ),
        out_shape=jax.ShapeDtypeStruct((parts, 4, rows, width), jnp.bfloat16),
        in_specs=[pl.BlockSpec(memory_space=pl.ANY)] * (4 + len(after)),
        out_specs=pl.BlockSpec(memory_space=pl.ANY),
        scratch_shapes=[
            pltpu.VMEM((parts, 4, rows, width), jnp.bfloat16),
            pltpu.SemaphoreType.DMA((parts * 4,)),
            pltpu.SemaphoreType.DMA((parts,)),
        ],
        compiler_params=pltpu.CompilerParams(vmem_limit_bytes=VMEM_LIMIT),
        cost_estimate=SMALL_COST,
    )(*arrays, *after)


def join_kernel(parts, stride, first, width, deps, *refs):
    arrays, received, refs = refs[:4], refs[4 : 3 + parts], refs[3 + parts + deps :]
    joined, stage, in_sems, out_sems = refs
    me = lax.axis_index("tensor")
    loads, stores = [], []
    for flip in range(1, parts):
        load = pltpu.make_async_copy(received[flip - 1], stage.at[flip], in_sems.at[3 + flip])
        load.start()
        loads.append([load])
    own = []
    for index, array in enumerate(arrays):
        load = pltpu.make_async_copy(
            columns(array, me, stride, first, width), stage.at[0, index], in_sems.at[index]
        )
        load.start()
        own.append(load)
    loads = [own] + loads
    for flip in range(parts):
        for load in loads[flip]:
            load.wait()
        store = pltpu.make_async_copy(stage.at[flip], joined.at[me ^ flip], out_sems.at[flip])
        store.start()
        stores.append(store)
    for store in stores:
        store.wait()


def join(arrays, received, first, after):
    parts = len(received) + 1
    rows, total = arrays[0].shape
    width = received[0].shape[2]
    return pl.pallas_call(
        functools.partial(
            join_kernel, parts, total // parts, first * HD, width, len(after)
        ),
        out_shape=jax.ShapeDtypeStruct((parts, 4, rows, width), jnp.bfloat16),
        in_specs=[pl.BlockSpec(memory_space=pl.ANY)] * (3 + parts + len(after)),
        out_specs=pl.BlockSpec(memory_space=pl.ANY),
        scratch_shapes=[
            pltpu.VMEM((parts, 4, rows, width), jnp.bfloat16),
            pltpu.SemaphoreType.DMA((parts + 3,)),
            pltpu.SemaphoreType.DMA((parts,)),
        ],
        compiler_params=pltpu.CompilerParams(vmem_limit_bytes=VMEM_LIMIT),
        cost_estimate=SMALL_COST,
    )(*arrays, *received, *after)


def own_kernel(stride, deps, *refs):
    arrays, (packed, stage, in_sems, out_sems) = refs[:4], refs[4 + deps :]
    me = lax.axis_index("tensor")
    loads, stores = [], []
    for index, array in enumerate(arrays):
        load = pltpu.make_async_copy(
            columns(array, me, stride, 0, stride), stage.at[index], in_sems.at[index]
        )
        load.start()
        loads.append(load)
    for index in range(4):
        loads[index].wait()
        store = pltpu.make_async_copy(stage.at[index], packed.at[index], out_sems.at[index])
        store.start()
        stores.append(store)
    for store in stores:
        store.wait()


def own_columns(arrays, parts, after):
    rows, total = arrays[0].shape
    shape = (4, rows, total // parts)
    return pl.pallas_call(
        functools.partial(own_kernel, total // parts, len(after)),
        out_shape=jax.ShapeDtypeStruct(shape, jnp.bfloat16),
        in_specs=[pl.BlockSpec(memory_space=pl.ANY)] * (4 + len(after)),
        out_specs=pl.BlockSpec(memory_space=pl.ANY),
        scratch_shapes=[
            pltpu.VMEM(shape, jnp.bfloat16),
            pltpu.SemaphoreType.DMA((4,)),
            pltpu.SemaphoreType.DMA((4,)),
        ],
        compiler_params=pltpu.CompilerParams(vmem_limit_bytes=VMEM_LIMIT),
        cost_estimate=SMALL_COST,
    )(*arrays, *after)


def others_kernel(others, *refs):
    crossed, (rest, stage, in_sems, out_sems) = refs[0], refs[-4:]
    me = lax.axis_index("tensor")
    loads, stores = [], []
    for other in range(others):
        load = pltpu.make_async_copy(
            crossed.at[me ^ (other + 1)], stage.at[other], in_sems.at[other]
        )
        load.start()
        loads.append(load)
    for other in range(others):
        loads[other].wait()
        store = pltpu.make_async_copy(stage.at[other], rest.at[other], out_sems.at[other])
        store.start()
        stores.append(store)
    for store in stores:
        store.wait()


def take_others(crossed, after):
    shape = (crossed.shape[0] - 1,) + crossed.shape[1:]
    return pl.pallas_call(
        functools.partial(others_kernel, shape[0]),
        out_shape=jax.ShapeDtypeStruct(shape, jnp.bfloat16),
        in_specs=[pl.BlockSpec(memory_space=pl.ANY)] * (1 + len(after)),
        out_specs=pl.BlockSpec(memory_space=pl.ANY),
        scratch_shapes=[
            pltpu.VMEM(shape, jnp.bfloat16),
            pltpu.SemaphoreType.DMA((shape[0],)),
            pltpu.SemaphoreType.DMA((shape[0],)),
        ],
        compiler_params=pltpu.CompilerParams(vmem_limit_bytes=VMEM_LIMIT),
        cost_estimate=SMALL_COST,
    )(crossed, *after)


def dot_nt(a, b):
    return lax.dot_general(a, b, (((1,), (1,)), ((), ())), preferred_element_type=jnp.float32)


def dot_tn(a, b):
    return lax.dot_general(a, b, (((0,), (0,)), ((), ())), preferred_element_type=jnp.float32)


def dot_nn(a, b):
    return jnp.dot(a, b, preferred_element_type=jnp.float32)


def attend_head(values_of, bias, size, rows):
    queries, keys, values, grads = values_of
    grad_k = grad_v = None
    for start in range(0, size, rows):
        tile = slice(start, start + rows)
        scores = dot_nt(keys, queries[tile]) + bias[:size, tile]
        weights = jnp.exp2((scores - jnp.max(scores, axis=0, keepdims=True)) * EXP2_SCALE)
        probs = weights * (1.0 / jnp.sum(weights, axis=0, keepdims=True))
        grad_probs = dot_nt(values, grads[tile])
        inner = jnp.sum(probs * grad_probs, axis=0, keepdims=True)
        low = probs.astype(jnp.bfloat16)
        grad_scores = (probs * (grad_probs - inner)).astype(jnp.bfloat16)
        tile_v = dot_nn(low[:rows], grads[tile])
        tile_k = dot_nn(grad_scores[:rows], queries[tile])
        if start == 0:
            attended = dot_tn(low, values)
            grad_q = dot_tn(grad_scores, keys)
            grad_k, grad_v = tile_k, tile_v
        else:
            grad_k, grad_v = grad_k + tile_k, grad_v + tile_v
    return attended, grad_q * SCALE, grad_k * SCALE, grad_v


def attend_kernel(parts, has_outs, *refs):
    image_ids, groups = refs[0], (refs[1:3], refs[3:5], refs[5:7])
    refs = refs[7 + (4 if has_outs else 0) :]
    outs, (bias, gathered, table) = refs[:4], refs[4:]
    part_rows = groups[0][0].shape[1]
    rows = parts * part_rows
    most = 3 * rows
    me = lax.axis_index("tensor")

    def id_of(group, slot):
        return image_ids[group, me ^ slot]

    @pl.when(pl.program_id(0) == 0)
    def _():
        count = jnp.int32(0)
        for other in range(2 * parts):
            other_id = id_of(1 + other // parts, other % parts)
            shared = other_id == id_of(0, 0)
            for slot in range(1, parts):
                shared = shared | (other_id == id_of(0, slot))
            table[count] = other
            count = count + shared.astype(jnp.int32)
        table[2 * parts] = count

        def ids_along(axis, size):
            shape = (size, 1) if axis == 0 else (1, size)
            place = lax.broadcasted_iota(jnp.int32, shape, axis)
            ids = jnp.full(shape, -2, jnp.int32)
            for slot in range(size // part_rows):
                if slot < parts:
                    slot_id = id_of(0, slot)
                else:
                    used = slot - parts < count
                    source = jnp.where(used, table[slot - parts], 0)
                    slot_id = id_of(1 + source // parts, lax.rem(source, parts))
                    slot_id = jnp.where(used, slot_id, -2)
                inside = (place >= slot * part_rows) & (place < (slot + 1) * part_rows)
                ids = jnp.where(inside, slot_id, ids)
            return ids

        for size in range(rows, most + 1, rows):
            slots = (size - rows) // part_rows

            @pl.when((count <= slots) & (count > slots - parts))
            def _():
                same = ids_along(0, size) == ids_along(1, size)
                bias[:size, :size] = jnp.where(same, 0.0, MASKED)

    count = table[2 * parts]

    def other_part(slot, index):
        source = jnp.where(slot < count, table[slot], 0)
        place = lax.rem(source, parts)
        taken = [
            jnp.where(place == 0, first[index], rest[jnp.maximum(place - 1, 0), index])
            for first, rest in groups[1:]
        ]
        return jnp.where(source < parts, *taken)

    for size in range(rows, most + 1, rows):
        slots = (size - rows) // part_rows

        @pl.when((count <= slots) & (count > slots - parts))
        def _():
            for slot in range(slots):
                for index in range(4):
                    place = slice(slot * part_rows, (slot + 1) * part_rows)
                    gathered[index, place] = other_part(slot, index)
            values_of = []
            for index in range(4):
                first, rest = groups[0]
                mine = [first[index], rest[:, index].reshape(rows - part_rows, HD)]
                if slots:
                    mine.append(gathered[index, : size - rows])
                values_of.append(jnp.concatenate(mine))
            for out, result in zip(outs, attend_head(values_of, bias, size, rows)):
                result = result.astype(jnp.bfloat16)
                for slot in range(parts):
                    target = pl.multiple_of((me ^ slot) * part_rows, part_rows)
                    out[pl.ds(target, part_rows), :] = result[
                        slot * part_rows : (slot + 1) * part_rows
                    ]


def attend(image_ids, groups, outs, first_head):
    (first, rest) = groups[0]
    others, _, part_rows, width = rest.shape
    parts = others + 1
    rows = parts * part_rows
    heads = width // HD
    first_block = pl.BlockSpec((4, part_rows, HD), lambda h: (0, 0, h + first_head))
    rest_block = pl.BlockSpec((others, 4, part_rows, HD), lambda h: (0, 0, 0, h))
    out_spec = pl.BlockSpec((rows, HD), lambda h: (0, h + first_head))
    has_outs = outs is not None
    aliases = {7 + i: i for i in range(4)} if has_outs else {}
    return pl.pallas_call(
        functools.partial(attend_kernel, parts, has_outs),
        grid=(heads,),
        out_shape=[jax.ShapeDtypeStruct((rows, first.shape[2]), jnp.bfloat16)] * 4,
        in_specs=[pl.BlockSpec(memory_space=pltpu.SMEM)]
        + [first_block, rest_block] * 3
        + ([pl.BlockSpec(memory_space=pl.ANY)] * 4 if has_outs else []),
        out_specs=[out_spec] * 4,
        scratch_shapes=[
            pltpu.VMEM((3 * rows, 3 * rows), jnp.float32),
            pltpu.VMEM((4, 2 * rows, HD), jnp.bfloat16),
            pltpu.SMEM((2 * parts + 1,), jnp.int32),
        ],
        input_output_aliases=aliases,
        compiler_params=pltpu.CompilerParams(
            dimension_semantics=("arbitrary",), vmem_limit_bytes=VMEM_LIMIT
        ),
        cost_estimate=pl.CostEstimate(
            flops=heads * ATTEND_FLOPS, bytes_accessed=1, transcendentals=0
        ),
    )(image_ids, *groups[0], *groups[1], *groups[2], *(outs or ()))


def shards(queries, key_vectors, value_vectors, grad_output, image_ids):
    arrays = (queries, key_vectors, value_vectors, grad_output)
    parts = lax.axis_size("tensor")
    part_rows = queries.shape[0]
    head_total = queries.shape[1] // HD // parts
    near_ids = nearby_ids(image_ids, parts, part_rows)
    chunks = split_counts(head_total, CHUNK_SHARES)

    packed = [pack(arrays, parts, *chunk, []) for chunk in chunks[:2]]
    first = own_columns(arrays, parts, [packed[0]])
    near_first = swap_pairs(first, "dp", 0)
    far_first = swap_pairs(first, "dp", 1)
    outs, out_history = None, []
    for number, (first_head, _) in enumerate(chunks):
        crossed = lax.all_to_all(packed[number], "tensor", split_axis=0, concat_axis=0, tiled=True)
        after = packed[number + 1 : number + 2]
        after += [near_first, far_first] if number == 0 else []
        if number >= 2:
            after.append(out_history[number - 2][0])
        rest = take_others(crossed, after)
        if number + 2 < len(chunks):
            packed.append(pack(arrays, parts, *chunks[number + 2], [rest]))
        near_rest = swap_pairs(rest, "dp", 0)
        far_rest = swap_pairs(rest, "dp", 1)
        groups = ((first, rest), (near_first, near_rest), (far_first, far_rest))
        outs = attend(near_ids, groups, outs, first_head)
        out_history.append(outs)
    return tuple(outs)


def solution(mesh):
    return jax.shard_map(
        shards,
        mesh=mesh,
        in_specs=(
            P(("dp", "tensor"), None),
            P(("dp", "tensor"), None),
            P(("dp", "tensor"), None),
            P(("dp", "tensor"), None),
            P(),
        ),
        out_specs=(P("dp", "tensor"), P("dp", "tensor"), P("dp", "tensor"), P("dp", "tensor")),
        check_vma=False,
    )
```

```python
import functools
import math

import jax
import jax.numpy as jnp
from jax import lax
from jax.experimental import pallas as pl
from jax.experimental.pallas import tpu as pltpu
from jax.sharding import PartitionSpec as P

HD = 128
SCALE = 1.0 / math.sqrt(HD)
EXP2_SCALE = SCALE * math.log2(math.e)
MASKED = -1e30
CHUNK_SHARES = (6, 4, 2)
VMEM_LIMIT = 63 * 1024 * 1024
ATTEND_FLOPS = 1_500_000_000
SMALL_COST = pl.CostEstimate(flops=1, bytes_accessed=1, transcendentals=0)


def split_counts(total, shares):
    whole = sum(shares)
    edges = [round(total * sum(shares[:i]) / whole) for i in range(len(shares) + 1)]
    return [(a, b - a) for a, b in zip(edges[:-1], edges[1:]) if b > a]


def swap_pairs(block, axis, first):
    count = lax.axis_size(axis)
    route = []
    for low in range(first, count - 1, 2):
        route += [(low, low + 1), (low + 1, low)]
    return lax.ppermute(block, axis, route)


def swap_flipped(block, axis, flip):
    return lax.ppermute(block, axis, [(i, i ^ flip) for i in range(lax.axis_size(axis))])


def nearby_ids(image_ids, parts, part_rows):
    shard = lax.axis_index("dp")
    padded = jnp.pad(image_ids[::part_rows], (parts, parts), constant_values=-1)
    odd = lax.rem(shard, 2)

    def ids_of(other):
        return lax.dynamic_slice_in_dim(padded, (other + 1) * parts, parts)

    return jnp.stack((ids_of(shard), ids_of(shard + 1 - 2 * odd), ids_of(shard - 1 + 2 * odd)))


def columns(array, part, stride, first, width):
    start = pl.multiple_of(part * stride + first, HD)
    return array.at[:, pl.ds(start, width)]


def pack_kernel(stride, jobs, *refs):
    arrays, packed, (stage, in_sems, out_sems) = refs[:4], refs[4:-3], refs[-3:]
    me = lax.axis_index("tensor")
    loads, stores = [], []
    for number, (flip, first, count) in enumerate(jobs):
        for index, array in enumerate(arrays):
            load = pltpu.make_async_copy(
                columns(array, me ^ flip, stride, first * HD, count * HD),
                stage.at[flip, index, :, pl.ds(first * HD, count * HD)],
                in_sems.at[number * 4 + index],
            )
            load.start()
            loads.append(load)
    for number, (flip, first, count) in enumerate(jobs):
        for load in loads[number * 4 : number * 4 + 4]:
            load.wait()
        store = pltpu.make_async_copy(
            stage.at[flip, :, :, pl.ds(first * HD, count * HD)],
            packed[number],
            out_sems.at[number],
        )
        store.start()
        stores.append(store)
    for store in stores:
        store.wait()


def pack(arrays, parts, jobs):
    rows, total = arrays[0].shape
    stride = total // parts
    return pl.pallas_call(
        functools.partial(pack_kernel, stride, jobs),
        out_shape=[
            jax.ShapeDtypeStruct((4, rows, count * HD), jnp.bfloat16) for _, _, count in jobs
        ],
        in_specs=[pl.BlockSpec(memory_space=pl.ANY)] * 4,
        out_specs=[pl.BlockSpec(memory_space=pl.ANY)] * len(jobs),
        scratch_shapes=[
            pltpu.VMEM((parts, 4, rows, stride), jnp.bfloat16),
            pltpu.SemaphoreType.DMA((4 * len(jobs),)),
            pltpu.SemaphoreType.DMA((len(jobs),)),
        ],
        compiler_params=pltpu.CompilerParams(vmem_limit_bytes=VMEM_LIMIT),
        cost_estimate=SMALL_COST,
    )(*arrays)


def hold(array, after):
    return pl.pallas_call(
        lambda *refs: None,
        out_shape=jax.ShapeDtypeStruct(array.shape, array.dtype),
        in_specs=[pl.BlockSpec(memory_space=pl.ANY)] * (1 + len(after)),
        out_specs=pl.BlockSpec(memory_space=pl.ANY),
        input_output_aliases={0: 0},
        compiler_params=pltpu.CompilerParams(vmem_limit_bytes=VMEM_LIMIT),
        cost_estimate=SMALL_COST,
    )(array, *after)


def dot_nt(a, b):
    return lax.dot_general(a, b, (((1,), (1,)), ((), ())), preferred_element_type=jnp.float32)


def dot_tn(a, b):
    return lax.dot_general(a, b, (((0,), (0,)), ((), ())), preferred_element_type=jnp.float32)


def dot_nn(a, b):
    return jnp.dot(a, b, preferred_element_type=jnp.float32)


def attend_head(values_of, bias, size, rows):
    queries, keys, values, grads = values_of
    grad_k = grad_v = None
    for start in range(0, size, rows):
        tile = slice(start, start + rows)
        scores = dot_nt(keys, queries[tile]) + bias[:size, tile]
        weights = jnp.exp2((scores - jnp.max(scores, axis=0, keepdims=True)) * EXP2_SCALE)
        probs = weights * (1.0 / jnp.sum(weights, axis=0, keepdims=True))
        grad_probs = dot_nt(values, grads[tile])
        inner = jnp.sum(probs * grad_probs, axis=0, keepdims=True)
        low = probs.astype(jnp.bfloat16)
        grad_scores = (probs * (grad_probs - inner)).astype(jnp.bfloat16)
        tile_v = dot_nn(low[:rows], grads[tile])
        tile_k = dot_nn(grad_scores[:rows], queries[tile])
        if start == 0:
            attended = dot_tn(low, values)
            grad_q = dot_tn(grad_scores, keys)
            grad_k, grad_v = tile_k, tile_v
        else:
            grad_k, grad_v = grad_k + tile_k, grad_v + tile_v
    return attended, grad_q * SCALE, grad_k * SCALE, grad_v


def attend_kernel(parts, part_rows, heads, first_head, has_outs, *refs):
    image_ids, refs = refs[0], refs[1:]
    mine, others = refs[:parts], refs[parts : 3 * parts]
    refs = refs[3 * parts + (4 if has_outs else 0) :]
    outs, (bias, window, table, sems) = refs[:4], refs[4:]
    rows = parts * part_rows
    most = 3 * rows
    me = lax.axis_index("tensor")
    head = pl.program_id(0)

    def head_columns(ref, number):
        if ref.shape[2] > heads * HD:
            number = number + first_head
        return ref.at[:, :, pl.ds(pl.multiple_of(number * HD, HD), HD)]

    def copy_of(ref, number, place, sem):
        buffer = lax.rem(number, 2)
        start = pl.multiple_of(place * part_rows, part_rows)
        return pltpu.make_async_copy(
            head_columns(ref, number),
            window.at[buffer, :, pl.ds(start, part_rows), :],
            sems.at[buffer, sem],
        )

    def fetch(number):
        for flip in range(parts):
            copy_of(mine[flip], number, me ^ flip, flip).start()
        for slot in range(2 * parts):

            @pl.when(slot < table[2 * parts])
            def _():
                for source in range(2 * parts):

                    @pl.when(table[slot] == source)
                    def _():
                        copy_of(others[source], number, parts + slot, parts + slot).start()

    def await_fetch(number):
        for flip in range(parts):
            copy_of(mine[flip], number, me ^ flip, flip).wait()
        for slot in range(2 * parts):

            @pl.when(slot < table[2 * parts])
            def _():
                copy_of(others[0], number, parts + slot, parts + slot).wait()

    @pl.when(head == 0)
    def _():
        window[...] = jnp.zeros_like(window)
        count = jnp.int32(0)
        for other in range(2 * parts):
            side, flip = 1 + other // parts, other % parts
            other_id = image_ids[side, me ^ flip]
            shared = other_id == image_ids[0, 0]
            for part in range(1, parts):
                shared = shared | (other_id == image_ids[0, part])
            table[count] = other
            count = count + shared.astype(jnp.int32)
        table[2 * parts] = count
        fetch(0)

        def ids_along(axis, size):
            shape = (size, 1) if axis == 0 else (1, size)
            place = lax.broadcasted_iota(jnp.int32, shape, axis)
            ids = jnp.full(shape, -2, jnp.int32)
            for slot in range(size // part_rows):
                if slot < parts:
                    slot_id = image_ids[0, slot]
                else:
                    used = slot - parts < count
                    source = jnp.where(used, table[slot - parts], 0)
                    slot_id = image_ids[1 + source // parts, me ^ lax.rem(source, parts)]
                    slot_id = jnp.where(used, slot_id, -2)
                inside = (place >= slot * part_rows) & (place < (slot + 1) * part_rows)
                ids = jnp.where(inside, slot_id, ids)
            return ids

        for size in range(rows, most + 1, rows):
            slots = (size - rows) // part_rows

            @pl.when((count <= slots) & (count > slots - parts))
            def _():
                same = ids_along(0, size) == ids_along(1, size)
                bias[:size, :size] = jnp.where(same, 0.0, MASKED)

    @pl.when(head + 1 < heads)
    def _():
        fetch(head + 1)

    await_fetch(head)
    count = table[2 * parts]
    buffer = lax.rem(head, 2)
    for size in range(rows, most + 1, rows):
        slots = (size - rows) // part_rows

        @pl.when((count <= slots) & (count > slots - parts))
        def _():
            values_of = [window[buffer, index, :size] for index in range(4)]
            for out, result in zip(outs, attend_head(values_of, bias, size, rows)):
                out[...] = result.astype(jnp.bfloat16)


def attend(image_ids, groups, outs, first_head, heads):
    parts = len(groups[0])
    _, part_rows, width = groups[0][0].shape
    rows = parts * part_rows
    out_spec = pl.BlockSpec((rows, HD), lambda h: (0, h + first_head))
    has_outs = outs is not None
    pieces = [piece for group in groups for piece in group]
    aliases = {1 + len(pieces) + i: i for i in range(4)} if has_outs else {}
    return pl.pallas_call(
        functools.partial(attend_kernel, parts, part_rows, heads, first_head, has_outs),
        grid=(heads,),
        out_shape=[jax.ShapeDtypeStruct((rows, width), jnp.bfloat16)] * 4,
        in_specs=[pl.BlockSpec(memory_space=pltpu.SMEM)]
        + [pl.BlockSpec(memory_space=pl.ANY)] * (len(pieces) + (4 if has_outs else 0)),
        out_specs=[out_spec] * 4,
        scratch_shapes=[
            pltpu.VMEM((3 * rows, 3 * rows), jnp.float32),
            pltpu.VMEM((2, 4, 3 * rows, HD), jnp.bfloat16),
            pltpu.SMEM((2 * parts + 1,), jnp.int32),
            pltpu.SemaphoreType.DMA((2, 3 * parts)),
        ],
        input_output_aliases=aliases,
        compiler_params=pltpu.CompilerParams(
            dimension_semantics=("arbitrary",), vmem_limit_bytes=VMEM_LIMIT
        ),
        cost_estimate=pl.CostEstimate(
            flops=heads * ATTEND_FLOPS, bytes_accessed=1, transcendentals=0
        ),
    )(image_ids, *pieces, *(outs or ()))


def shards(queries, key_vectors, value_vectors, grad_output, image_ids):
    arrays = (queries, key_vectors, value_vectors, grad_output)
    parts = lax.axis_size("tensor")
    part_rows = queries.shape[0]
    head_total = queries.shape[1] // HD // parts
    near_ids = nearby_ids(image_ids, parts, part_rows)
    chunks = split_counts(head_total, CHUNK_SHARES)
    last = parts - 1

    jobs = [(flip, 0, head_total) for flip in range(last)]
    jobs += [(last, first, count) for first, count in chunks]
    packed = pack(arrays, parts, jobs)

    def spread(piece):
        return piece, swap_pairs(piece, "dp", 0), swap_pairs(piece, "dp", 1)

    wide = [spread(packed[0])]
    for flip in range(1, last):
        wide.append(spread(swap_flipped(packed[flip], "tensor", flip)))
    outs, narrow = None, []
    for number, (first_head, count) in enumerate(chunks):
        piece = packed[last + number]
        if number < 2:
            piece = hold(piece, [wide[max(1, last - 2 + number)][0]])
        else:
            piece = hold(piece, [narrow[number - 2][0]])
        narrow.append(spread(swap_flipped(piece, "tensor", last)))
    for number, (first_head, count) in enumerate(chunks):
        groups = list(zip(*wide, narrow[number]))
        outs = attend(near_ids, groups, outs, first_head, count)
    return tuple(outs)


def solution(mesh):
    return jax.shard_map(
        shards,
        mesh=mesh,
        in_specs=(
            P(("dp", "tensor"), None),
            P(("dp", "tensor"), None),
            P(("dp", "tensor"), None),
            P(("dp", "tensor"), None),
            P(),
        ),
        out_specs=(P("dp", "tensor"), P("dp", "tensor"), P("dp", "tensor"), P("dp", "tensor")),
        check_vma=False,
    )
```

```python
import functools
import math

import jax
import jax.numpy as jnp
from jax import lax
from jax.experimental import pallas as pl
from jax.experimental.pallas import tpu as pltpu
from jax.sharding import PartitionSpec as P

HD = 128
SCALE = 1.0 / math.sqrt(HD)
EXP2_SCALE = SCALE * math.log2(math.e)
MASKED = -1e30
HALF_SHARES = (6, 6)
CHUNK_SHARES = (6, 4, 2)
VMEM_LIMIT = 64 * 1024 * 1024 - 256 * 1024
ATTEND_FLOPS = 1_500_000_000
SMALL_COST = pl.CostEstimate(flops=1, bytes_accessed=1, transcendentals=0)


def split_counts(total, shares):
    whole = sum(shares)
    edges = [round(total * sum(shares[:i]) / whole) for i in range(len(shares) + 1)]
    return [(a, b - a) for a, b in zip(edges[:-1], edges[1:]) if b > a]


def swap_pairs(block, axis, first):
    count = lax.axis_size(axis)
    route = []
    for low in range(first, count - 1, 2):
        route += [(low, low + 1), (low + 1, low)]
    return lax.ppermute(block, axis, route)


def swap_flipped(block, axis, flip):
    return lax.ppermute(block, axis, [(i, i ^ flip) for i in range(lax.axis_size(axis))])


def nearby_ids(image_ids, parts, part_rows):
    shard = lax.axis_index("dp")
    padded = jnp.pad(image_ids[::part_rows], (parts, parts), constant_values=-1)
    odd = lax.rem(shard, 2)

    def ids_of(other):
        return lax.dynamic_slice_in_dim(padded, (other + 1) * parts, parts)

    return jnp.stack((ids_of(shard), ids_of(shard + 1 - 2 * odd), ids_of(shard - 1 + 2 * odd)))


def columns(array, part, stride, first, width):
    start = pl.multiple_of(part * stride + first, HD)
    return array.at[:, pl.ds(start, width)]


def pack_kernel(stride, jobs, *refs):
    arrays, packed, (stage, in_sems, out_sems) = refs[:4], refs[4:-3], refs[-3:]
    me = lax.axis_index("tensor")
    loads, stores = [], []
    for number, (flip, first, count) in enumerate(jobs):
        for index, array in enumerate(arrays):
            load = pltpu.make_async_copy(
                columns(array, me ^ flip, stride, first * HD, count * HD),
                stage.at[flip, index, :, pl.ds(first * HD, count * HD)],
                in_sems.at[number * 4 + index],
            )
            load.start()
            loads.append(load)
    for number, (flip, first, count) in enumerate(jobs):
        for load in loads[number * 4 : number * 4 + 4]:
            load.wait()
        store = pltpu.make_async_copy(
            stage.at[flip, :, :, pl.ds(first * HD, count * HD)],
            packed[number],
            out_sems.at[number],
        )
        store.start()
        stores.append(store)
    for store in stores:
        store.wait()


def pack(arrays, parts, jobs):
    rows, total = arrays[0].shape
    stride = total // parts
    return pl.pallas_call(
        functools.partial(pack_kernel, stride, jobs),
        out_shape=[
            jax.ShapeDtypeStruct((4, rows, count * HD), jnp.bfloat16) for _, _, count in jobs
        ],
        in_specs=[pl.BlockSpec(memory_space=pl.ANY)] * 4,
        out_specs=[pl.BlockSpec(memory_space=pl.ANY)] * len(jobs),
        scratch_shapes=[
            pltpu.VMEM((parts, 4, rows, stride), jnp.bfloat16),
            pltpu.SemaphoreType.DMA((4 * len(jobs),)),
            pltpu.SemaphoreType.DMA((len(jobs),)),
        ],
        compiler_params=pltpu.CompilerParams(vmem_limit_bytes=VMEM_LIMIT),
        cost_estimate=SMALL_COST,
    )(*arrays)


def hold(array, after):
    return pl.pallas_call(
        lambda *refs: None,
        out_shape=jax.ShapeDtypeStruct(array.shape, array.dtype),
        in_specs=[pl.BlockSpec(memory_space=pl.ANY)] * (1 + len(after)),
        out_specs=pl.BlockSpec(memory_space=pl.ANY),
        input_output_aliases={0: 0},
        compiler_params=pltpu.CompilerParams(vmem_limit_bytes=VMEM_LIMIT),
        cost_estimate=SMALL_COST,
    )(array, *after)


def dot_nt(a, b):
    return lax.dot_general(a, b, (((1,), (1,)), ((), ())), preferred_element_type=jnp.float32)


def dot_tn(a, b):
    return lax.dot_general(a, b, (((0,), (0,)), ((), ())), preferred_element_type=jnp.float32)


def dot_nn(a, b):
    return jnp.dot(a, b, preferred_element_type=jnp.float32)


def attend_head(values_of, bias, size, rows):
    queries, keys, values, grads = values_of
    grad_k = grad_v = None
    for start in range(0, size, rows):
        tile = slice(start, start + rows)
        scores = dot_nt(keys, queries[tile]) + bias[:size, tile]
        weights = jnp.exp2((scores - jnp.max(scores, axis=0, keepdims=True)) * EXP2_SCALE)
        probs = weights * (1.0 / jnp.sum(weights, axis=0, keepdims=True))
        grad_probs = dot_nt(values, grads[tile])
        inner = jnp.sum(probs * grad_probs, axis=0, keepdims=True)
        low = probs.astype(jnp.bfloat16)
        grad_scores = (probs * (grad_probs - inner)).astype(jnp.bfloat16)
        tile_v = dot_nn(low[:rows], grads[tile])
        tile_k = dot_nn(grad_scores[:rows], queries[tile])
        if start == 0:
            attended = dot_tn(low, values)
            grad_q = dot_tn(grad_scores, keys)
            grad_k, grad_v = tile_k, tile_v
        else:
            grad_k, grad_v = grad_k + tile_k, grad_v + tile_v
    return attended, grad_q * SCALE, grad_k * SCALE, grad_v


def attend_kernel(parts, part_rows, heads, offsets, has_outs, *refs):
    image_ids, refs = refs[0], refs[1:]
    mine, others = refs[:parts], refs[parts : 3 * parts]
    refs = refs[3 * parts + (4 if has_outs else 0) :]
    outs, (bias, window, slot_of, table, sems) = refs[:4], refs[4:]
    rows = parts * part_rows
    most = 3 * rows
    me = lax.axis_index("tensor")
    head = pl.program_id(0)

    def copy_of(ref, flip, number, place, sem):
        buffer = lax.rem(number, 2)
        start = pl.multiple_of(place * part_rows, part_rows)
        column = pl.multiple_of((number + offsets[flip]) * HD, HD)
        return pltpu.make_async_copy(
            ref.at[:, :, pl.ds(column, HD)],
            window.at[buffer, :, pl.ds(start, part_rows), :],
            sems.at[buffer, sem],
        )

    def copies(number, act):
        for flip in range(parts):
            act(copy_of(mine[flip], flip, number, me ^ flip, flip))
        for source in range(2 * parts):
            slot = slot_of[source]

            @pl.when(slot >= 0)
            def _():
                act(copy_of(others[source], source % parts, number, parts + slot, parts + source))

    @pl.when(head == 0)
    def _():
        count = jnp.int32(0)
        for source in range(2 * parts):
            side, flip = 1 + source // parts, source % parts
            other_id = image_ids[side, me ^ flip]
            shared = other_id == image_ids[0, 0]
            for part in range(1, parts):
                shared = shared | (other_id == image_ids[0, part])
            slot_of[source] = jnp.where(shared, count, -1)
            table[count] = other_id
            count = count + shared.astype(jnp.int32)
        table[2 * parts] = count
        window[...] = jnp.zeros_like(window)
        copies(0, lambda copy: copy.start())

        def ids_along(axis, size):
            shape = (size, 1) if axis == 0 else (1, size)
            place = lax.broadcasted_iota(jnp.int32, shape, axis)
            ids = jnp.full(shape, -2, jnp.int32)
            for slot in range(size // part_rows):
                if slot < parts:
                    slot_id = image_ids[0, slot]
                else:
                    slot_id = jnp.where(slot - parts < count, table[slot - parts], -2)
                inside = (place >= slot * part_rows) & (place < (slot + 1) * part_rows)
                ids = jnp.where(inside, slot_id, ids)
            return ids

        for size in range(rows, most + 1, rows):
            slots = (size - rows) // part_rows

            @pl.when((count <= slots) & (count > slots - parts))
            def _():
                same = ids_along(0, size) == ids_along(1, size)
                bias[:size, :size] = jnp.where(same, 0.0, MASKED)

    @pl.when(head + 1 < heads)
    def _():
        copies(head + 1, lambda copy: copy.start())

    copies(head, lambda copy: copy.wait())
    count = table[2 * parts]
    buffer = lax.rem(head, 2)
    for size in range(rows, most + 1, rows):
        slots = (size - rows) // part_rows

        @pl.when((count <= slots) & (count > slots - parts))
        def _():
            values_of = [window[buffer, index, :size] for index in range(4)]
            for out, result in zip(outs, attend_head(values_of, bias, size, rows)):
                out[...] = result.astype(jnp.bfloat16)


def attend(image_ids, groups, offsets, outs, first_head, heads):
    parts = len(groups[0])
    _, part_rows, width = groups[0][0].shape
    rows = parts * part_rows
    out_spec = pl.BlockSpec((rows, HD), lambda h: (0, h + first_head))
    has_outs = outs is not None
    pieces = [piece for group in groups for piece in group]
    aliases = {1 + len(pieces) + i: i for i in range(4)} if has_outs else {}
    return pl.pallas_call(
        functools.partial(attend_kernel, parts, part_rows, heads, offsets, has_outs),
        grid=(heads,),
        out_shape=[jax.ShapeDtypeStruct((rows, width), jnp.bfloat16)] * 4,
        in_specs=[pl.BlockSpec(memory_space=pltpu.SMEM)]
        + [pl.BlockSpec(memory_space=pl.ANY)] * (len(pieces) + (4 if has_outs else 0)),
        out_specs=[out_spec] * 4,
        scratch_shapes=[
            pltpu.VMEM((3 * rows, 3 * rows), jnp.float32),
            pltpu.VMEM((2, 4, 3 * rows, HD), jnp.bfloat16),
            pltpu.SMEM((2 * parts,), jnp.int32),
            pltpu.SMEM((2 * parts + 1,), jnp.int32),
            pltpu.SemaphoreType.DMA((2, 3 * parts)),
        ],
        input_output_aliases=aliases,
        compiler_params=pltpu.CompilerParams(
            dimension_semantics=("arbitrary",), vmem_limit_bytes=VMEM_LIMIT
        ),
        cost_estimate=pl.CostEstimate(
            flops=heads * ATTEND_FLOPS, bytes_accessed=1, transcendentals=0
        ),
    )(image_ids, *pieces, *(outs or ()))


def shards(queries, key_vectors, value_vectors, grad_output, image_ids):
    arrays = (queries, key_vectors, value_vectors, grad_output)
    parts = lax.axis_size("tensor")
    part_rows = queries.shape[0]
    head_total = queries.shape[1] // HD // parts
    near_ids = nearby_ids(image_ids, parts, part_rows)
    whole = [(0, head_total)]
    halves = split_counts(head_total, HALF_SHARES)
    chunks = split_counts(head_total, CHUNK_SHARES)
    last, middle = parts - 1, parts - 2

    jobs = [(middle, *halves[0]), (0, *whole[0])]
    jobs += [(flip, *whole[0]) for flip in range(1, middle)]
    jobs += [(middle, *half) for half in halves[1:]]
    jobs += [(last, *chunk) for chunk in chunks]
    packed = dict(zip(jobs, pack(arrays, parts, jobs)))
    crossed, spread = {(0, *whole[0]): packed[(0, *whole[0])]}, {}

    def cross(job, after):
        piece = hold(packed[job], after) if after else packed[job]
        crossed[job] = swap_flipped(piece, "tensor", job[0])
        return [piece]

    def send(job, after):
        held = hold(crossed[job], after) if after else crossed[job]
        spread[job] = (held, swap_pairs(held, "dp", 0), swap_pairs(held, "dp", 1))

    heavy = [(middle, *half) for half in halves] + [(last, *chunk) for chunk in chunks]
    light = [(flip, *whole[0]) for flip in range(1, middle)]
    order = [(0, *whole[0])] + heavy[:2] + light + heavy[2:]
    cross(heavy[0], [])
    for job in light:
        cross(job, [])
    for number, job in enumerate(order):
        after = []
        if number >= 1:
            after.append(spread[order[number - 1]][1])
        if number >= 2:
            after.append(spread[order[number - 2]][2])
        if job in heavy:
            place = heavy.index(job)
            if place + 1 < len(heavy) and heavy[place + 1] not in crossed:
                after += cross(heavy[place + 1], [crossed[job]])
        send(job, after)
    outs = None
    for first_head, count in chunks:
        jobs_of = []
        for flip in range(parts):
            parts_of = halves if flip == middle else chunks if flip == last else whole
            inside = [span for span in parts_of if span[0] <= first_head < sum(span)]
            jobs_of.append((flip, *inside[0]))
        groups = list(zip(*(spread[job] for job in jobs_of)))
        offsets = [first_head - job[1] for job in jobs_of]
        outs = attend(near_ids, groups, offsets, outs, first_head, count)
    return tuple(outs)


def solution(mesh):
    return jax.shard_map(
        shards,
        mesh=mesh,
        in_specs=(
            P(("dp", "tensor"), None),
            P(("dp", "tensor"), None),
            P(("dp", "tensor"), None),
            P(("dp", "tensor"), None),
            P(),
        ),
        out_specs=(P("dp", "tensor"), P("dp", "tensor"), P("dp", "tensor"), P("dp", "tensor")),
        check_vma=False,
    )
```

```python
import functools
import math

import jax
import jax.numpy as jnp
from jax import lax
from jax.experimental import pallas as pl
from jax.experimental.pallas import tpu as pltpu
from jax.sharding import PartitionSpec as P

HD = 128
SCALE = 1.0 / math.sqrt(HD)
EXP2_SCALE = SCALE * math.log2(math.e)
MASKED = -1e30
GROUPS = ((8,), (2, 2))
VMEM_LIMIT = 64 * 1024 * 1024 - 256 * 1024
ATTEND_FLOPS = 1_500_000_000
SMALL_COST = pl.CostEstimate(flops=1, bytes_accessed=1, transcendentals=0)


def split_counts(total, shares):
    whole = sum(shares)
    edges = [round(total * sum(shares[:i]) / whole) for i in range(len(shares) + 1)]
    return [(a, b - a) for a, b in zip(edges[:-1], edges[1:]) if b > a]


def swap_pairs(block, axis, first):
    count = lax.axis_size(axis)
    route = []
    for low in range(first, count - 1, 2):
        route += [(low, low + 1), (low + 1, low)]
    return lax.ppermute(block, axis, route)


def swap_flipped(block, axis, flip):
    return lax.ppermute(block, axis, [(i, i ^ flip) for i in range(lax.axis_size(axis))])


def nearby_ids(image_ids, parts, part_rows):
    shard = lax.axis_index("dp")
    padded = jnp.pad(image_ids[::part_rows], (parts, parts), constant_values=-1)
    odd = lax.rem(shard, 2)

    def ids_of(other):
        return lax.dynamic_slice_in_dim(padded, (other + 1) * parts, parts)

    return jnp.stack((ids_of(shard), ids_of(shard + 1 - 2 * odd), ids_of(shard - 1 + 2 * odd)))


def columns(array, part, stride, first, width):
    start = pl.multiple_of(part * stride + first, HD)
    return array.at[:, pl.ds(start, width)]


def pack_kernel(stride, jobs, *refs):
    arrays, packed, (stage, in_sems, out_sems) = refs[:4], refs[4:-3], refs[-3:]
    me = lax.axis_index("tensor")
    loads, stores = [], []
    for number, (flip, first, count) in enumerate(jobs):
        for index, array in enumerate(arrays):
            load = pltpu.make_async_copy(
                columns(array, me ^ flip, stride, first * HD, count * HD),
                stage.at[flip, index, :, pl.ds(first * HD, count * HD)],
                in_sems.at[number * 4 + index],
            )
            load.start()
            loads.append(load)
    for number, (flip, first, count) in enumerate(jobs):
        for load in loads[number * 4 : number * 4 + 4]:
            load.wait()
        store = pltpu.make_async_copy(
            stage.at[flip, :, :, pl.ds(first * HD, count * HD)],
            packed[number],
            out_sems.at[number],
        )
        store.start()
        stores.append(store)
    for store in stores:
        store.wait()


def pack(arrays, parts, jobs):
    rows, total = arrays[0].shape
    stride = total // parts
    return pl.pallas_call(
        functools.partial(pack_kernel, stride, jobs),
        out_shape=[
            jax.ShapeDtypeStruct((4, rows, count * HD), jnp.bfloat16) for _, _, count in jobs
        ],
        in_specs=[pl.BlockSpec(memory_space=pl.ANY)] * 4,
        out_specs=[pl.BlockSpec(memory_space=pl.ANY)] * len(jobs),
        scratch_shapes=[
            pltpu.VMEM((parts, 4, rows, stride), jnp.bfloat16),
            pltpu.SemaphoreType.DMA((4 * len(jobs),)),
            pltpu.SemaphoreType.DMA((len(jobs),)),
        ],
        compiler_params=pltpu.CompilerParams(vmem_limit_bytes=VMEM_LIMIT),
        cost_estimate=SMALL_COST,
    )(*arrays)


def join_kernel(pieces, *refs):
    received, (joined, stage, in_sems, out_sems) = refs[:pieces], refs[-4:]
    loads, stores = [], []
    for piece in range(pieces):
        load = pltpu.make_async_copy(received[piece], stage.at[piece], in_sems.at[piece])
        load.start()
        loads.append(load)
    for piece in range(pieces):
        loads[piece].wait()
        store = pltpu.make_async_copy(stage.at[piece], joined.at[piece], out_sems.at[piece])
        store.start()
        stores.append(store)
    for store in stores:
        store.wait()


def join(received, after):
    pieces = len(received)
    shape = (pieces,) + received[0].shape
    return pl.pallas_call(
        functools.partial(join_kernel, pieces),
        out_shape=jax.ShapeDtypeStruct(shape, jnp.bfloat16),
        in_specs=[pl.BlockSpec(memory_space=pl.ANY)] * (pieces + len(after)),
        out_specs=pl.BlockSpec(memory_space=pl.ANY),
        scratch_shapes=[
            pltpu.VMEM(shape, jnp.bfloat16),
            pltpu.SemaphoreType.DMA((pieces,)),
            pltpu.SemaphoreType.DMA((pieces,)),
        ],
        compiler_params=pltpu.CompilerParams(vmem_limit_bytes=VMEM_LIMIT),
        cost_estimate=SMALL_COST,
    )(*received, *after)


def hold(array, after):
    return pl.pallas_call(
        lambda *refs: None,
        out_shape=jax.ShapeDtypeStruct(array.shape, array.dtype),
        in_specs=[pl.BlockSpec(memory_space=pl.ANY)] * (1 + len(after)),
        out_specs=pl.BlockSpec(memory_space=pl.ANY),
        input_output_aliases={0: 0},
        compiler_params=pltpu.CompilerParams(vmem_limit_bytes=VMEM_LIMIT),
        cost_estimate=SMALL_COST,
    )(array, *after)


def dot_nt(a, b):
    return lax.dot_general(a, b, (((1,), (1,)), ((), ())), preferred_element_type=jnp.float32)


def dot_tn(a, b):
    return lax.dot_general(a, b, (((0,), (0,)), ((), ())), preferred_element_type=jnp.float32)


def dot_nn(a, b):
    return jnp.dot(a, b, preferred_element_type=jnp.float32)


def attend_head(values_of, slot_ids, lane_ids, part_rows, rows):
    queries, keys, values, grads = values_of
    size = keys.shape[0]
    slots = size // part_rows
    grad_k = grad_v = None

    def per_slot(array):
        return [array[slot * part_rows : (slot + 1) * part_rows] for slot in range(slots)]

    def over_slots(reduce, combine, arrays):
        total = reduce(arrays[0], axis=0, keepdims=True)
        for array in arrays[1:]:
            total = combine(total, reduce(array, axis=0, keepdims=True))
        return total

    for start in range(0, size, rows):
        tile = slice(start, start + rows)
        scores = [
            part + jnp.where(lane_ids[:, tile] == slot_id, 0.0, MASKED)
            for part, slot_id in zip(per_slot(dot_nt(keys, queries[tile])), slot_ids)
        ]
        row_max = over_slots(jnp.max, jnp.maximum, scores)
        weights = [jnp.exp2((part - row_max) * EXP2_SCALE) for part in scores]
        inverse = 1.0 / over_slots(jnp.sum, jnp.add, weights)
        probs = [part * inverse for part in weights]
        grad_probs = per_slot(dot_nt(values, grads[tile]))
        inner = over_slots(jnp.sum, jnp.add, [p * g for p, g in zip(probs, grad_probs)])
        low = jnp.concatenate([p.astype(jnp.bfloat16) for p in probs])
        grad_scores = jnp.concatenate(
            [(p * (g - inner)).astype(jnp.bfloat16) for p, g in zip(probs, grad_probs)]
        )
        tile_v = dot_nn(low[:rows], grads[tile])
        tile_k = dot_nn(grad_scores[:rows], queries[tile])
        if start == 0:
            attended = dot_tn(low, values)
            grad_q = dot_tn(grad_scores, keys)
            grad_k, grad_v = tile_k, tile_v
        else:
            grad_k, grad_v = grad_k + tile_k, grad_v + tile_v
    return attended, grad_q * SCALE, grad_k * SCALE, grad_v


def attend_kernel(parts, part_rows, steps, width, offsets, has_outs, *refs):
    image_ids, mine, sides = refs[0], refs[1:4], (refs[4:7], refs[7:10])
    refs = refs[10 + (4 if has_outs else 0) :]
    outs, (window, lane_ids, slot_of, table, sems) = refs[:4], refs[4:]
    rows = parts * part_rows
    most = 3 * rows
    last = parts - 1
    me = lax.axis_index("tensor")
    step = pl.program_id(0)

    def copy_of(group, flip, number, place, sem):
        kind = 0 if flip == 0 else 2 if flip == last else 1
        buffer = lax.rem(number, 2)
        start = pl.multiple_of(place * part_rows, part_rows)
        column = pl.multiple_of(number * width + offsets[kind] * HD, HD)
        source = group[kind].at[flip - 1] if kind == 1 else group[kind]
        return pltpu.make_async_copy(
            source.at[:, :, pl.ds(column, width)],
            window.at[buffer, :, pl.ds(start, part_rows), :],
            sems.at[buffer, sem],
        )

    def copies(number, act):
        for flip in range(parts):
            act(copy_of(mine, flip, number, me ^ flip, flip))
        for source in range(2 * parts):
            slot = slot_of[source]

            @pl.when(slot >= 0)
            def _():
                group = sides[source // parts]
                act(copy_of(group, source % parts, number, parts + slot, parts + source))

    @pl.when(step == 0)
    def _():
        count = jnp.int32(0)
        for slot in range(2 * parts):
            table[slot] = -2
        for source in range(2 * parts):
            side, flip = 1 + source // parts, source % parts
            other_id = image_ids[side, me ^ flip]
            shared = other_id == image_ids[0, 0]
            for part in range(1, parts):
                shared = shared | (other_id == image_ids[0, part])
            slot_of[source] = jnp.where(shared, count, -1)
            table[count] = jnp.where(shared, other_id, -2)
            count = count + shared.astype(jnp.int32)
        table[2 * parts] = count
        window[:, :, rows:] = jnp.zeros((2, 4, most - rows, width), window.dtype)
        copies(0, lambda copy: copy.start())
        place = lax.broadcasted_iota(jnp.int32, (8, most), 1)
        ids = jnp.full((8, most), -2, jnp.int32)
        for slot in range(3 * parts):
            slot_id = image_ids[0, slot] if slot < parts else table[slot - parts]
            inside = (place >= slot * part_rows) & (place < (slot + 1) * part_rows)
            ids = jnp.where(inside, slot_id, ids)
        lane_ids[...] = ids

    @pl.when(step + 1 < steps)
    def _():
        copies(step + 1, lambda copy: copy.start())

    copies(step, lambda copy: copy.wait())
    count = table[2 * parts]
    buffer = lax.rem(step, 2)
    for size in range(rows, most + 1, rows):
        slots = (size - rows) // part_rows

        @pl.when((count <= slots) & (count > slots - parts))
        def _():
            slot_ids = [image_ids[0, slot] for slot in range(parts)]
            slot_ids += [table[slot] for slot in range(slots)]
            for start in range(0, width, HD):
                head = slice(start, start + HD)
                values_of = [window[buffer, index, :size, head] for index in range(4)]
                results = attend_head(values_of, slot_ids, lane_ids[0:1], part_rows, rows)
                for out, result in zip(outs, results):
                    out[:, head] = result.astype(jnp.bfloat16)


def attend(image_ids, groups, offsets, outs, first_head, heads):
    _, part_rows, total = groups[0][0].shape
    parts = groups[0][1].shape[0] + 2
    rows = parts * part_rows
    width = HD * math.gcd(2, math.gcd(first_head, heads))
    steps = heads * HD // width
    first_block = first_head * HD // width
    out_spec = pl.BlockSpec((rows, width), lambda s: (0, s + first_block))
    has_outs = outs is not None
    pieces = [piece for group in groups for piece in group]
    aliases = {1 + len(pieces) + i: i for i in range(4)} if has_outs else {}
    return pl.pallas_call(
        functools.partial(
            attend_kernel, parts, part_rows, steps, width, offsets, has_outs
        ),
        grid=(steps,),
        out_shape=[jax.ShapeDtypeStruct((rows, total), jnp.bfloat16)] * 4,
        in_specs=[pl.BlockSpec(memory_space=pltpu.SMEM)]
        + [pl.BlockSpec(memory_space=pl.ANY)] * (len(pieces) + (4 if has_outs else 0)),
        out_specs=[out_spec] * 4,
        scratch_shapes=[
            pltpu.VMEM((2, 4, 3 * rows, width), jnp.bfloat16),
            pltpu.VMEM((8, 3 * rows), jnp.int32),
            pltpu.SMEM((2 * parts,), jnp.int32),
            pltpu.SMEM((2 * parts + 1,), jnp.int32),
            pltpu.SemaphoreType.DMA((2, 3 * parts)),
        ],
        input_output_aliases=aliases,
        compiler_params=pltpu.CompilerParams(
            dimension_semantics=("arbitrary",), vmem_limit_bytes=VMEM_LIMIT
        ),
        cost_estimate=pl.CostEstimate(
            flops=heads * ATTEND_FLOPS, bytes_accessed=1, transcendentals=0
        ),
    )(image_ids, *pieces, *(outs or ()))


def shards(queries, key_vectors, value_vectors, grad_output, image_ids):
    arrays = (queries, key_vectors, value_vectors, grad_output)
    parts = lax.axis_size("tensor")
    part_rows = queries.shape[0]
    head_total = queries.shape[1] // HD // parts
    near_ids = nearby_ids(image_ids, parts, part_rows)
    last = parts - 1
    spans = split_counts(head_total, [sum(shares) for shares in GROUPS])
    groups = []
    for (start, count), shares in zip(spans, GROUPS):
        groups.append([(start + first, size) for first, size in split_counts(count, shares)])

    jobs = []
    for span, chunks in zip(spans, groups):
        jobs += [(flip, *span) for flip in range(last - 1, 0, -1)]
        jobs += [(last, *chunk) for chunk in chunks]
    jobs.insert(last - 1, (0, 0, head_total))
    packed = dict(zip(jobs, pack(arrays, parts, jobs)))

    steps = []
    for span, chunks in zip(spans, groups):
        steps.append([(flip, *span) for flip in range(1, last)])
        steps += [[(last, *chunk)] for chunk in chunks]

    def cross(step, after):
        held = [hold(packed[job], after) if after else packed[job] for job in step]
        return held, [swap_flipped(piece, "tensor", job[0]) for job, piece in zip(step, held)]

    def spread(piece):
        return piece, swap_pairs(piece, "dp", 0), swap_pairs(piece, "dp", 1)

    _, crossed = cross(steps[0], [])
    sent = [spread(packed[(0, 0, head_total)])]
    outs, joined, number = None, None, 0
    for span, chunks in zip(spans, groups):
        for place in range(1 + len(chunks)):
            after = [sent[-1][1]] + [earlier[2] for earlier in sent[-2:-1]]
            received = crossed
            number += 1
            if number < len(steps):
                held, crossed = cross(steps[number], [received[-1]])
                after += held
            if place == 0:
                joined = spread(join(received, after))
                sent.append(joined)
                continue
            if outs is not None and place == len(chunks):
                after.append(outs[0])
            piece = spread(hold(received[0], after))
            sent.append(piece)
            first_head, count = chunks[place - 1]
            offsets = (first_head, first_head - span[0], 0)
            outs = attend(
                near_ids, list(zip(sent[0], joined, piece)), offsets, outs, first_head, count
            )
    return tuple(outs)


def solution(mesh):
    return jax.shard_map(
        shards,
        mesh=mesh,
        in_specs=(
            P(("dp", "tensor"), None),
            P(("dp", "tensor"), None),
            P(("dp", "tensor"), None),
            P(("dp", "tensor"), None),
            P(),
        ),
        out_specs=(P("dp", "tensor"), P("dp", "tensor"), P("dp", "tensor"), P("dp", "tensor")),
        check_vma=False,
    )
```

```python
import functools
import math

import jax
import jax.numpy as jnp
from jax import lax
from jax.experimental import pallas as pl
from jax.experimental.pallas import tpu as pltpu
from jax.sharding import PartitionSpec as P

HD = 128
SCALE = 1.0 / math.sqrt(HD)
EXP2_SCALE = SCALE * math.log2(math.e)
MASKED = -1e30
GROUPS = ((8,), (4,))
VMEM_LIMIT = 64 * 1024 * 1024 - 256 * 1024
ATTEND_FLOPS = 1_500_000_000
SMALL_COST = pl.CostEstimate(flops=1, bytes_accessed=1, transcendentals=0)


def split_counts(total, shares):
    whole = sum(shares)
    edges = [round(total * sum(shares[:i]) / whole) for i in range(len(shares) + 1)]
    return [(a, b - a) for a, b in zip(edges[:-1], edges[1:]) if b > a]


def swap_pairs(block, axis, first):
    count = lax.axis_size(axis)
    route = []
    for low in range(first, count - 1, 2):
        route += [(low, low + 1), (low + 1, low)]
    return lax.ppermute(block, axis, route)


def swap_flipped(block, axis, flip):
    return lax.ppermute(block, axis, [(i, i ^ flip) for i in range(lax.axis_size(axis))])


def nearby_ids(image_ids, parts, part_rows):
    shard = lax.axis_index("dp")
    padded = jnp.pad(image_ids[::part_rows], (parts, parts), constant_values=-1)
    odd = lax.rem(shard, 2)

    def ids_of(other):
        return lax.dynamic_slice_in_dim(padded, (other + 1) * parts, parts)

    return jnp.stack((ids_of(shard), ids_of(shard + 1 - 2 * odd), ids_of(shard - 1 + 2 * odd)))


def columns(array, part, stride, first, width):
    start = pl.multiple_of(part * stride + first, HD)
    return array.at[:, pl.ds(start, width)]


def pack_kernel(stride, jobs, *refs):
    arrays, packed, (stage, in_sems, out_sems) = refs[:4], refs[4:-3], refs[-3:]
    me = lax.axis_index("tensor")
    loads, stores = [], []
    for number, (flip, first, count) in enumerate(jobs):
        for index, array in enumerate(arrays):
            load = pltpu.make_async_copy(
                columns(array, me ^ flip, stride, first * HD, count * HD),
                stage.at[flip, index, :, pl.ds(first * HD, count * HD)],
                in_sems.at[number * 4 + index],
            )
            load.start()
            loads.append(load)
    for number, (flip, first, count) in enumerate(jobs):
        for load in loads[number * 4 : number * 4 + 4]:
            load.wait()
        store = pltpu.make_async_copy(
            stage.at[flip, :, :, pl.ds(first * HD, count * HD)],
            packed[number],
            out_sems.at[number],
        )
        store.start()
        stores.append(store)
    for store in stores:
        store.wait()


def pack(arrays, parts, jobs):
    rows, total = arrays[0].shape
    stride = total // parts
    return pl.pallas_call(
        functools.partial(pack_kernel, stride, jobs),
        out_shape=[
            jax.ShapeDtypeStruct((4, rows, count * HD), jnp.bfloat16) for _, _, count in jobs
        ],
        in_specs=[pl.BlockSpec(memory_space=pl.ANY)] * 4,
        out_specs=[pl.BlockSpec(memory_space=pl.ANY)] * len(jobs),
        scratch_shapes=[
            pltpu.VMEM((parts, 4, rows, stride), jnp.bfloat16),
            pltpu.SemaphoreType.DMA((4 * len(jobs),)),
            pltpu.SemaphoreType.DMA((len(jobs),)),
        ],
        compiler_params=pltpu.CompilerParams(vmem_limit_bytes=VMEM_LIMIT),
        cost_estimate=SMALL_COST,
    )(*arrays)


def join_kernel(pieces, *refs):
    received, (joined, stage, in_sems, out_sems) = refs[:pieces], refs[-4:]
    loads, stores = [], []
    for piece in range(pieces):
        load = pltpu.make_async_copy(received[piece], stage.at[piece], in_sems.at[piece])
        load.start()
        loads.append(load)
    for piece in range(pieces):
        loads[piece].wait()
        store = pltpu.make_async_copy(stage.at[piece], joined.at[piece], out_sems.at[piece])
        store.start()
        stores.append(store)
    for store in stores:
        store.wait()


def join(received, after):
    pieces = len(received)
    shape = (pieces,) + received[0].shape
    return pl.pallas_call(
        functools.partial(join_kernel, pieces),
        out_shape=jax.ShapeDtypeStruct(shape, jnp.bfloat16),
        in_specs=[pl.BlockSpec(memory_space=pl.ANY)] * (pieces + len(after)),
        out_specs=pl.BlockSpec(memory_space=pl.ANY),
        scratch_shapes=[
            pltpu.VMEM(shape, jnp.bfloat16),
            pltpu.SemaphoreType.DMA((pieces,)),
            pltpu.SemaphoreType.DMA((pieces,)),
        ],
        compiler_params=pltpu.CompilerParams(vmem_limit_bytes=VMEM_LIMIT),
        cost_estimate=SMALL_COST,
    )(*received, *after)


def hold(array, after):
    return pl.pallas_call(
        lambda *refs: None,
        out_shape=jax.ShapeDtypeStruct(array.shape, array.dtype),
        in_specs=[pl.BlockSpec(memory_space=pl.ANY)] * (1 + len(after)),
        out_specs=pl.BlockSpec(memory_space=pl.ANY),
        input_output_aliases={0: 0},
        compiler_params=pltpu.CompilerParams(vmem_limit_bytes=VMEM_LIMIT),
        cost_estimate=SMALL_COST,
    )(array, *after)


def dot_nt(a, b):
    return lax.dot_general(a, b, (((1,), (1,)), ((), ())), preferred_element_type=jnp.float32)


def dot_tn(a, b):
    return lax.dot_general(a, b, (((0,), (0,)), ((), ())), preferred_element_type=jnp.float32)


def dot_nn(a, b):
    return jnp.dot(a, b, preferred_element_type=jnp.float32)


def attend_head(values_of, slot_ids, lane_ids, part_rows, rows):
    queries, keys, values, grads = values_of
    size = keys.shape[0]
    slots = size // part_rows
    grad_k = grad_v = None

    def per_slot(array):
        return [array[slot * part_rows : (slot + 1) * part_rows] for slot in range(slots)]

    def over_slots(reduce, combine, arrays):
        total = reduce(arrays[0], axis=0, keepdims=True)
        for array in arrays[1:]:
            total = combine(total, reduce(array, axis=0, keepdims=True))
        return total

    for start in range(0, size, rows):
        tile = slice(start, start + rows)
        scores = [
            part + jnp.where(lane_ids[:, tile] == slot_id, 0.0, MASKED)
            for part, slot_id in zip(per_slot(dot_nt(keys, queries[tile])), slot_ids)
        ]
        row_max = over_slots(jnp.max, jnp.maximum, scores)
        weights = [jnp.exp2((part - row_max) * EXP2_SCALE) for part in scores]
        inverse = 1.0 / over_slots(jnp.sum, jnp.add, weights)
        probs = [part * inverse for part in weights]
        grad_probs = per_slot(dot_nt(values, grads[tile]))
        inner = over_slots(jnp.sum, jnp.add, [p * g for p, g in zip(probs, grad_probs)])
        low = jnp.concatenate([p.astype(jnp.bfloat16) for p in probs])
        grad_scores = jnp.concatenate(
            [(p * (g - inner)).astype(jnp.bfloat16) for p, g in zip(probs, grad_probs)]
        )
        tile_v = dot_nn(low[:rows], grads[tile])
        tile_k = dot_nn(grad_scores[:rows], queries[tile])
        if start == 0:
            attended = dot_tn(low, values)
            grad_q = dot_tn(grad_scores, keys)
            grad_k, grad_v = tile_k, tile_v
        else:
            grad_k, grad_v = grad_k + tile_k, grad_v + tile_v
    return attended, grad_q * SCALE, grad_k * SCALE, grad_v


def attend_kernel(parts, part_rows, steps, width, offsets, has_outs, *refs):
    image_ids, mine, sides = refs[0], refs[1:4], (refs[4:7], refs[7:10])
    refs = refs[10 + (4 if has_outs else 0) :]
    outs, (window, lane_ids, slot_of, table, sems) = refs[:4], refs[4:]
    rows = parts * part_rows
    most = 3 * rows
    last = parts - 1
    me = lax.axis_index("tensor")
    step = pl.program_id(0)

    def copy_of(group, flip, number, place, sem):
        kind = 0 if flip == 0 else 2 if flip == last else 1
        buffer = lax.rem(number, 2)
        start = pl.multiple_of(place * part_rows, part_rows)
        column = pl.multiple_of(number * width + offsets[kind] * HD, HD)
        source = group[kind].at[flip - 1] if kind == 1 else group[kind]
        return pltpu.make_async_copy(
            source.at[:, :, pl.ds(column, width)],
            window.at[buffer, :, pl.ds(start, part_rows), :],
            sems.at[buffer, sem],
        )

    def copies(number, act):
        for flip in range(parts):
            act(copy_of(mine, flip, number, me ^ flip, flip))
        for source in range(2 * parts):
            slot = slot_of[source]

            @pl.when(slot >= 0)
            def _():
                group = sides[source // parts]
                act(copy_of(group, source % parts, number, parts + slot, parts + source))

    @pl.when(step == 0)
    def _():
        count = jnp.int32(0)
        for slot in range(2 * parts):
            table[slot] = -2
        for source in range(2 * parts):
            side, flip = 1 + source // parts, source % parts
            other_id = image_ids[side, me ^ flip]
            shared = other_id == image_ids[0, 0]
            for part in range(1, parts):
                shared = shared | (other_id == image_ids[0, part])
            slot_of[source] = jnp.where(shared, count, -1)
            table[count] = jnp.where(shared, other_id, -2)
            count = count + shared.astype(jnp.int32)
        table[2 * parts] = count
        window[:, :, rows:] = jnp.zeros((2, 4, most - rows, width), window.dtype)
        copies(0, lambda copy: copy.start())
        place = lax.broadcasted_iota(jnp.int32, (8, most), 1)
        ids = jnp.full((8, most), -2, jnp.int32)
        for slot in range(3 * parts):
            slot_id = image_ids[0, slot] if slot < parts else table[slot - parts]
            inside = (place >= slot * part_rows) & (place < (slot + 1) * part_rows)
            ids = jnp.where(inside, slot_id, ids)
        lane_ids[...] = ids

    @pl.when(step + 1 < steps)
    def _():
        copies(step + 1, lambda copy: copy.start())

    copies(step, lambda copy: copy.wait())
    count = table[2 * parts]
    buffer = lax.rem(step, 2)
    for size in range(rows, most + 1, rows):
        slots = (size - rows) // part_rows

        @pl.when((count <= slots) & (count > slots - parts))
        def _():
            slot_ids = [image_ids[0, slot] for slot in range(parts)]
            slot_ids += [table[slot] for slot in range(slots)]
            for start in range(0, width, HD):
                head = slice(start, start + HD)
                values_of = [window[buffer, index, :size, head] for index in range(4)]
                results = attend_head(values_of, slot_ids, lane_ids[0:1], part_rows, rows)
                for out, result in zip(outs, results):
                    out[:, head] = result.astype(jnp.bfloat16)


def attend(image_ids, groups, offsets, outs, first_head, heads):
    _, part_rows, total = groups[0][0].shape
    parts = groups[0][1].shape[0] + 2
    rows = parts * part_rows
    width = HD * math.gcd(2, math.gcd(first_head, heads))
    steps = heads * HD // width
    first_block = first_head * HD // width
    out_spec = pl.BlockSpec((rows, width), lambda s: (0, s + first_block))
    has_outs = outs is not None
    pieces = [piece for group in groups for piece in group]
    aliases = {1 + len(pieces) + i: i for i in range(4)} if has_outs else {}
    return pl.pallas_call(
        functools.partial(
            attend_kernel, parts, part_rows, steps, width, offsets, has_outs
        ),
        grid=(steps,),
        out_shape=[jax.ShapeDtypeStruct((rows, total), jnp.bfloat16)] * 4,
        in_specs=[pl.BlockSpec(memory_space=pltpu.SMEM)]
        + [pl.BlockSpec(memory_space=pl.ANY)] * (len(pieces) + (4 if has_outs else 0)),
        out_specs=[out_spec] * 4,
        scratch_shapes=[
            pltpu.VMEM((2, 4, 3 * rows, width), jnp.bfloat16),
            pltpu.VMEM((8, 3 * rows), jnp.int32),
            pltpu.SMEM((2 * parts,), jnp.int32),
            pltpu.SMEM((2 * parts + 1,), jnp.int32),
            pltpu.SemaphoreType.DMA((2, 3 * parts)),
        ],
        input_output_aliases=aliases,
        compiler_params=pltpu.CompilerParams(
            dimension_semantics=("arbitrary",), vmem_limit_bytes=VMEM_LIMIT
        ),
        cost_estimate=pl.CostEstimate(
            flops=heads * ATTEND_FLOPS, bytes_accessed=1, transcendentals=0
        ),
    )(image_ids, *pieces, *(outs or ()))


def shards(queries, key_vectors, value_vectors, grad_output, image_ids):
    arrays = (queries, key_vectors, value_vectors, grad_output)
    parts = lax.axis_size("tensor")
    part_rows = queries.shape[0]
    head_total = queries.shape[1] // HD // parts
    near_ids = nearby_ids(image_ids, parts, part_rows)
    last = parts - 1
    spans = split_counts(head_total, [sum(shares) for shares in GROUPS])
    groups = []
    for (start, count), shares in zip(spans, GROUPS):
        groups.append([(start + first, size) for first, size in split_counts(count, shares)])

    jobs = []
    for span, chunks in zip(spans, groups):
        jobs += [(flip, *span) for flip in range(last - 1, 0, -1)]
        jobs += [(last, *chunk) for chunk in chunks]
    jobs.insert(last - 1, (0, 0, head_total))
    packed = dict(zip(jobs, pack(arrays, parts, jobs)))

    steps = []
    for span, chunks in zip(spans, groups):
        steps.append([(flip, *span) for flip in range(1, last)])
        steps += [[(last, *chunk)] for chunk in chunks]

    def cross(step, after):
        held = [hold(packed[job], after) if after else packed[job] for job in step]
        return held, [swap_flipped(piece, "tensor", job[0]) for job, piece in zip(step, held)]

    def spread(piece):
        return piece, swap_pairs(piece, "dp", 0), swap_pairs(piece, "dp", 1)

    _, crossed = cross(steps[0], [])
    sent = [spread(packed[(0, 0, head_total)])]
    outs, joined, number = None, None, 0
    for span, chunks in zip(spans, groups):
        for place in range(1 + len(chunks)):
            after = list(sent[-1][1:])
            received = crossed
            number += 1
            if number < len(steps):
                held, crossed = cross(steps[number], [received[-1]])
                after += held
            if place == 0:
                joined = spread(join(received, after))
                sent.append(joined)
                continue
            piece = spread(hold(received[0], after))
            sent.append(piece)
            first_head, count = chunks[place - 1]
            offsets = (first_head, first_head - span[0], 0)
            outs = attend(
                near_ids, list(zip(sent[0], joined, piece)), offsets, outs, first_head, count
            )
    return tuple(outs)


def solution(mesh):
    return jax.shard_map(
        shards,
        mesh=mesh,
        in_specs=(
            P(("dp", "tensor"), None),
            P(("dp", "tensor"), None),
            P(("dp", "tensor"), None),
            P(("dp", "tensor"), None),
            P(),
        ),
        out_specs=(P("dp", "tensor"), P("dp", "tensor"), P("dp", "tensor"), P("dp", "tensor")),
        check_vma=False,
    )
```

```python
import functools
import math

import jax
import jax.numpy as jnp
from jax import lax
from jax.experimental import pallas as pl
from jax.experimental.pallas import tpu as pltpu
from jax.sharding import PartitionSpec as P

HD = 128
SCALE = 1.0 / math.sqrt(HD)
EXP2_SCALE = SCALE * math.log2(math.e)
MASKED = -1e30
GROUPS = ((8,), (4,))
VMEM_LIMIT = 64 * 1024 * 1024 - 256 * 1024
ATTEND_FLOPS = 1_500_000_000
LARGE_COST = pl.CostEstimate(flops=40_000_000_000, bytes_accessed=1, transcendentals=0)
SMALL_COST = pl.CostEstimate(flops=1, bytes_accessed=1, transcendentals=0)


def split_counts(total, shares):
    whole = sum(shares)
    edges = [round(total * sum(shares[:i]) / whole) for i in range(len(shares) + 1)]
    return [(a, b - a) for a, b in zip(edges[:-1], edges[1:]) if b > a]


def swap_pairs(block, axis, first):
    count = lax.axis_size(axis)
    route = []
    for low in range(first, count - 1, 2):
        route += [(low, low + 1), (low + 1, low)]
    return lax.ppermute(block, axis, route)


def swap_flipped(block, axis, flip):
    return lax.ppermute(block, axis, [(i, i ^ flip) for i in range(lax.axis_size(axis))])


def nearby_ids(image_ids, parts, part_rows):
    shard = lax.axis_index("dp")
    padded = jnp.pad(image_ids[::part_rows], (parts, parts), constant_values=-1)
    odd = lax.rem(shard, 2)

    def ids_of(other):
        return lax.dynamic_slice_in_dim(padded, (other + 1) * parts, parts)

    return jnp.stack((ids_of(shard), ids_of(shard + 1 - 2 * odd), ids_of(shard - 1 + 2 * odd)))


def columns(array, part, stride, first, width):
    start = pl.multiple_of(part * stride + first, HD)
    return array.at[:, pl.ds(start, width)]


def pack_kernel(stride, jobs, *refs):
    arrays, packed, (stage, in_sems, out_sems) = refs[:4], refs[4:-3], refs[-3:]
    me = lax.axis_index("tensor")
    loads, stores = [], []
    for number, (flip, first, count) in enumerate(jobs):
        for index, array in enumerate(arrays):
            load = pltpu.make_async_copy(
                columns(array, me ^ flip, stride, first * HD, count * HD),
                stage.at[flip, index, :, pl.ds(first * HD, count * HD)],
                in_sems.at[number * 4 + index],
            )
            load.start()
            loads.append(load)
    for number, (flip, first, count) in enumerate(jobs):
        for load in loads[number * 4 : number * 4 + 4]:
            load.wait()
        store = pltpu.make_async_copy(
            stage.at[flip, :, :, pl.ds(first * HD, count * HD)],
            packed[number],
            out_sems.at[number],
        )
        store.start()
        stores.append(store)
    for store in stores:
        store.wait()


def pack(arrays, parts, jobs):
    rows, total = arrays[0].shape
    stride = total // parts
    return pl.pallas_call(
        functools.partial(pack_kernel, stride, jobs),
        out_shape=[
            jax.ShapeDtypeStruct((4, rows, count * HD), jnp.bfloat16) for _, _, count in jobs
        ],
        in_specs=[pl.BlockSpec(memory_space=pl.ANY)] * 4,
        out_specs=[pl.BlockSpec(memory_space=pl.ANY)] * len(jobs),
        scratch_shapes=[
            pltpu.VMEM((parts, 4, rows, stride), jnp.bfloat16),
            pltpu.SemaphoreType.DMA((4 * len(jobs),)),
            pltpu.SemaphoreType.DMA((len(jobs),)),
        ],
        compiler_params=pltpu.CompilerParams(vmem_limit_bytes=VMEM_LIMIT),
        cost_estimate=SMALL_COST,
    )(*arrays)


def join_kernel(pieces, *refs):
    received, (joined, stage, in_sems, out_sems) = refs[:pieces], refs[-4:]
    loads, stores = [], []
    for piece in range(pieces):
        load = pltpu.make_async_copy(received[piece], stage.at[piece], in_sems.at[piece])
        load.start()
        loads.append(load)
    for piece in range(pieces):
        loads[piece].wait()
        store = pltpu.make_async_copy(stage.at[piece], joined.at[piece], out_sems.at[piece])
        store.start()
        stores.append(store)
    for store in stores:
        store.wait()


def join(received, after):
    pieces = len(received)
    shape = (pieces,) + received[0].shape
    return pl.pallas_call(
        functools.partial(join_kernel, pieces),
        out_shape=jax.ShapeDtypeStruct(shape, jnp.bfloat16),
        in_specs=[pl.BlockSpec(memory_space=pl.ANY)] * (pieces + len(after)),
        out_specs=pl.BlockSpec(memory_space=pl.ANY),
        scratch_shapes=[
            pltpu.VMEM(shape, jnp.bfloat16),
            pltpu.SemaphoreType.DMA((pieces,)),
            pltpu.SemaphoreType.DMA((pieces,)),
        ],
        compiler_params=pltpu.CompilerParams(vmem_limit_bytes=VMEM_LIMIT),
        cost_estimate=LARGE_COST,
    )(*received, *after)


def hold(array, after, cost=SMALL_COST):
    return pl.pallas_call(
        lambda *refs: None,
        out_shape=jax.ShapeDtypeStruct(array.shape, array.dtype),
        in_specs=[pl.BlockSpec(memory_space=pl.ANY)] * (1 + len(after)),
        out_specs=pl.BlockSpec(memory_space=pl.ANY),
        input_output_aliases={0: 0},
        compiler_params=pltpu.CompilerParams(vmem_limit_bytes=VMEM_LIMIT),
        cost_estimate=cost,
    )(array, *after)


def dot_nt(a, b):
    return lax.dot_general(a, b, (((1,), (1,)), ((), ())), preferred_element_type=jnp.float32)


def dot_tn(a, b):
    return lax.dot_general(a, b, (((0,), (0,)), ((), ())), preferred_element_type=jnp.float32)


def dot_nn(a, b):
    return jnp.dot(a, b, preferred_element_type=jnp.float32)


def attend_heads(heads, slot_ids, lane_ids, part_rows, rows):
    size = heads[0][0].shape[0]
    slots = size // part_rows

    def per_slot(array):
        return [array[slot * part_rows : (slot + 1) * part_rows] for slot in range(slots)]

    def over_slots(reduce, combine, arrays):
        total = reduce(arrays[0], axis=0, keepdims=True)
        for array in arrays[1:]:
            total = combine(total, reduce(array, axis=0, keepdims=True))
        return total

    def products(head, start):
        queries, keys, values, grads = heads[head]
        tile = slice(start, start + rows)
        return dot_nt(keys, queries[tile]), dot_nt(values, grads[tile])

    def weigh(scores, grad_probs, start):
        lanes = lane_ids[:, start : start + rows]
        scores = [
            part + jnp.where(lanes == slot_id, 0.0, MASKED)
            for part, slot_id in zip(per_slot(scores), slot_ids)
        ]
        row_max = over_slots(jnp.max, jnp.maximum, scores)
        weights = [jnp.exp2((part - row_max) * EXP2_SCALE) for part in scores]
        inverse = 1.0 / over_slots(jnp.sum, jnp.add, weights)
        probs = [part * inverse for part in weights]
        grad_probs = per_slot(grad_probs)
        inner = over_slots(jnp.sum, jnp.add, [p * g for p, g in zip(probs, grad_probs)])
        low = jnp.concatenate([p.astype(jnp.bfloat16) for p in probs])
        grad_scores = [(p * (g - inner)).astype(jnp.bfloat16) for p, g in zip(probs, grad_probs)]
        return low, jnp.concatenate(grad_scores)

    def finish(head, low, grad_scores, start):
        queries, keys, values, grads = heads[head]
        tile = slice(start, start + rows)
        result = results[head]
        if start == 0:
            result[0] = dot_tn(values, low).astype(jnp.bfloat16).T
            result[1] = (dot_tn(keys, grad_scores) * SCALE).astype(jnp.bfloat16).T
            result[2] = result[3] = 0.0
        result[2] += dot_nn(grad_scores[:rows], queries[tile])
        result[3] += dot_nn(low[:rows], grads[tile])

    results = [[None] * 4 for _ in heads]
    work = [(head, start) for head in range(len(heads)) for start in range(0, size, rows)]
    ahead = products(*work[0])
    for number, (head, start) in enumerate(work):
        scores, grad_probs = ahead
        if number + 1 < len(work):
            ahead = products(*work[number + 1])
        finish(head, *weigh(scores, grad_probs, start), start)
    for result in results:
        result[2] = (result[2] * SCALE).astype(jnp.bfloat16)
        result[3] = result[3].astype(jnp.bfloat16)
    return results


def attend_kernel(parts, part_rows, steps, width, offsets, has_outs, *refs):
    image_ids, mine, sides = refs[0], refs[1:4], (refs[4:7], refs[7:10])
    refs = refs[10 + (4 if has_outs else 0) :]
    outs, (window, lane_ids, slot_of, table, sems) = refs[:4], refs[4:]
    rows = parts * part_rows
    most = 3 * rows
    last = parts - 1
    me = lax.axis_index("tensor")
    step = pl.program_id(0)

    def copy_of(group, flip, number, place, sem):
        kind = 0 if flip == 0 else 2 if flip == last else 1
        buffer = lax.rem(number, 2)
        start = pl.multiple_of(place * part_rows, part_rows)
        column = pl.multiple_of(number * width + offsets[kind] * HD, HD)
        source = group[kind].at[flip - 1] if kind == 1 else group[kind]
        return pltpu.make_async_copy(
            source.at[:, :, pl.ds(column, width)],
            window.at[buffer, :, pl.ds(start, part_rows), :],
            sems.at[buffer, sem],
        )

    def copies(number, act):
        for flip in range(parts):
            act(copy_of(mine, flip, number, me ^ flip, flip))
        for source in range(2 * parts):
            slot = slot_of[source]

            @pl.when(slot >= 0)
            def _():
                group = sides[source // parts]
                act(copy_of(group, source % parts, number, parts + slot, parts + source))

    @pl.when(step == 0)
    def _():
        count = jnp.int32(0)
        for slot in range(2 * parts):
            table[slot] = -2
        for source in range(2 * parts):
            side, flip = 1 + source // parts, source % parts
            other_id = image_ids[side, me ^ flip]
            shared = other_id == image_ids[0, 0]
            for part in range(1, parts):
                shared = shared | (other_id == image_ids[0, part])
            slot_of[source] = jnp.where(shared, count, -1)
            table[count] = jnp.where(shared, other_id, -2)
            count = count + shared.astype(jnp.int32)
        table[2 * parts] = count
        window[:, :, rows:] = jnp.zeros((2, 4, most - rows, width), window.dtype)
        copies(0, lambda copy: copy.start())
        place = lax.broadcasted_iota(jnp.int32, (8, most), 1)
        ids = jnp.full((8, most), -2, jnp.int32)
        for slot in range(3 * parts):
            slot_id = image_ids[0, slot] if slot < parts else table[slot - parts]
            inside = (place >= slot * part_rows) & (place < (slot + 1) * part_rows)
            ids = jnp.where(inside, slot_id, ids)
        lane_ids[...] = ids

    @pl.when(step + 1 < steps)
    def _():
        copies(step + 1, lambda copy: copy.start())

    copies(step, lambda copy: copy.wait())
    count = table[2 * parts]
    buffer = lax.rem(step, 2)
    for size in range(rows, most + 1, rows):
        slots = (size - rows) // part_rows

        @pl.when((count <= slots) & (count > slots - parts))
        def _():
            slot_ids = [image_ids[0, slot] for slot in range(parts)]
            slot_ids += [table[slot] for slot in range(slots)]
            spans = [slice(start, start + HD) for start in range(0, width, HD)]
            heads = [[window[buffer, i, :size, span] for i in range(4)] for span in spans]
            results = attend_heads(heads, slot_ids, lane_ids[0:1], part_rows, rows)
            for span, result in zip(spans, results):
                for out, part in zip(outs, result):
                    out[:, span] = part


def attend(image_ids, groups, offsets, outs, first_head, heads):
    _, part_rows, total = groups[0][0].shape
    parts = groups[0][1].shape[0] + 2
    rows = parts * part_rows
    width = HD * math.gcd(2, math.gcd(first_head, heads))
    steps = heads * HD // width
    first_block = first_head * HD // width
    out_spec = pl.BlockSpec((rows, width), lambda s: (0, s + first_block))
    has_outs = outs is not None
    pieces = [piece for group in groups for piece in group]
    aliases = {1 + len(pieces) + i: i for i in range(4)} if has_outs else {}
    return pl.pallas_call(
        functools.partial(
            attend_kernel, parts, part_rows, steps, width, offsets, has_outs
        ),
        grid=(steps,),
        out_shape=[jax.ShapeDtypeStruct((rows, total), jnp.bfloat16)] * 4,
        in_specs=[pl.BlockSpec(memory_space=pltpu.SMEM)]
        + [pl.BlockSpec(memory_space=pl.ANY)] * (len(pieces) + (4 if has_outs else 0)),
        out_specs=[out_spec] * 4,
        scratch_shapes=[
            pltpu.VMEM((2, 4, 3 * rows, width), jnp.bfloat16),
            pltpu.VMEM((8, 3 * rows), jnp.int32),
            pltpu.SMEM((2 * parts,), jnp.int32),
            pltpu.SMEM((2 * parts + 1,), jnp.int32),
            pltpu.SemaphoreType.DMA((2, 3 * parts)),
        ],
        input_output_aliases=aliases,
        compiler_params=pltpu.CompilerParams(
            dimension_semantics=("arbitrary",), vmem_limit_bytes=VMEM_LIMIT
        ),
        cost_estimate=pl.CostEstimate(
            flops=heads * ATTEND_FLOPS, bytes_accessed=1, transcendentals=0
        ),
    )(image_ids, *pieces, *(outs or ()))


def shards(queries, key_vectors, value_vectors, grad_output, image_ids):
    arrays = (queries, key_vectors, value_vectors, grad_output)
    parts = lax.axis_size("tensor")
    part_rows = queries.shape[0]
    head_total = queries.shape[1] // HD // parts
    near_ids = nearby_ids(image_ids, parts, part_rows)
    last = parts - 1
    spans = split_counts(head_total, [sum(shares) for shares in GROUPS])
    groups = []
    for (start, count), shares in zip(spans, GROUPS):
        groups.append([(start + first, size) for first, size in split_counts(count, shares)])

    jobs = []
    for span, chunks in zip(spans, groups):
        jobs += [(flip, *span) for flip in range(last - 1, 0, -1)]
        jobs += [(last, *chunk) for chunk in chunks]
    jobs.insert(last - 1, (0, 0, head_total))
    packed = dict(zip(jobs, pack(arrays, parts, jobs)))

    steps = []
    for span, chunks in zip(spans, groups):
        steps.append([(flip, *span) for flip in range(1, last)])
        steps += [[(last, *chunk)] for chunk in chunks]

    def cross(step, after):
        held = [hold(packed[job], after) if after else packed[job] for job in step]
        return held, [swap_flipped(piece, "tensor", job[0]) for job, piece in zip(step, held)]

    def spread(piece):
        return piece, swap_pairs(piece, "dp", 0), swap_pairs(piece, "dp", 1)

    _, crossed = cross(steps[0], [])
    sent = [spread(packed[(0, 0, head_total)])]
    outs, joined, number = None, None, 0
    for span, chunks in zip(spans, groups):
        for place in range(1 + len(chunks)):
            after = list(sent[-1][1:])
            received, held = crossed, []
            number += 1
            if number < len(steps):
                held, crossed = cross(steps[number], [received[-1]])
            elif outs is not None:
                after.append(outs[0])
            if place == 0:
                joined = spread(hold(join(received, held), after))
                sent.append(joined)
                continue
            piece = spread(hold(hold(received[0], held, LARGE_COST), after))
            sent.append(piece)
            first_head, count = chunks[place - 1]
            offsets = (first_head, first_head - span[0], 0)
            outs = attend(
                near_ids, list(zip(sent[0], joined, piece)), offsets, outs, first_head, count
            )
    return tuple(outs)


def solution(mesh):
    return jax.shard_map(
        shards,
        mesh=mesh,
        in_specs=(
            P(("dp", "tensor"), None),
            P(("dp", "tensor"), None),
            P(("dp", "tensor"), None),
            P(("dp", "tensor"), None),
            P(),
        ),
        out_specs=(P("dp", "tensor"), P("dp", "tensor"), P("dp", "tensor"), P("dp", "tensor")),
        check_vma=False,
    )
```

```python
import functools
import math

import jax
import jax.numpy as jnp
from jax import lax
from jax.experimental import pallas as pl
from jax.experimental.pallas import tpu as pltpu
from jax.sharding import PartitionSpec as P

HD = 128
SCALE = 1.0 / math.sqrt(HD)
EXP2_SCALE = SCALE * math.log2(math.e)
MASKED = -1e30
GROUPS = ((8,), (4,))
VMEM_LIMIT = 64 * 1024 * 1024 - 256 * 1024
ATTEND_FLOPS = 1_500_000_000
FLOPS_PER_BYTE = 62_500
SMALL_COST = pl.CostEstimate(flops=1, bytes_accessed=1, transcendentals=0)


def split_counts(total, shares):
    whole = sum(shares)
    edges = [round(total * sum(shares[:i]) / whole) for i in range(len(shares) + 1)]
    return [(a, b - a) for a, b in zip(edges[:-1], edges[1:]) if b > a]


def swap_pairs(block, axis, first):
    count = lax.axis_size(axis)
    route = []
    for low in range(first, count - 1, 2):
        route += [(low, low + 1), (low + 1, low)]
    return lax.ppermute(block, axis, route)


def swap_flipped(block, axis, flip):
    return lax.ppermute(block, axis, [(i, i ^ flip) for i in range(lax.axis_size(axis))])


def nearby_ids(image_ids, parts, part_rows):
    shard = lax.axis_index("dp")
    padded = jnp.pad(image_ids[::part_rows], (parts, parts), constant_values=-1)
    odd = lax.rem(shard, 2)

    def ids_of(other):
        return lax.dynamic_slice_in_dim(padded, (other + 1) * parts, parts)

    return jnp.stack((ids_of(shard), ids_of(shard + 1 - 2 * odd), ids_of(shard - 1 + 2 * odd)))


def columns(array, part, stride, first, width):
    start = pl.multiple_of(part * stride + first, HD)
    return array.at[:, pl.ds(start, width)]


def pack_kernel(stride, jobs, *refs):
    arrays, packed, (stage, in_sems, out_sems) = refs[:4], refs[4:-3], refs[-3:]
    me = lax.axis_index("tensor")
    loads, stores = [], []
    for number, (flip, first, count) in enumerate(jobs):
        for index, array in enumerate(arrays):
            load = pltpu.make_async_copy(
                columns(array, me ^ flip, stride, first * HD, count * HD),
                stage.at[flip, index, :, pl.ds(first * HD, count * HD)],
                in_sems.at[number * 4 + index],
            )
            load.start()
            loads.append(load)
    for number, (flip, first, count) in enumerate(jobs):
        for load in loads[number * 4 : number * 4 + 4]:
            load.wait()
        store = pltpu.make_async_copy(
            stage.at[flip, :, :, pl.ds(first * HD, count * HD)],
            packed[number],
            out_sems.at[number],
        )
        store.start()
        stores.append(store)
    for store in stores:
        store.wait()


def pack(arrays, parts, jobs):
    rows, total = arrays[0].shape
    stride = total // parts
    return pl.pallas_call(
        functools.partial(pack_kernel, stride, jobs),
        out_shape=[
            jax.ShapeDtypeStruct((4, rows, count * HD), jnp.bfloat16) for _, _, count in jobs
        ],
        in_specs=[pl.BlockSpec(memory_space=pl.ANY)] * 4,
        out_specs=[pl.BlockSpec(memory_space=pl.ANY)] * len(jobs),
        scratch_shapes=[
            pltpu.VMEM((parts, 4, rows, stride), jnp.bfloat16),
            pltpu.SemaphoreType.DMA((4 * len(jobs),)),
            pltpu.SemaphoreType.DMA((len(jobs),)),
        ],
        compiler_params=pltpu.CompilerParams(vmem_limit_bytes=VMEM_LIMIT),
        cost_estimate=SMALL_COST,
    )(*arrays)


def join_kernel(pieces, *refs):
    received, (joined, stage, in_sems, out_sems) = refs[:pieces], refs[-4:]
    loads, stores = [], []
    for piece in range(pieces):
        load = pltpu.make_async_copy(received[piece], stage.at[piece], in_sems.at[piece])
        load.start()
        loads.append(load)
    for piece in range(pieces):
        loads[piece].wait()
        store = pltpu.make_async_copy(stage.at[piece], joined.at[piece], out_sems.at[piece])
        store.start()
        stores.append(store)
    for store in stores:
        store.wait()


def join(received, after, cost):
    pieces = len(received)
    shape = (pieces,) + received[0].shape
    return pl.pallas_call(
        functools.partial(join_kernel, pieces),
        out_shape=jax.ShapeDtypeStruct(shape, jnp.bfloat16),
        in_specs=[pl.BlockSpec(memory_space=pl.ANY)] * (pieces + len(after)),
        out_specs=pl.BlockSpec(memory_space=pl.ANY),
        scratch_shapes=[
            pltpu.VMEM(shape, jnp.bfloat16),
            pltpu.SemaphoreType.DMA((pieces,)),
            pltpu.SemaphoreType.DMA((pieces,)),
        ],
        compiler_params=pltpu.CompilerParams(vmem_limit_bytes=VMEM_LIMIT),
        cost_estimate=cost,
    )(*received, *after)


def hold(array, after, cost=SMALL_COST):
    return pl.pallas_call(
        lambda *refs: None,
        out_shape=jax.ShapeDtypeStruct(array.shape, array.dtype),
        in_specs=[pl.BlockSpec(memory_space=pl.ANY)] * (1 + len(after)),
        out_specs=pl.BlockSpec(memory_space=pl.ANY),
        input_output_aliases={0: 0},
        compiler_params=pltpu.CompilerParams(vmem_limit_bytes=VMEM_LIMIT),
        cost_estimate=cost,
    )(array, *after)


def dot_nt(a, b):
    return lax.dot_general(a, b, (((1,), (1,)), ((), ())), preferred_element_type=jnp.float32)


def dot_tn(a, b):
    return lax.dot_general(a, b, (((0,), (0,)), ((), ())), preferred_element_type=jnp.float32)


def dot_nn(a, b):
    return jnp.dot(a, b, preferred_element_type=jnp.float32)


def attend_heads(heads, slot_ids, lane_ids, part_rows, rows):
    size = heads[0][0].shape[0]
    slots = size // part_rows

    def per_slot(array):
        return [array[slot * part_rows : (slot + 1) * part_rows] for slot in range(slots)]

    def over_slots(reduce, combine, arrays):
        total = reduce(arrays[0], axis=0, keepdims=True)
        for array in arrays[1:]:
            total = combine(total, reduce(array, axis=0, keepdims=True))
        return total

    def products(head, start):
        queries, keys, values, grads = heads[head]
        tile = slice(start, start + rows)
        return dot_nt(keys, queries[tile]), dot_nt(values, grads[tile])

    def weigh(scores, grad_probs, start):
        lanes = lane_ids[:, start : start + rows]
        scores = [
            part + jnp.where(lanes == slot_id, 0.0, MASKED)
            for part, slot_id in zip(per_slot(scores), slot_ids)
        ]
        row_max = over_slots(jnp.max, jnp.maximum, scores)
        weights = [jnp.exp2((part - row_max) * EXP2_SCALE) for part in scores]
        inverse = 1.0 / over_slots(jnp.sum, jnp.add, weights)
        probs = [part * inverse for part in weights]
        grad_probs = per_slot(grad_probs)
        inner = over_slots(jnp.sum, jnp.add, [p * g for p, g in zip(probs, grad_probs)])
        low = jnp.concatenate([p.astype(jnp.bfloat16) for p in probs])
        grad_scores = [(p * (g - inner)).astype(jnp.bfloat16) for p, g in zip(probs, grad_probs)]
        return low, jnp.concatenate(grad_scores)

    def finish(head, low, grad_scores, start):
        queries, keys, values, grads = heads[head]
        tile = slice(start, start + rows)
        result = results[head]
        if start == 0:
            result[0] = dot_tn(values, low).astype(jnp.bfloat16).T
            result[1] = (dot_tn(keys, grad_scores) * SCALE).astype(jnp.bfloat16).T
            result[2] = result[3] = 0.0
        result[2] += dot_nn(grad_scores[:rows], queries[tile])
        result[3] += dot_nn(low[:rows], grads[tile])

    results = [[None] * 4 for _ in heads]
    work = [(head, start) for head in range(len(heads)) for start in range(0, size, rows)]
    ahead = products(*work[0])
    for number, (head, start) in enumerate(work):
        scores, grad_probs = ahead
        if number + 1 < len(work):
            ahead = products(*work[number + 1])
        finish(head, *weigh(scores, grad_probs, start), start)
    for result in results:
        result[2] = (result[2] * SCALE).astype(jnp.bfloat16)
        result[3] = result[3].astype(jnp.bfloat16)
    return results


def attend_kernel(parts, part_rows, steps, width, offsets, has_outs, *refs):
    image_ids, mine, sides = refs[0], refs[1:4], (refs[4:7], refs[7:10])
    refs = refs[10 + (4 if has_outs else 0) :]
    outs, (window, lane_ids, slot_of, table, sems) = refs[:4], refs[4:]
    rows = parts * part_rows
    most = 3 * rows
    last = parts - 1
    me = lax.axis_index("tensor")
    step = pl.program_id(0)

    def copy_of(group, flip, number, place, sem):
        kind = 0 if flip == 0 else 2 if flip == last else 1
        buffer = lax.rem(number, 2)
        start = pl.multiple_of(place * part_rows, part_rows)
        column = pl.multiple_of(number * width + offsets[kind] * HD, HD)
        source = group[kind].at[flip - 1] if kind == 1 else group[kind]
        return pltpu.make_async_copy(
            source.at[:, :, pl.ds(column, width)],
            window.at[buffer, :, pl.ds(start, part_rows), :],
            sems.at[buffer, sem],
        )

    def copies(number, act):
        for flip in range(parts):
            act(copy_of(mine, flip, number, me ^ flip, flip))
        for source in range(2 * parts):
            slot = slot_of[source]

            @pl.when(slot >= 0)
            def _():
                group = sides[source // parts]
                act(copy_of(group, source % parts, number, parts + slot, parts + source))

    @pl.when(step == 0)
    def _():
        count = jnp.int32(0)
        for slot in range(2 * parts):
            table[slot] = -2
        for source in range(2 * parts):
            side, flip = 1 + source // parts, source % parts
            other_id = image_ids[side, me ^ flip]
            shared = other_id == image_ids[0, 0]
            for part in range(1, parts):
                shared = shared | (other_id == image_ids[0, part])
            slot_of[source] = jnp.where(shared, count, -1)
            table[count] = jnp.where(shared, other_id, -2)
            count = count + shared.astype(jnp.int32)
        table[2 * parts] = count
        window[:, :, rows:] = jnp.zeros((2, 4, most - rows, width), window.dtype)
        copies(0, lambda copy: copy.start())
        place = lax.broadcasted_iota(jnp.int32, (8, most), 1)
        ids = jnp.full((8, most), -2, jnp.int32)
        for slot in range(3 * parts):
            slot_id = image_ids[0, slot] if slot < parts else table[slot - parts]
            inside = (place >= slot * part_rows) & (place < (slot + 1) * part_rows)
            ids = jnp.where(inside, slot_id, ids)
        lane_ids[...] = ids

    @pl.when(step + 1 < steps)
    def _():
        copies(step + 1, lambda copy: copy.start())

    copies(step, lambda copy: copy.wait())
    count = table[2 * parts]
    buffer = lax.rem(step, 2)
    for size in range(rows, most + 1, rows):
        slots = (size - rows) // part_rows

        @pl.when((count <= slots) & (count > slots - parts))
        def _():
            slot_ids = [image_ids[0, slot] for slot in range(parts)]
            slot_ids += [table[slot] for slot in range(slots)]
            spans = [slice(start, start + HD) for start in range(0, width, HD)]
            heads = [[window[buffer, i, :size, span] for i in range(4)] for span in spans]
            results = attend_heads(heads, slot_ids, lane_ids[0:1], part_rows, rows)
            for span, result in zip(spans, results):
                for out, part in zip(outs, result):
                    out[:, span] = part


def attend(image_ids, groups, offsets, outs, first_head, heads):
    _, part_rows, total = groups[0][0].shape
    parts = groups[0][1].shape[0] + 2
    rows = parts * part_rows
    width = HD * math.gcd(2, math.gcd(first_head, heads))
    steps = heads * HD // width
    first_block = first_head * HD // width
    out_spec = pl.BlockSpec((rows, width), lambda s: (0, s + first_block))
    has_outs = outs is not None
    pieces = [piece for group in groups for piece in group]
    aliases = {1 + len(pieces) + i: i for i in range(4)} if has_outs else {}
    return pl.pallas_call(
        functools.partial(
            attend_kernel, parts, part_rows, steps, width, offsets, has_outs
        ),
        grid=(steps,),
        out_shape=[jax.ShapeDtypeStruct((rows, total), jnp.bfloat16)] * 4,
        in_specs=[pl.BlockSpec(memory_space=pltpu.SMEM)]
        + [pl.BlockSpec(memory_space=pl.ANY)] * (len(pieces) + (4 if has_outs else 0)),
        out_specs=[out_spec] * 4,
        scratch_shapes=[
            pltpu.VMEM((2, 4, 3 * rows, width), jnp.bfloat16),
            pltpu.VMEM((8, 3 * rows), jnp.int32),
            pltpu.SMEM((2 * parts,), jnp.int32),
            pltpu.SMEM((2 * parts + 1,), jnp.int32),
            pltpu.SemaphoreType.DMA((2, 3 * parts)),
        ],
        input_output_aliases=aliases,
        compiler_params=pltpu.CompilerParams(
            dimension_semantics=("arbitrary",), vmem_limit_bytes=VMEM_LIMIT
        ),
        cost_estimate=pl.CostEstimate(
            flops=heads * ATTEND_FLOPS, bytes_accessed=1, transcendentals=0
        ),
    )(image_ids, *pieces, *(outs or ()))


def between(sent, received):
    size = 2 * sent.size - received.size
    return pl.CostEstimate(flops=FLOPS_PER_BYTE * size, bytes_accessed=1, transcendentals=0)


def shards(queries, key_vectors, value_vectors, grad_output, image_ids):
    arrays = (queries, key_vectors, value_vectors, grad_output)
    parts = lax.axis_size("tensor")
    part_rows = queries.shape[0]
    head_total = queries.shape[1] // HD // parts
    near_ids = nearby_ids(image_ids, parts, part_rows)
    last = parts - 1
    spans = split_counts(head_total, [sum(shares) for shares in GROUPS])
    groups = []
    for (start, count), shares in zip(spans, GROUPS):
        groups.append([(start + first, size) for first, size in split_counts(count, shares)])

    jobs = []
    for span, chunks in zip(spans, groups):
        jobs += [(flip, *span) for flip in range(last - 1, 0, -1)]
        jobs += [(last, *chunk) for chunk in chunks]
    jobs.insert(last - 1, (0, 0, head_total))
    packed = dict(zip(jobs, pack(arrays, parts, jobs)))

    steps = []
    for span, chunks in zip(spans, groups):
        steps.append([(flip, *span) for flip in range(1, last)])
        steps += [[(last, *chunk)] for chunk in chunks]

    def cross(step, after):
        held = [hold(packed[job], after) if after else packed[job] for job in step]
        return held, [swap_flipped(piece, "tensor", job[0]) for job, piece in zip(step, held)]

    def spread(piece):
        return piece, swap_pairs(piece, "dp", 0), swap_pairs(piece, "dp", 1)

    _, crossed = cross(steps[0], [])
    sent = [spread(packed[(0, 0, head_total)])]
    outs, joined, number = None, None, 0
    for span, chunks in zip(spans, groups):
        for place in range(1 + len(chunks)):
            after = list(sent[-1][1:])
            received, held = crossed, []
            number += 1
            if number < len(steps):
                held, crossed = cross(steps[number], [received[-1]])
            elif outs is not None:
                after.append(outs[0])
            cost = between(sent[-1][0], received[0])
            if place == 0:
                joined = spread(hold(join(received, held, cost), after))
                sent.append(joined)
                continue
            piece = spread(hold(hold(received[0], held, cost), after))
            sent.append(piece)
            first_head, count = chunks[place - 1]
            offsets = (first_head, first_head - span[0], 0)
            outs = attend(
                near_ids, list(zip(sent[0], joined, piece)), offsets, outs, first_head, count
            )
    return tuple(outs)


def solution(mesh):
    return jax.shard_map(
        shards,
        mesh=mesh,
        in_specs=(
            P(("dp", "tensor"), None),
            P(("dp", "tensor"), None),
            P(("dp", "tensor"), None),
            P(("dp", "tensor"), None),
            P(),
        ),
        out_specs=(P("dp", "tensor"), P("dp", "tensor"), P("dp", "tensor"), P("dp", "tensor")),
        check_vma=False,
    )
```

```python
import functools
import math

import jax
import jax.numpy as jnp
from jax import lax
from jax.experimental import pallas as pl
from jax.experimental.pallas import tpu as pltpu
from jax.sharding import PartitionSpec as P

HD = 128
SCALE = 1.0 / math.sqrt(HD)
EXP2_SCALE = SCALE * math.log2(math.e)
MASKED = -1e30
GROUPS = ((8,), (4,))
VMEM_LIMIT = 64 * 1024 * 1024 - 256 * 1024
ATTEND_FLOPS = 1_500_000_000
FLOPS_PER_BYTE = 62_500
SMALL_COST = pl.CostEstimate(flops=1, bytes_accessed=1, transcendentals=0)


def split_counts(total, shares):
    whole = sum(shares)
    edges = [round(total * sum(shares[:i]) / whole) for i in range(len(shares) + 1)]
    return [(a, b - a) for a, b in zip(edges[:-1], edges[1:]) if b > a]


def swap_pairs(block, axis, first):
    count = lax.axis_size(axis)
    route = []
    for low in range(first, count - 1, 2):
        route += [(low, low + 1), (low + 1, low)]
    return lax.ppermute(block, axis, route)


def swap_flipped(block, axis, flip):
    return lax.ppermute(block, axis, [(i, i ^ flip) for i in range(lax.axis_size(axis))])


def nearby_ids(image_ids, parts, part_rows):
    shard = lax.axis_index("dp")
    padded = jnp.pad(image_ids[::part_rows], (parts, parts), constant_values=-1)
    odd = lax.rem(shard, 2)

    def ids_of(other):
        return lax.dynamic_slice_in_dim(padded, (other + 1) * parts, parts)

    return jnp.stack((ids_of(shard), ids_of(shard + 1 - 2 * odd), ids_of(shard - 1 + 2 * odd)))


def columns(array, part, stride, first, width):
    start = pl.multiple_of(part * stride + first, HD)
    return array.at[:, pl.ds(start, width)]


def pack_kernel(stride, jobs, *refs):
    arrays, packed, (stage, in_sems, out_sems) = refs[:4], refs[4:-3], refs[-3:]
    me = lax.axis_index("tensor")
    loads, stores = [], []
    for number, (flip, first, count) in enumerate(jobs):
        for index, array in enumerate(arrays):
            load = pltpu.make_async_copy(
                columns(array, me ^ flip, stride, first * HD, count * HD),
                stage.at[flip, index, :, pl.ds(first * HD, count * HD)],
                in_sems.at[number * 4 + index],
            )
            load.start()
            loads.append(load)
    for number, (flip, first, count) in enumerate(jobs):
        for load in loads[number * 4 : number * 4 + 4]:
            load.wait()
        store = pltpu.make_async_copy(
            stage.at[flip, :, :, pl.ds(first * HD, count * HD)],
            packed[number],
            out_sems.at[number],
        )
        store.start()
        stores.append(store)
    for store in stores:
        store.wait()


def pack(arrays, parts, jobs):
    rows, total = arrays[0].shape
    stride = total // parts
    return pl.pallas_call(
        functools.partial(pack_kernel, stride, jobs),
        out_shape=[
            jax.ShapeDtypeStruct((4, rows, count * HD), jnp.bfloat16) for _, _, count in jobs
        ],
        in_specs=[pl.BlockSpec(memory_space=pl.ANY)] * 4,
        out_specs=[pl.BlockSpec(memory_space=pl.ANY)] * len(jobs),
        scratch_shapes=[
            pltpu.VMEM((parts, 4, rows, stride), jnp.bfloat16),
            pltpu.SemaphoreType.DMA((4 * len(jobs),)),
            pltpu.SemaphoreType.DMA((len(jobs),)),
        ],
        compiler_params=pltpu.CompilerParams(vmem_limit_bytes=VMEM_LIMIT),
        cost_estimate=SMALL_COST,
    )(*arrays)


def join_kernel(pieces, *refs):
    received, (joined, stage, in_sems, out_sems) = refs[:pieces], refs[-4:]
    loads, stores = [], []
    for piece in range(pieces):
        load = pltpu.make_async_copy(received[piece], stage.at[piece], in_sems.at[piece])
        load.start()
        loads.append(load)
    for piece in range(pieces):
        loads[piece].wait()
        store = pltpu.make_async_copy(stage.at[piece], joined.at[piece], out_sems.at[piece])
        store.start()
        stores.append(store)
    for store in stores:
        store.wait()


def join(received, after, cost):
    pieces = len(received)
    shape = (pieces,) + received[0].shape
    return pl.pallas_call(
        functools.partial(join_kernel, pieces),
        out_shape=jax.ShapeDtypeStruct(shape, jnp.bfloat16),
        in_specs=[pl.BlockSpec(memory_space=pl.ANY)] * (pieces + len(after)),
        out_specs=pl.BlockSpec(memory_space=pl.ANY),
        scratch_shapes=[
            pltpu.VMEM(shape, jnp.bfloat16),
            pltpu.SemaphoreType.DMA((pieces,)),
            pltpu.SemaphoreType.DMA((pieces,)),
        ],
        compiler_params=pltpu.CompilerParams(vmem_limit_bytes=VMEM_LIMIT),
        cost_estimate=cost,
    )(*received, *after)


def hold(array, after, cost=SMALL_COST):
    return pl.pallas_call(
        lambda *refs: None,
        out_shape=jax.ShapeDtypeStruct(array.shape, array.dtype),
        in_specs=[pl.BlockSpec(memory_space=pl.ANY)] * (1 + len(after)),
        out_specs=pl.BlockSpec(memory_space=pl.ANY),
        input_output_aliases={0: 0},
        compiler_params=pltpu.CompilerParams(vmem_limit_bytes=VMEM_LIMIT),
        cost_estimate=cost,
    )(array, *after)


def dot_nt(a, b):
    return lax.dot_general(a, b, (((1,), (1,)), ((), ())), preferred_element_type=jnp.float32)


def dot_tn(a, b):
    return lax.dot_general(a, b, (((0,), (0,)), ((), ())), preferred_element_type=jnp.float32)


def dot_nn(a, b):
    return jnp.dot(a, b, preferred_element_type=jnp.float32)


def attend_heads(heads, slot_ids, lane_ids, part_rows, rows):
    size = heads[0][0].shape[0]
    slots = size // part_rows

    def per_slot(array):
        return [array[slot * part_rows : (slot + 1) * part_rows] for slot in range(slots)]

    def over_slots(reduce, combine, arrays):
        total = reduce(arrays[0], axis=0, keepdims=True)
        for array in arrays[1:]:
            total = combine(total, reduce(array, axis=0, keepdims=True))
        return total

    def products(head, start):
        queries, keys, values, grads = heads[head]
        tile = slice(start, start + rows)
        return dot_nt(keys, queries[tile]), dot_nt(values, grads[tile])

    def weigh(scores, grad_probs, start):
        lanes = lane_ids[:, start : start + rows]
        scores = [
            part + jnp.where(lanes == slot_id, 0.0, MASKED)
            for part, slot_id in zip(per_slot(scores), slot_ids)
        ]
        row_max = over_slots(jnp.max, jnp.maximum, scores)
        weights = [jnp.exp2((part - row_max) * EXP2_SCALE) for part in scores]
        inverse = 1.0 / over_slots(jnp.sum, jnp.add, weights)
        probs = [part * inverse for part in weights]
        grad_probs = per_slot(grad_probs)
        inner = over_slots(jnp.sum, jnp.add, [p * g for p, g in zip(probs, grad_probs)])
        low = jnp.concatenate([p.astype(jnp.bfloat16) for p in probs])
        grad_scores = [(p * (g - inner)).astype(jnp.bfloat16) for p, g in zip(probs, grad_probs)]
        return low, jnp.concatenate(grad_scores)

    def finish(head, low, grad_scores, start):
        queries, keys, values, grads = heads[head]
        tile = slice(start, start + rows)
        result = results[head]
        if start == 0:
            result[0] = dot_tn(values, low).astype(jnp.bfloat16).T
            result[1] = (dot_tn(keys, grad_scores) * SCALE).astype(jnp.bfloat16).T
            result[2] = result[3] = 0.0
        result[2] += dot_nn(grad_scores[:rows], queries[tile])
        result[3] += dot_nn(low[:rows], grads[tile])

    results = [[None] * 4 for _ in heads]
    work = [(head, start) for head in range(len(heads)) for start in range(0, size, rows)]
    ahead = products(*work[0])
    for number, (head, start) in enumerate(work):
        scores, grad_probs = ahead
        if number + 1 < len(work):
            ahead = products(*work[number + 1])
        finish(head, *weigh(scores, grad_probs, start), start)
    for result in results:
        result[2] = (result[2] * SCALE).astype(jnp.bfloat16)
        result[3] = result[3].astype(jnp.bfloat16)
    return results


def attend_kernel(parts, part_rows, steps, width, offsets, has_outs, *refs):
    image_ids, mine, sides = refs[0], refs[1:4], (refs[4:7], refs[7:10])
    refs = refs[10 + (4 if has_outs else 0) :]
    outs, (window, lane_ids, slot_of, table, sems) = refs[:4], refs[4:]
    rows = parts * part_rows
    most = 3 * rows
    last = parts - 1
    me = lax.axis_index("tensor")
    step = pl.program_id(0)

    def copy_of(group, flip, number, place, sem):
        kind = 0 if flip == 0 else 2 if flip == last else 1
        buffer = lax.rem(number, 2)
        start = pl.multiple_of(place * part_rows, part_rows)
        column = pl.multiple_of(number * width + offsets[kind] * HD, HD)
        source = group[kind].at[flip - 1] if kind == 1 else group[kind]
        return pltpu.make_async_copy(
            source.at[:, :, pl.ds(column, width)],
            window.at[buffer, :, pl.ds(start, part_rows), :],
            sems.at[buffer, sem],
        )

    def copies(number, act):
        for flip in range(parts):
            act(copy_of(mine, flip, number, me ^ flip, flip))
        for source in range(2 * parts):
            slot = slot_of[source]

            @pl.when(slot >= 0)
            def _():
                group = sides[source // parts]
                act(copy_of(group, source % parts, number, parts + slot, parts + source))

    @pl.when(step == 0)
    def _():
        count = jnp.int32(0)
        for slot in range(2 * parts):
            table[slot] = -2
        for source in range(2 * parts):
            side, flip = 1 + source // parts, source % parts
            other_id = image_ids[side, me ^ flip]
            shared = other_id == image_ids[0, 0]
            for part in range(1, parts):
                shared = shared | (other_id == image_ids[0, part])
            slot_of[source] = jnp.where(shared, count, -1)
            table[count] = jnp.where(shared, other_id, -2)
            count = count + shared.astype(jnp.int32)
        table[2 * parts] = count
        window[:, :, rows:] = jnp.zeros((2, 4, most - rows, width), window.dtype)
        copies(0, lambda copy: copy.start())
        place = lax.broadcasted_iota(jnp.int32, (8, most), 1)
        ids = jnp.full((8, most), -2, jnp.int32)
        for slot in range(3 * parts):
            slot_id = image_ids[0, slot] if slot < parts else table[slot - parts]
            inside = (place >= slot * part_rows) & (place < (slot + 1) * part_rows)
            ids = jnp.where(inside, slot_id, ids)
        lane_ids[...] = ids

    @pl.when(step + 1 < steps)
    def _():
        copies(step + 1, lambda copy: copy.start())

    copies(step, lambda copy: copy.wait())
    count = table[2 * parts]
    buffer = lax.rem(step, 2)
    for size in range(rows, most + 1, rows):
        slots = (size - rows) // part_rows

        @pl.when((count <= slots) & (count > slots - parts))
        def _():
            slot_ids = [image_ids[0, slot] for slot in range(parts)]
            slot_ids += [table[slot] for slot in range(slots)]
            spans = [slice(start, start + HD) for start in range(0, width, HD)]
            heads = [[window[buffer, i, :size, span] for i in range(4)] for span in spans]
            results = attend_heads(heads, slot_ids, lane_ids[0:1], part_rows, rows)
            for span, result in zip(spans, results):
                for out, part in zip(outs, result):
                    out[:, span] = part


def attend(image_ids, groups, offsets, outs, first_head, heads):
    _, part_rows, total = groups[0][0].shape
    parts = groups[0][1].shape[0] + 2
    rows = parts * part_rows
    width = HD * math.gcd(2, math.gcd(first_head, heads))
    steps = heads * HD // width
    first_block = first_head * HD // width
    out_spec = pl.BlockSpec((rows, width), lambda s: (0, s + first_block))
    has_outs = outs is not None
    pieces = [piece for group in groups for piece in group]
    aliases = {1 + len(pieces) + i: i for i in range(4)} if has_outs else {}
    return pl.pallas_call(
        functools.partial(
            attend_kernel, parts, part_rows, steps, width, offsets, has_outs
        ),
        grid=(steps,),
        out_shape=[jax.ShapeDtypeStruct((rows, total), jnp.bfloat16)] * 4,
        in_specs=[pl.BlockSpec(memory_space=pltpu.SMEM)]
        + [pl.BlockSpec(memory_space=pl.ANY)] * (len(pieces) + (4 if has_outs else 0)),
        out_specs=[out_spec] * 4,
        scratch_shapes=[
            pltpu.VMEM((2, 4, 3 * rows, width), jnp.bfloat16),
            pltpu.VMEM((8, 3 * rows), jnp.int32),
            pltpu.SMEM((2 * parts,), jnp.int32),
            pltpu.SMEM((2 * parts + 1,), jnp.int32),
            pltpu.SemaphoreType.DMA((2, 3 * parts)),
        ],
        input_output_aliases=aliases,
        compiler_params=pltpu.CompilerParams(
            dimension_semantics=("arbitrary",), vmem_limit_bytes=VMEM_LIMIT
        ),
        cost_estimate=pl.CostEstimate(
            flops=heads * ATTEND_FLOPS, bytes_accessed=1, transcendentals=0
        ),
    )(image_ids, *pieces, *(outs or ()))


def between(sent, received):
    size = 2 * sent.size - received.size
    return pl.CostEstimate(flops=FLOPS_PER_BYTE * size, bytes_accessed=1, transcendentals=0)


def shards(queries, key_vectors, value_vectors, grad_output, image_ids):
    arrays = (queries, key_vectors, value_vectors, grad_output)
    parts = lax.axis_size("tensor")
    part_rows = queries.shape[0]
    head_total = queries.shape[1] // HD // parts
    near_ids = nearby_ids(image_ids, parts, part_rows)
    last = parts - 1
    spans = split_counts(head_total, [sum(shares) for shares in GROUPS])
    groups = []
    for (start, count), shares in zip(spans, GROUPS):
        groups.append([(start + first, size) for first, size in split_counts(count, shares)])

    jobs = []
    for span, chunks in zip(spans, groups):
        jobs += [(flip, *span) for flip in range(last - 1, 0, -1)]
        jobs += [(last, *chunk) for chunk in chunks]
    jobs.insert(last - 1, (0, 0, head_total))
    packed = dict(zip(jobs, pack(arrays, parts, jobs)))

    steps = []
    for span, chunks in zip(spans, groups):
        steps.append([(flip, *span) for flip in range(1, last)])
        steps += [[(last, *chunk)] for chunk in chunks]

    def cross(step, after):
        held = [hold(packed[job], after) if after else packed[job] for job in step]
        return held, [swap_flipped(piece, "tensor", job[0]) for job, piece in zip(step, held)]

    def spread(piece):
        return piece, swap_pairs(piece, "dp", 0), swap_pairs(piece, "dp", 1)

    _, crossed = cross(steps[0], [])
    sent = [spread(packed[(0, 0, head_total)])]
    outs, joined, number = None, None, 0
    for span, chunks in zip(spans, groups):
        for place in range(1 + len(chunks)):
            after = list(sent[-1][1:])
            received, held = crossed, []
            number += 1
            if number < len(steps):
                held, crossed = cross(steps[number], [received[-1]])
            elif outs is not None:
                after.append(outs[0])
            cost = between(sent[-1][0], received[0])
            held.append(sent[-1][0])
            if place == 0:
                joined = spread(hold(join(received, held, cost), after))
                sent.append(joined)
                continue
            piece = spread(hold(hold(received[0], held, cost), after))
            sent.append(piece)
            first_head, count = chunks[place - 1]
            offsets = (first_head, first_head - span[0], 0)
            outs = attend(
                near_ids, list(zip(sent[0], joined, piece)), offsets, outs, first_head, count
            )
    return tuple(outs)


def solution(mesh):
    return jax.shard_map(
        shards,
        mesh=mesh,
        in_specs=(
            P(("dp", "tensor"), None),
            P(("dp", "tensor"), None),
            P(("dp", "tensor"), None),
            P(("dp", "tensor"), None),
            P(),
        ),
        out_specs=(P("dp", "tensor"), P("dp", "tensor"), P("dp", "tensor"), P("dp", "tensor")),
        check_vma=False,
    )
```

```python
import functools
import math

import jax
import jax.numpy as jnp
from jax import lax
from jax.experimental import pallas as pl
from jax.experimental.pallas import tpu as pltpu
from jax.sharding import PartitionSpec as P

HD = 128
SCALE = 1.0 / math.sqrt(HD)
EXP2_SCALE = SCALE * math.log2(math.e)
MASKED = -1e30
GROUPS = ((8,), (4,))
VMEM_LIMIT = 64 * 1024 * 1024 - 256 * 1024
ATTEND_FLOPS = 1_500_000_000
FLOPS_PER_BYTE = 62_500
SMALL_COST = pl.CostEstimate(flops=1, bytes_accessed=1, transcendentals=0)


def split_counts(total, shares):
    whole = sum(shares)
    edges = [round(total * sum(shares[:i]) / whole) for i in range(len(shares) + 1)]
    return [(a, b - a) for a, b in zip(edges[:-1], edges[1:]) if b > a]


def swap_pairs(block, axis, first):
    count = lax.axis_size(axis)
    route = []
    for low in range(first, count - 1, 2):
        route += [(low, low + 1), (low + 1, low)]
    return lax.ppermute(block, axis, route)


def swap_flipped(block, axis, flip):
    return lax.ppermute(block, axis, [(i, i ^ flip) for i in range(lax.axis_size(axis))])


def nearby_ids(image_ids, parts, part_rows):
    shard = lax.axis_index("dp")
    padded = jnp.pad(image_ids[::part_rows], (parts, parts), constant_values=-1)
    odd = lax.rem(shard, 2)

    def ids_of(other):
        return lax.dynamic_slice_in_dim(padded, (other + 1) * parts, parts)

    return jnp.stack((ids_of(shard), ids_of(shard + 1 - 2 * odd), ids_of(shard - 1 + 2 * odd)))


def columns(array, part, stride, first, width):
    start = pl.multiple_of(part * stride + first, HD)
    return array.at[:, pl.ds(start, width)]


def pack_kernel(stride, jobs, *refs):
    arrays, packed, (stage, in_sems, out_sems) = refs[:4], refs[4:-3], refs[-3:]
    me = lax.axis_index("tensor")
    loads, stores = [], []
    for number, (flip, first, count) in enumerate(jobs):
        for index, array in enumerate(arrays):
            load = pltpu.make_async_copy(
                columns(array, me ^ flip, stride, first * HD, count * HD),
                stage.at[flip, index, :, pl.ds(first * HD, count * HD)],
                in_sems.at[number * 4 + index],
            )
            load.start()
            loads.append(load)
    for number, (flip, first, count) in enumerate(jobs):
        for load in loads[number * 4 : number * 4 + 4]:
            load.wait()
        store = pltpu.make_async_copy(
            stage.at[flip, :, :, pl.ds(first * HD, count * HD)],
            packed[number],
            out_sems.at[number],
        )
        store.start()
        stores.append(store)
    for store in stores:
        store.wait()


def pack(arrays, parts, jobs):
    rows, total = arrays[0].shape
    stride = total // parts
    return pl.pallas_call(
        functools.partial(pack_kernel, stride, jobs),
        out_shape=[
            jax.ShapeDtypeStruct((4, rows, count * HD), jnp.bfloat16) for _, _, count in jobs
        ],
        in_specs=[pl.BlockSpec(memory_space=pl.ANY)] * 4,
        out_specs=[pl.BlockSpec(memory_space=pl.ANY)] * len(jobs),
        scratch_shapes=[
            pltpu.VMEM((parts, 4, rows, stride), jnp.bfloat16),
            pltpu.SemaphoreType.DMA((4 * len(jobs),)),
            pltpu.SemaphoreType.DMA((len(jobs),)),
        ],
        compiler_params=pltpu.CompilerParams(vmem_limit_bytes=VMEM_LIMIT),
        cost_estimate=SMALL_COST,
    )(*arrays)


def join_kernel(pieces, *refs):
    received, (joined, stage, in_sems, out_sems) = refs[:pieces], refs[-4:]
    loads, stores = [], []
    for piece in range(pieces):
        load = pltpu.make_async_copy(received[piece], stage.at[piece], in_sems.at[piece])
        load.start()
        loads.append(load)
    for piece in range(pieces):
        loads[piece].wait()
        store = pltpu.make_async_copy(stage.at[piece], joined.at[piece], out_sems.at[piece])
        store.start()
        stores.append(store)
    for store in stores:
        store.wait()


def join(received, after, cost):
    pieces = len(received)
    shape = (pieces,) + received[0].shape
    return pl.pallas_call(
        functools.partial(join_kernel, pieces),
        out_shape=jax.ShapeDtypeStruct(shape, jnp.bfloat16),
        in_specs=[pl.BlockSpec(memory_space=pl.ANY)] * (pieces + len(after)),
        out_specs=pl.BlockSpec(memory_space=pl.ANY),
        scratch_shapes=[
            pltpu.VMEM(shape, jnp.bfloat16),
            pltpu.SemaphoreType.DMA((pieces,)),
            pltpu.SemaphoreType.DMA((pieces,)),
        ],
        compiler_params=pltpu.CompilerParams(vmem_limit_bytes=VMEM_LIMIT),
        cost_estimate=cost,
    )(*received, *after)


def hold(array, after, cost=SMALL_COST):
    return pl.pallas_call(
        lambda *refs: None,
        out_shape=jax.ShapeDtypeStruct(array.shape, array.dtype),
        in_specs=[pl.BlockSpec(memory_space=pl.ANY)] * (1 + len(after)),
        out_specs=pl.BlockSpec(memory_space=pl.ANY),
        input_output_aliases={0: 0},
        compiler_params=pltpu.CompilerParams(vmem_limit_bytes=VMEM_LIMIT),
        cost_estimate=cost,
    )(array, *after)


def dot_nt(a, b):
    return lax.dot_general(a, b, (((1,), (1,)), ((), ())), preferred_element_type=jnp.float32)


def dot_tn(a, b):
    return lax.dot_general(a, b, (((0,), (0,)), ((), ())), preferred_element_type=jnp.float32)


def dot_nn(a, b):
    return jnp.dot(a, b, preferred_element_type=jnp.float32)


def attend_heads(heads, slot_ids, lane_ids, part_rows, rows):
    size = heads[0][0].shape[0]
    slots = size // part_rows

    def per_slot(array):
        return [array[slot * part_rows : (slot + 1) * part_rows] for slot in range(slots)]

    def over_slots(reduce, combine, arrays):
        total = reduce(arrays[0], axis=0, keepdims=True)
        for array in arrays[1:]:
            total = combine(total, reduce(array, axis=0, keepdims=True))
        return total

    def products(head, start):
        queries, keys, values, grads = heads[head]
        tile = slice(start, start + rows)
        return dot_nt(keys, queries[tile]), dot_nt(values, grads[tile])

    def weigh(scores, grad_probs, start):
        lanes = lane_ids[:, start : start + rows]
        scores = [
            part + jnp.where(lanes == slot_id, 0.0, MASKED)
            for part, slot_id in zip(per_slot(scores), slot_ids)
        ]
        row_max = over_slots(jnp.max, jnp.maximum, scores)
        weights = [jnp.exp2((part - row_max) * EXP2_SCALE) for part in scores]
        inverse = 1.0 / over_slots(jnp.sum, jnp.add, weights)
        probs = [part * inverse for part in weights]
        grad_probs = per_slot(grad_probs)
        inner = over_slots(jnp.sum, jnp.add, [p * g for p, g in zip(probs, grad_probs)])
        low = jnp.concatenate([p.astype(jnp.bfloat16) for p in probs])
        grad_scores = [(p * (g - inner)).astype(jnp.bfloat16) for p, g in zip(probs, grad_probs)]
        return low, jnp.concatenate(grad_scores)

    def finish(head, low, grad_scores, start):
        queries, keys, values, grads = heads[head]
        tile = slice(start, start + rows)
        result = results[head]
        if start == 0:
            result[0] = dot_tn(values, low).astype(jnp.bfloat16).T
            result[1] = (dot_tn(keys, grad_scores) * SCALE).astype(jnp.bfloat16).T
            result[2] = result[3] = 0.0
        result[2] += dot_nn(grad_scores[:rows], queries[tile])
        result[3] += dot_nn(low[:rows], grads[tile])

    results = [[None] * 4 for _ in heads]
    work = [(head, start) for head in range(len(heads)) for start in range(0, size, rows)]
    ahead = products(*work[0])
    for number, (head, start) in enumerate(work):
        scores, grad_probs = ahead
        if number + 1 < len(work):
            ahead = products(*work[number + 1])
        finish(head, *weigh(scores, grad_probs, start), start)
    for result in results:
        result[2] = (result[2] * SCALE).astype(jnp.bfloat16)
        result[3] = result[3].astype(jnp.bfloat16)
    return results


def attend_kernel(parts, part_rows, steps, width, offsets, has_outs, *refs):
    image_ids, mine, sides = refs[0], refs[1:4], (refs[4:7], refs[7:10])
    refs = refs[10 + (4 if has_outs else 0) :]
    outs, (window, lane_ids, slot_of, table, sems) = refs[:4], refs[4:]
    rows = parts * part_rows
    most = 3 * rows
    last = parts - 1
    me = lax.axis_index("tensor")
    step = pl.program_id(0)

    def copy_of(group, flip, number, place, sem):
        kind = 0 if flip == 0 else 2 if flip == last else 1
        buffer = lax.rem(number, 2)
        start = pl.multiple_of(place * part_rows, part_rows)
        column = pl.multiple_of(number * width + offsets[kind] * HD, HD)
        source = group[kind].at[flip - 1] if kind == 1 else group[kind]
        return pltpu.make_async_copy(
            source.at[:, :, pl.ds(column, width)],
            window.at[buffer, :, pl.ds(start, part_rows), :],
            sems.at[buffer, sem],
        )

    def copies(number, act):
        for flip in range(parts):
            act(copy_of(mine, flip, number, me ^ flip, flip))
        for source in range(2 * parts):
            slot = slot_of[source]

            @pl.when(slot >= 0)
            def _():
                group = sides[source // parts]
                act(copy_of(group, source % parts, number, parts + slot, parts + source))

    @pl.when(step == 0)
    def _():
        count = jnp.int32(0)
        for slot in range(2 * parts):
            table[slot] = -2
        for source in range(2 * parts):
            side, flip = 1 + source // parts, source % parts
            other_id = image_ids[side, me ^ flip]
            shared = other_id == image_ids[0, 0]
            for part in range(1, parts):
                shared = shared | (other_id == image_ids[0, part])
            slot_of[source] = jnp.where(shared, count, -1)
            table[count] = jnp.where(shared, other_id, -2)
            count = count + shared.astype(jnp.int32)
        table[2 * parts] = count
        window[:, :, rows:] = jnp.zeros((2, 4, most - rows, width), window.dtype)
        copies(0, lambda copy: copy.start())
        place = lax.broadcasted_iota(jnp.int32, (8, most), 1)
        ids = jnp.full((8, most), -2, jnp.int32)
        for slot in range(3 * parts):
            slot_id = image_ids[0, slot] if slot < parts else table[slot - parts]
            inside = (place >= slot * part_rows) & (place < (slot + 1) * part_rows)
            ids = jnp.where(inside, slot_id, ids)
        lane_ids[...] = ids

    @pl.when(step + 1 < steps)
    def _():
        copies(step + 1, lambda copy: copy.start())

    copies(step, lambda copy: copy.wait())
    count = table[2 * parts]
    buffer = lax.rem(step, 2)
    for size in range(rows, most + 1, rows):
        slots = (size - rows) // part_rows

        @pl.when((count <= slots) & (count > slots - parts))
        def _():
            slot_ids = [image_ids[0, slot] for slot in range(parts)]
            slot_ids += [table[slot] for slot in range(slots)]
            spans = [slice(start, start + HD) for start in range(0, width, HD)]
            heads = [[window[buffer, i, :size, span] for i in range(4)] for span in spans]
            results = attend_heads(heads, slot_ids, lane_ids[0:1], part_rows, rows)
            for span, result in zip(spans, results):
                for out, part in zip(outs, result):
                    out[:, span] = part


def attend(image_ids, groups, offsets, outs, first_head, heads):
    _, part_rows, total = groups[0][0].shape
    parts = groups[0][1].shape[0] + 2
    rows = parts * part_rows
    width = HD * math.gcd(2, math.gcd(first_head, heads))
    steps = heads * HD // width
    first_block = first_head * HD // width
    out_spec = pl.BlockSpec((rows, width), lambda s: (0, s + first_block))
    has_outs = outs is not None
    pieces = [piece for group in groups for piece in group]
    aliases = {1 + len(pieces) + i: i for i in range(4)} if has_outs else {}
    return pl.pallas_call(
        functools.partial(
            attend_kernel, parts, part_rows, steps, width, offsets, has_outs
        ),
        grid=(steps,),
        out_shape=[jax.ShapeDtypeStruct((rows, total), jnp.bfloat16)] * 4,
        in_specs=[pl.BlockSpec(memory_space=pltpu.SMEM)]
        + [pl.BlockSpec(memory_space=pl.ANY)] * (len(pieces) + (4 if has_outs else 0)),
        out_specs=[out_spec] * 4,
        scratch_shapes=[
            pltpu.VMEM((2, 4, 3 * rows, width), jnp.bfloat16),
            pltpu.VMEM((8, 3 * rows), jnp.int32),
            pltpu.SMEM((2 * parts,), jnp.int32),
            pltpu.SMEM((2 * parts + 1,), jnp.int32),
            pltpu.SemaphoreType.DMA((2, 3 * parts)),
        ],
        input_output_aliases=aliases,
        compiler_params=pltpu.CompilerParams(
            dimension_semantics=("arbitrary",), vmem_limit_bytes=VMEM_LIMIT
        ),
        cost_estimate=pl.CostEstimate(
            flops=heads * ATTEND_FLOPS, bytes_accessed=1, transcendentals=0
        ),
    )(image_ids, *pieces, *(outs or ()))


def between(sent, received, divisor):
    flops = FLOPS_PER_BYTE * (2 * sent.size - received.size) // divisor
    return pl.CostEstimate(flops=flops, bytes_accessed=1, transcendentals=0)


def shards(queries, key_vectors, value_vectors, grad_output, image_ids):
    arrays = (queries, key_vectors, value_vectors, grad_output)
    parts = lax.axis_size("tensor")
    part_rows = queries.shape[0]
    head_total = queries.shape[1] // HD // parts
    near_ids = nearby_ids(image_ids, parts, part_rows)
    last = parts - 1
    spans = split_counts(head_total, [sum(shares) for shares in GROUPS])
    groups = []
    for (start, count), shares in zip(spans, GROUPS):
        groups.append([(start + first, size) for first, size in split_counts(count, shares)])

    jobs = []
    for span, chunks in zip(spans, groups):
        jobs += [(flip, *span) for flip in range(last - 1, 0, -1)]
        jobs += [(last, *chunk) for chunk in chunks]
    jobs.insert(last - 1, (0, 0, head_total))
    packed = dict(zip(jobs, pack(arrays, parts, jobs)))

    steps = []
    for span, chunks in zip(spans, groups):
        steps.append([(flip, *span) for flip in range(1, last)])
        steps += [[(last, *chunk)] for chunk in chunks]

    def cross(step, after):
        held = [hold(packed[job], after) if after else packed[job] for job in step]
        return held, [swap_flipped(piece, "tensor", job[0]) for job, piece in zip(step, held)]

    def spread(piece):
        return piece, swap_pairs(piece, "dp", 0), swap_pairs(piece, "dp", 1)

    _, crossed = cross(steps[0], [])
    sent = [spread(packed[(0, 0, head_total)])]
    outs, joined, number = None, None, 0
    for span, chunks in zip(spans, groups):
        for place in range(1 + len(chunks)):
            after = list(sent[-1][1:])
            received, held = crossed, []
            number += 1
            if number < len(steps):
                held, crossed = cross(steps[number], [received[-1]])
            elif outs is not None:
                after.append(outs[0])
            cost = between(sent[-1][0], received[0], 1 if span is spans[0] else 2)
            held.append(sent[-1][0])
            if place == 0:
                joined = spread(hold(join(received, held, cost), after))
                sent.append(joined)
                continue
            piece = spread(hold(hold(received[0], held, cost), after))
            sent.append(piece)
            first_head, count = chunks[place - 1]
            offsets = (first_head, first_head - span[0], 0)
            outs = attend(
                near_ids, list(zip(sent[0], joined, piece)), offsets, outs, first_head, count
            )
    return tuple(outs)


def solution(mesh):
    return jax.shard_map(
        shards,
        mesh=mesh,
        in_specs=(
            P(("dp", "tensor"), None),
            P(("dp", "tensor"), None),
            P(("dp", "tensor"), None),
            P(("dp", "tensor"), None),
            P(),
        ),
        out_specs=(P("dp", "tensor"), P("dp", "tensor"), P("dp", "tensor"), P("dp", "tensor")),
        check_vma=False,
    )
```

```python
import functools
import math

import jax
import jax.numpy as jnp
from jax import lax
from jax.experimental import pallas as pl
from jax.experimental.pallas import tpu as pltpu
from jax.sharding import PartitionSpec as P

HD = 128
SCALE = 1.0 / math.sqrt(HD)
EXP2_SCALE = SCALE * math.log2(math.e)
MASKED = -1e30
GROUPS = ((8,), (4,))
VMEM_LIMIT = 64 * 1024 * 1024 - 256 * 1024
ATTEND_FLOPS = 1_500_000_000
FLOPS_PER_BYTE = 52_000
SMALL_COST = pl.CostEstimate(flops=1, bytes_accessed=1, transcendentals=0)


def split_counts(total, shares):
    whole = sum(shares)
    edges = [round(total * sum(shares[:i]) / whole) for i in range(len(shares) + 1)]
    return [(a, b - a) for a, b in zip(edges[:-1], edges[1:]) if b > a]


def swap_pairs(block, axis, first):
    count = lax.axis_size(axis)
    route = []
    for low in range(first, count - 1, 2):
        route += [(low, low + 1), (low + 1, low)]
    return lax.ppermute(block, axis, route)


def swap_flipped(block, axis, flip):
    return lax.ppermute(block, axis, [(i, i ^ flip) for i in range(lax.axis_size(axis))])


def nearby_ids(image_ids, parts, part_rows):
    shard = lax.axis_index("dp")
    padded = jnp.pad(image_ids[::part_rows], (parts, parts), constant_values=-1)
    odd = lax.rem(shard, 2)

    def ids_of(other):
        return lax.dynamic_slice_in_dim(padded, (other + 1) * parts, parts)

    return jnp.stack((ids_of(shard), ids_of(shard + 1 - 2 * odd), ids_of(shard - 1 + 2 * odd)))


def columns(array, part, stride, first, width):
    start = pl.multiple_of(part * stride + first, HD)
    return array.at[:, pl.ds(start, width)]


def pack_kernel(stride, jobs, *refs):
    arrays, packed, (stage, in_sems, out_sems) = refs[:4], refs[4:-3], refs[-3:]
    me = lax.axis_index("tensor")
    loads, stores = [], []
    for number, (flip, first, count) in enumerate(jobs):
        for index, array in enumerate(arrays):
            load = pltpu.make_async_copy(
                columns(array, me ^ flip, stride, first * HD, count * HD),
                stage.at[flip, index, :, pl.ds(first * HD, count * HD)],
                in_sems.at[number * 4 + index],
            )
            load.start()
            loads.append(load)
    for number, (flip, first, count) in enumerate(jobs):
        for load in loads[number * 4 : number * 4 + 4]:
            load.wait()
        store = pltpu.make_async_copy(
            stage.at[flip, :, :, pl.ds(first * HD, count * HD)],
            packed[number],
            out_sems.at[number],
        )
        store.start()
        stores.append(store)
    for store in stores:
        store.wait()


def pack(arrays, parts, jobs):
    rows, total = arrays[0].shape
    stride = total // parts
    return pl.pallas_call(
        functools.partial(pack_kernel, stride, jobs),
        out_shape=[
            jax.ShapeDtypeStruct((4, rows, count * HD), jnp.bfloat16) for _, _, count in jobs
        ],
        in_specs=[pl.BlockSpec(memory_space=pl.ANY)] * 4,
        out_specs=[pl.BlockSpec(memory_space=pl.ANY)] * len(jobs),
        scratch_shapes=[
            pltpu.VMEM((parts, 4, rows, stride), jnp.bfloat16),
            pltpu.SemaphoreType.DMA((4 * len(jobs),)),
            pltpu.SemaphoreType.DMA((len(jobs),)),
        ],
        compiler_params=pltpu.CompilerParams(vmem_limit_bytes=VMEM_LIMIT),
        cost_estimate=SMALL_COST,
    )(*arrays)


def join_kernel(pieces, *refs):
    received, (joined, stage, in_sems, out_sems) = refs[:pieces], refs[-4:]
    loads, stores = [], []
    for piece in range(pieces):
        load = pltpu.make_async_copy(received[piece], stage.at[piece], in_sems.at[piece])
        load.start()
        loads.append(load)
    for piece in range(pieces):
        loads[piece].wait()
        store = pltpu.make_async_copy(stage.at[piece], joined.at[piece], out_sems.at[piece])
        store.start()
        stores.append(store)
    for store in stores:
        store.wait()


def join(received, after, cost):
    pieces = len(received)
    shape = (pieces,) + received[0].shape
    return pl.pallas_call(
        functools.partial(join_kernel, pieces),
        out_shape=jax.ShapeDtypeStruct(shape, jnp.bfloat16),
        in_specs=[pl.BlockSpec(memory_space=pl.ANY)] * (pieces + len(after)),
        out_specs=pl.BlockSpec(memory_space=pl.ANY),
        scratch_shapes=[
            pltpu.VMEM(shape, jnp.bfloat16),
            pltpu.SemaphoreType.DMA((pieces,)),
            pltpu.SemaphoreType.DMA((pieces,)),
        ],
        compiler_params=pltpu.CompilerParams(vmem_limit_bytes=VMEM_LIMIT),
        cost_estimate=cost,
    )(*received, *after)


def hold(array, after, cost=SMALL_COST):
    return pl.pallas_call(
        lambda *refs: None,
        out_shape=jax.ShapeDtypeStruct(array.shape, array.dtype),
        in_specs=[pl.BlockSpec(memory_space=pl.ANY)] * (1 + len(after)),
        out_specs=pl.BlockSpec(memory_space=pl.ANY),
        input_output_aliases={0: 0},
        compiler_params=pltpu.CompilerParams(vmem_limit_bytes=VMEM_LIMIT),
        cost_estimate=cost,
    )(array, *after)


def dot_nt(a, b):
    return lax.dot_general(a, b, (((1,), (1,)), ((), ())), preferred_element_type=jnp.float32)


def dot_tn(a, b):
    return lax.dot_general(a, b, (((0,), (0,)), ((), ())), preferred_element_type=jnp.float32)


def dot_nn(a, b):
    return jnp.dot(a, b, preferred_element_type=jnp.float32)


def attend_heads(heads, slot_ids, lane_ids, part_rows, rows):
    size = heads[0][0].shape[0]
    slots = size // part_rows

    def per_slot(array):
        return [array[slot * part_rows : (slot + 1) * part_rows] for slot in range(slots)]

    def over_slots(reduce, combine, arrays):
        total = reduce(arrays[0], axis=0, keepdims=True)
        for array in arrays[1:]:
            total = combine(total, reduce(array, axis=0, keepdims=True))
        return total

    def products(head, start):
        queries, keys, values, grads = heads[head]
        tile = slice(start, start + rows)
        return dot_nt(keys, queries[tile]), dot_nt(values, grads[tile])

    def weigh(scores, grad_probs, start):
        lanes = lane_ids[:, start : start + rows]
        scores = [
            part + jnp.where(lanes == slot_id, 0.0, MASKED)
            for part, slot_id in zip(per_slot(scores), slot_ids)
        ]
        row_max = over_slots(jnp.max, jnp.maximum, scores)
        weights = [jnp.exp2((part - row_max) * EXP2_SCALE) for part in scores]
        inverse = 1.0 / over_slots(jnp.sum, jnp.add, weights)
        probs = [part * inverse for part in weights]
        grad_probs = per_slot(grad_probs)
        inner = over_slots(jnp.sum, jnp.add, [p * g for p, g in zip(probs, grad_probs)])
        low = jnp.concatenate([p.astype(jnp.bfloat16) for p in probs])
        grad_scores = [(p * (g - inner)).astype(jnp.bfloat16) for p, g in zip(probs, grad_probs)]
        return low, jnp.concatenate(grad_scores)

    def finish(head, low, grad_scores, start):
        queries, keys, values, grads = heads[head]
        tile = slice(start, start + rows)
        result = results[head]
        if start == 0:
            result[0] = dot_tn(values, low).astype(jnp.bfloat16).T
            result[1] = (dot_tn(keys, grad_scores) * SCALE).astype(jnp.bfloat16).T
            result[2] = result[3] = 0.0
        result[2] += dot_nn(grad_scores[:rows], queries[tile])
        result[3] += dot_nn(low[:rows], grads[tile])

    results = [[None] * 4 for _ in heads]
    work = [(head, start) for head in range(len(heads)) for start in range(0, size, rows)]
    ahead = products(*work[0])
    for number, (head, start) in enumerate(work):
        scores, grad_probs = ahead
        if number + 1 < len(work):
            ahead = products(*work[number + 1])
        finish(head, *weigh(scores, grad_probs, start), start)
    for result in results:
        result[2] = (result[2] * SCALE).astype(jnp.bfloat16)
        result[3] = result[3].astype(jnp.bfloat16)
    return results


def attend_kernel(parts, part_rows, steps, width, offsets, has_outs, *refs):
    image_ids, mine, sides = refs[0], refs[1:4], (refs[4:7], refs[7:10])
    refs = refs[10 + (4 if has_outs else 0) :]
    outs, (window, lane_ids, slot_of, table, sems) = refs[:4], refs[4:]
    rows = parts * part_rows
    most = 3 * rows
    last = parts - 1
    me = lax.axis_index("tensor")
    step = pl.program_id(0)

    def copy_of(group, flip, number, place, sem):
        kind = 0 if flip == 0 else 2 if flip == last else 1
        buffer = lax.rem(number, 2)
        start = pl.multiple_of(place * part_rows, part_rows)
        column = pl.multiple_of(number * width + offsets[kind] * HD, HD)
        source = group[kind].at[flip - 1] if kind == 1 else group[kind]
        return pltpu.make_async_copy(
            source.at[:, :, pl.ds(column, width)],
            window.at[buffer, :, pl.ds(start, part_rows), :],
            sems.at[buffer, sem],
        )

    def copies(number, act):
        for flip in range(parts):
            act(copy_of(mine, flip, number, me ^ flip, flip))
        for source in range(2 * parts):
            slot = slot_of[source]

            @pl.when(slot >= 0)
            def _():
                group = sides[source // parts]
                act(copy_of(group, source % parts, number, parts + slot, parts + source))

    @pl.when(step == 0)
    def _():
        count = jnp.int32(0)
        for slot in range(2 * parts):
            table[slot] = -2
        for source in range(2 * parts):
            side, flip = 1 + source // parts, source % parts
            other_id = image_ids[side, me ^ flip]
            shared = other_id == image_ids[0, 0]
            for part in range(1, parts):
                shared = shared | (other_id == image_ids[0, part])
            slot_of[source] = jnp.where(shared, count, -1)
            table[count] = jnp.where(shared, other_id, -2)
            count = count + shared.astype(jnp.int32)
        table[2 * parts] = count
        window[:, :, rows:] = jnp.zeros((2, 4, most - rows, width), window.dtype)
        copies(0, lambda copy: copy.start())
        place = lax.broadcasted_iota(jnp.int32, (8, most), 1)
        ids = jnp.full((8, most), -2, jnp.int32)
        for slot in range(3 * parts):
            slot_id = image_ids[0, slot] if slot < parts else table[slot - parts]
            inside = (place >= slot * part_rows) & (place < (slot + 1) * part_rows)
            ids = jnp.where(inside, slot_id, ids)
        lane_ids[...] = ids

    @pl.when(step + 1 < steps)
    def _():
        copies(step + 1, lambda copy: copy.start())

    copies(step, lambda copy: copy.wait())
    count = table[2 * parts]
    buffer = lax.rem(step, 2)
    for size in range(rows, most + 1, rows):
        slots = (size - rows) // part_rows

        @pl.when((count <= slots) & (count > slots - parts))
        def _():
            slot_ids = [image_ids[0, slot] for slot in range(parts)]
            slot_ids += [table[slot] for slot in range(slots)]
            spans = [slice(start, start + HD) for start in range(0, width, HD)]
            heads = [[window[buffer, i, :size, span] for i in range(4)] for span in spans]
            results = attend_heads(heads, slot_ids, lane_ids[0:1], part_rows, rows)
            for span, result in zip(spans, results):
                for out, part in zip(outs, result):
                    out[:, span] = part


def attend(image_ids, groups, offsets, outs, first_head, heads):
    _, part_rows, total = groups[0][0].shape
    parts = groups[0][1].shape[0] + 2
    rows = parts * part_rows
    width = HD * math.gcd(2, math.gcd(first_head, heads))
    steps = heads * HD // width
    first_block = first_head * HD // width
    out_spec = pl.BlockSpec((rows, width), lambda s: (0, s + first_block))
    has_outs = outs is not None
    pieces = [piece for group in groups for piece in group]
    aliases = {1 + len(pieces) + i: i for i in range(4)} if has_outs else {}
    return pl.pallas_call(
        functools.partial(
            attend_kernel, parts, part_rows, steps, width, offsets, has_outs
        ),
        grid=(steps,),
        out_shape=[jax.ShapeDtypeStruct((rows, total), jnp.bfloat16)] * 4,
        in_specs=[pl.BlockSpec(memory_space=pltpu.SMEM)]
        + [pl.BlockSpec(memory_space=pl.ANY)] * (len(pieces) + (4 if has_outs else 0)),
        out_specs=[out_spec] * 4,
        scratch_shapes=[
            pltpu.VMEM((2, 4, 3 * rows, width), jnp.bfloat16),
            pltpu.VMEM((8, 3 * rows), jnp.int32),
            pltpu.SMEM((2 * parts,), jnp.int32),
            pltpu.SMEM((2 * parts + 1,), jnp.int32),
            pltpu.SemaphoreType.DMA((2, 3 * parts)),
        ],
        input_output_aliases=aliases,
        compiler_params=pltpu.CompilerParams(
            dimension_semantics=("arbitrary",), vmem_limit_bytes=VMEM_LIMIT
        ),
        cost_estimate=pl.CostEstimate(
            flops=heads * ATTEND_FLOPS, bytes_accessed=1, transcendentals=0
        ),
    )(image_ids, *pieces, *(outs or ()))


def between(sent, received):
    flops = FLOPS_PER_BYTE * (2 * sent.size - received.size)
    return pl.CostEstimate(flops=flops, bytes_accessed=1, transcendentals=0)


def shards(queries, key_vectors, value_vectors, grad_output, image_ids):
    arrays = (queries, key_vectors, value_vectors, grad_output)
    parts = lax.axis_size("tensor")
    part_rows = queries.shape[0]
    head_total = queries.shape[1] // HD // parts
    near_ids = nearby_ids(image_ids, parts, part_rows)
    last = parts - 1
    spans = split_counts(head_total, [sum(shares) for shares in GROUPS])
    groups = []
    for (start, count), shares in zip(spans, GROUPS):
        groups.append([(start + first, size) for first, size in split_counts(count, shares)])

    jobs = []
    for span, chunks in zip(spans, groups):
        jobs += [(flip, *span) for flip in range(last - 1, 0, -1)]
        jobs += [(last, *chunk) for chunk in chunks]
    jobs.insert(last - 1, (0, 0, head_total))
    packed = dict(zip(jobs, pack(arrays, parts, jobs)))

    steps = []
    for span, chunks in zip(spans, groups):
        steps.append([(flip, *span) for flip in range(1, last)])
        steps += [[(last, *chunk)] for chunk in chunks]

    def cross(step, after, cost=SMALL_COST, late=()):
        held = [hold(packed[job], after, cost) if after else packed[job] for job in step]
        held = [hold(piece, late) if late else piece for piece in held]
        return held, [swap_flipped(piece, "tensor", job[0]) for job, piece in zip(step, held)]

    def spread(piece):
        return piece, swap_pairs(piece, "dp", 0), swap_pairs(piece, "dp", 1)

    _, crossed = cross(steps[0], [])
    sent = [spread(packed[(0, 0, head_total)])]
    outs, joined, number = None, None, 0
    for span, chunks in zip(spans, groups):
        for place in range(1 + len(chunks)):
            after = list(sent[-1][1:])
            received, held = crossed, []
            number += 1
            if number < len(steps):
                late = sent[-1][1:] if number > 1 and place == 0 else ()
                cost = between(sent[-1][0], received[0]) if late else SMALL_COST
                held, crossed = cross(steps[number], [received[-1]], cost, late)
            elif outs is not None:
                after.append(outs[0])
            cost = between(sent[-1][0], received[0])
            held.append(sent[-1][0])
            if place == 0:
                joined = spread(hold(join(received, held, cost), after))
                sent.append(joined)
                continue
            piece = spread(hold(hold(received[0], held, cost), after))
            sent.append(piece)
            first_head, count = chunks[place - 1]
            offsets = (first_head, first_head - span[0], 0)
            outs = attend(
                near_ids, list(zip(sent[0], joined, piece)), offsets, outs, first_head, count
            )
    return tuple(outs)


def solution(mesh):
    return jax.shard_map(
        shards,
        mesh=mesh,
        in_specs=(
            P(("dp", "tensor"), None),
            P(("dp", "tensor"), None),
            P(("dp", "tensor"), None),
            P(("dp", "tensor"), None),
            P(),
        ),
        out_specs=(P("dp", "tensor"), P("dp", "tensor"), P("dp", "tensor"), P("dp", "tensor")),
        check_vma=False,
    )
```

```python
import functools
import math

import jax
import jax.numpy as jnp
from jax import lax
from jax.experimental import pallas as pl
from jax.experimental.pallas import tpu as pltpu
from jax.sharding import PartitionSpec as P

HD = 128
SCALE = 1.0 / math.sqrt(HD)
EXP2_SCALE = SCALE * math.log2(math.e)
MASKED = -1e30
GROUPS = ((6,), (6,))
VMEM_LIMIT = 64 * 1024 * 1024 - 256 * 1024
ATTEND_FLOPS = 1_500_000_000
FLOPS_PER_BYTE = 52_000
SMALL_COST = pl.CostEstimate(flops=1, bytes_accessed=1, transcendentals=0)


def split_counts(total, shares):
    whole = sum(shares)
    edges = [round(total * sum(shares[:i]) / whole) for i in range(len(shares) + 1)]
    return [(a, b - a) for a, b in zip(edges[:-1], edges[1:]) if b > a]


def swap_pairs(block, axis, first):
    count = lax.axis_size(axis)
    route = []
    for low in range(first, count - 1, 2):
        route += [(low, low + 1), (low + 1, low)]
    return lax.ppermute(block, axis, route)


def swap_flipped(block, axis, flip):
    return lax.ppermute(block, axis, [(i, i ^ flip) for i in range(lax.axis_size(axis))])


def nearby_ids(image_ids, parts, part_rows):
    shard = lax.axis_index("dp")
    padded = jnp.pad(image_ids[::part_rows], (parts, parts), constant_values=-1)
    odd = lax.rem(shard, 2)

    def ids_of(other):
        return lax.dynamic_slice_in_dim(padded, (other + 1) * parts, parts)

    return jnp.stack((ids_of(shard), ids_of(shard + 1 - 2 * odd), ids_of(shard - 1 + 2 * odd)))


def columns(array, part, stride, first, width):
    start = pl.multiple_of(part * stride + first, HD)
    return array.at[:, pl.ds(start, width)]


def pack_kernel(stride, jobs, *refs):
    arrays, packed, (stage, in_sems, out_sems) = refs[:4], refs[4:-3], refs[-3:]
    me = lax.axis_index("tensor")
    loads, stores = [], []
    for number, (flip, first, count) in enumerate(jobs):
        for index, array in enumerate(arrays):
            load = pltpu.make_async_copy(
                columns(array, me ^ flip, stride, first * HD, count * HD),
                stage.at[flip, index, :, pl.ds(first * HD, count * HD)],
                in_sems.at[number * 4 + index],
            )
            load.start()
            loads.append(load)
    for number, (flip, first, count) in enumerate(jobs):
        for load in loads[number * 4 : number * 4 + 4]:
            load.wait()
        store = pltpu.make_async_copy(
            stage.at[flip, :, :, pl.ds(first * HD, count * HD)],
            packed[number],
            out_sems.at[number],
        )
        store.start()
        stores.append(store)
    for store in stores:
        store.wait()


def pack(arrays, parts, jobs):
    rows, total = arrays[0].shape
    stride = total // parts
    return pl.pallas_call(
        functools.partial(pack_kernel, stride, jobs),
        out_shape=[
            jax.ShapeDtypeStruct((4, rows, count * HD), jnp.bfloat16) for _, _, count in jobs
        ],
        in_specs=[pl.BlockSpec(memory_space=pl.ANY)] * 4,
        out_specs=[pl.BlockSpec(memory_space=pl.ANY)] * len(jobs),
        scratch_shapes=[
            pltpu.VMEM((parts, 4, rows, stride), jnp.bfloat16),
            pltpu.SemaphoreType.DMA((4 * len(jobs),)),
            pltpu.SemaphoreType.DMA((len(jobs),)),
        ],
        compiler_params=pltpu.CompilerParams(vmem_limit_bytes=VMEM_LIMIT),
        cost_estimate=SMALL_COST,
    )(*arrays)


def join_kernel(pieces, *refs):
    received, (joined, stage, in_sems, out_sems) = refs[:pieces], refs[-4:]
    loads, stores = [], []
    for piece in range(pieces):
        load = pltpu.make_async_copy(received[piece], stage.at[piece], in_sems.at[piece])
        load.start()
        loads.append(load)
    for piece in range(pieces):
        loads[piece].wait()
        store = pltpu.make_async_copy(stage.at[piece], joined.at[piece], out_sems.at[piece])
        store.start()
        stores.append(store)
    for store in stores:
        store.wait()


def join(received, after, cost):
    pieces = len(received)
    shape = (pieces,) + received[0].shape
    return pl.pallas_call(
        functools.partial(join_kernel, pieces),
        out_shape=jax.ShapeDtypeStruct(shape, jnp.bfloat16),
        in_specs=[pl.BlockSpec(memory_space=pl.ANY)] * (pieces + len(after)),
        out_specs=pl.BlockSpec(memory_space=pl.ANY),
        scratch_shapes=[
            pltpu.VMEM(shape, jnp.bfloat16),
            pltpu.SemaphoreType.DMA((pieces,)),
            pltpu.SemaphoreType.DMA((pieces,)),
        ],
        compiler_params=pltpu.CompilerParams(vmem_limit_bytes=VMEM_LIMIT),
        cost_estimate=cost,
    )(*received, *after)


def hold(array, after, cost=SMALL_COST):
    return pl.pallas_call(
        lambda *refs: None,
        out_shape=jax.ShapeDtypeStruct(array.shape, array.dtype),
        in_specs=[pl.BlockSpec(memory_space=pl.ANY)] * (1 + len(after)),
        out_specs=pl.BlockSpec(memory_space=pl.ANY),
        input_output_aliases={0: 0},
        compiler_params=pltpu.CompilerParams(vmem_limit_bytes=VMEM_LIMIT),
        cost_estimate=cost,
    )(array, *after)


def dot_nt(a, b):
    return lax.dot_general(a, b, (((1,), (1,)), ((), ())), preferred_element_type=jnp.float32)


def dot_tn(a, b):
    return lax.dot_general(a, b, (((0,), (0,)), ((), ())), preferred_element_type=jnp.float32)


def dot_nn(a, b):
    return jnp.dot(a, b, preferred_element_type=jnp.float32)


def attend_heads(heads, slot_ids, lane_ids, part_rows, rows):
    size = heads[0][0].shape[0]
    slots = size // part_rows

    def per_slot(array):
        return [array[slot * part_rows : (slot + 1) * part_rows] for slot in range(slots)]

    def over_slots(reduce, combine, arrays):
        total = reduce(arrays[0], axis=0, keepdims=True)
        for array in arrays[1:]:
            total = combine(total, reduce(array, axis=0, keepdims=True))
        return total

    def products(head, start):
        queries, keys, values, grads = heads[head]
        tile = slice(start, start + rows)
        return dot_nt(keys, queries[tile]), dot_nt(values, grads[tile])

    def weigh(scores, grad_probs, start):
        lanes = lane_ids[:, start : start + rows]
        scores = [
            part + jnp.where(lanes == slot_id, 0.0, MASKED)
            for part, slot_id in zip(per_slot(scores), slot_ids)
        ]
        row_max = over_slots(jnp.max, jnp.maximum, scores)
        weights = [jnp.exp2((part - row_max) * EXP2_SCALE) for part in scores]
        inverse = 1.0 / over_slots(jnp.sum, jnp.add, weights)
        probs = [part * inverse for part in weights]
        grad_probs = per_slot(grad_probs)
        inner = over_slots(jnp.sum, jnp.add, [p * g for p, g in zip(probs, grad_probs)])
        low = jnp.concatenate([p.astype(jnp.bfloat16) for p in probs])
        grad_scores = [(p * (g - inner)).astype(jnp.bfloat16) for p, g in zip(probs, grad_probs)]
        return low, jnp.concatenate(grad_scores)

    def finish(head, low, grad_scores, start):
        queries, keys, values, grads = heads[head]
        tile = slice(start, start + rows)
        result = results[head]
        if start == 0:
            result[0] = dot_tn(values, low).astype(jnp.bfloat16).T
            result[1] = (dot_tn(keys, grad_scores) * SCALE).astype(jnp.bfloat16).T
            result[2] = result[3] = 0.0
        result[2] += dot_nn(grad_scores[:rows], queries[tile])
        result[3] += dot_nn(low[:rows], grads[tile])

    results = [[None] * 4 for _ in heads]
    work = [(head, start) for head in range(len(heads)) for start in range(0, size, rows)]
    ahead = products(*work[0])
    for number, (head, start) in enumerate(work):
        scores, grad_probs = ahead
        if number + 1 < len(work):
            ahead = products(*work[number + 1])
        finish(head, *weigh(scores, grad_probs, start), start)
    for result in results:
        result[2] = (result[2] * SCALE).astype(jnp.bfloat16)
        result[3] = result[3].astype(jnp.bfloat16)
    return results


def attend_kernel(parts, part_rows, steps, width, offsets, has_outs, *refs):
    image_ids, mine, sides = refs[0], refs[1:4], (refs[4:7], refs[7:10])
    refs = refs[10 + (4 if has_outs else 0) :]
    outs, (window, lane_ids, slot_of, table, sems) = refs[:4], refs[4:]
    rows = parts * part_rows
    most = 3 * rows
    last = parts - 1
    me = lax.axis_index("tensor")
    step = pl.program_id(0)

    def copy_of(group, flip, number, place, sem):
        kind = 0 if flip == 0 else 2 if flip == last else 1
        buffer = lax.rem(number, 2)
        start = pl.multiple_of(place * part_rows, part_rows)
        column = pl.multiple_of(number * width + offsets[kind] * HD, HD)
        source = group[kind].at[flip - 1] if kind == 1 else group[kind]
        return pltpu.make_async_copy(
            source.at[:, :, pl.ds(column, width)],
            window.at[buffer, :, pl.ds(start, part_rows), :],
            sems.at[buffer, sem],
        )

    def copies(number, act):
        for flip in range(parts):
            act(copy_of(mine, flip, number, me ^ flip, flip))
        for source in range(2 * parts):
            slot = slot_of[source]

            @pl.when(slot >= 0)
            def _():
                group = sides[source // parts]
                act(copy_of(group, source % parts, number, parts + slot, parts + source))

    @pl.when(step == 0)
    def _():
        count = jnp.int32(0)
        for slot in range(2 * parts):
            table[slot] = -2
        for source in range(2 * parts):
            side, flip = 1 + source // parts, source % parts
            other_id = image_ids[side, me ^ flip]
            shared = other_id == image_ids[0, 0]
            for part in range(1, parts):
                shared = shared | (other_id == image_ids[0, part])
            slot_of[source] = jnp.where(shared, count, -1)
            table[count] = jnp.where(shared, other_id, -2)
            count = count + shared.astype(jnp.int32)
        table[2 * parts] = count
        window[:, :, rows:] = jnp.zeros((2, 4, most - rows, width), window.dtype)
        copies(0, lambda copy: copy.start())
        place = lax.broadcasted_iota(jnp.int32, (8, most), 1)
        ids = jnp.full((8, most), -2, jnp.int32)
        for slot in range(3 * parts):
            slot_id = image_ids[0, slot] if slot < parts else table[slot - parts]
            inside = (place >= slot * part_rows) & (place < (slot + 1) * part_rows)
            ids = jnp.where(inside, slot_id, ids)
        lane_ids[...] = ids

    @pl.when(step + 1 < steps)
    def _():
        copies(step + 1, lambda copy: copy.start())

    copies(step, lambda copy: copy.wait())
    count = table[2 * parts]
    buffer = lax.rem(step, 2)
    for size in range(rows, most + 1, rows):
        slots = (size - rows) // part_rows

        @pl.when((count <= slots) & (count > slots - parts))
        def _():
            slot_ids = [image_ids[0, slot] for slot in range(parts)]
            slot_ids += [table[slot] for slot in range(slots)]
            spans = [slice(start, start + HD) for start in range(0, width, HD)]
            heads = [[window[buffer, i, :size, span] for i in range(4)] for span in spans]
            results = attend_heads(heads, slot_ids, lane_ids[0:1], part_rows, rows)
            for span, result in zip(spans, results):
                for out, part in zip(outs, result):
                    out[:, span] = part


def attend(image_ids, groups, offsets, outs, first_head, heads):
    _, part_rows, total = groups[0][0].shape
    parts = groups[0][1].shape[0] + 2
    rows = parts * part_rows
    width = HD * math.gcd(2, math.gcd(first_head, heads))
    steps = heads * HD // width
    first_block = first_head * HD // width
    out_spec = pl.BlockSpec((rows, width), lambda s: (0, s + first_block))
    has_outs = outs is not None
    pieces = [piece for group in groups for piece in group]
    aliases = {1 + len(pieces) + i: i for i in range(4)} if has_outs else {}
    return pl.pallas_call(
        functools.partial(
            attend_kernel, parts, part_rows, steps, width, offsets, has_outs
        ),
        grid=(steps,),
        out_shape=[jax.ShapeDtypeStruct((rows, total), jnp.bfloat16)] * 4,
        in_specs=[pl.BlockSpec(memory_space=pltpu.SMEM)]
        + [pl.BlockSpec(memory_space=pl.ANY)] * (len(pieces) + (4 if has_outs else 0)),
        out_specs=[out_spec] * 4,
        scratch_shapes=[
            pltpu.VMEM((2, 4, 3 * rows, width), jnp.bfloat16),
            pltpu.VMEM((8, 3 * rows), jnp.int32),
            pltpu.SMEM((2 * parts,), jnp.int32),
            pltpu.SMEM((2 * parts + 1,), jnp.int32),
            pltpu.SemaphoreType.DMA((2, 3 * parts)),
        ],
        input_output_aliases=aliases,
        compiler_params=pltpu.CompilerParams(
            dimension_semantics=("arbitrary",), vmem_limit_bytes=VMEM_LIMIT
        ),
        cost_estimate=pl.CostEstimate(
            flops=heads * ATTEND_FLOPS, bytes_accessed=1, transcendentals=0
        ),
    )(image_ids, *pieces, *(outs or ()))


def between(sent, received):
    flops = FLOPS_PER_BYTE * (2 * sent.size - received.size)
    return pl.CostEstimate(flops=flops, bytes_accessed=1, transcendentals=0)


def shards(queries, key_vectors, value_vectors, grad_output, image_ids):
    arrays = (queries, key_vectors, value_vectors, grad_output)
    parts = lax.axis_size("tensor")
    part_rows = queries.shape[0]
    head_total = queries.shape[1] // HD // parts
    near_ids = nearby_ids(image_ids, parts, part_rows)
    last = parts - 1
    spans = split_counts(head_total, [sum(shares) for shares in GROUPS])
    groups = []
    for (start, count), shares in zip(spans, GROUPS):
        groups.append([(start + first, size) for first, size in split_counts(count, shares)])

    jobs = []
    for span, chunks in zip(spans, groups):
        jobs += [(flip, *span) for flip in range(last - 1, 0, -1)]
        jobs += [(last, *chunk) for chunk in chunks]
    jobs.insert(last - 1, (0, 0, head_total))
    soon, later = jobs[: last - 1], jobs[last - 1 :]
    packed = dict(zip(soon, pack(arrays, parts, soon)))
    packed.update(zip(later, pack(arrays, parts, later)))

    steps = []
    for span, chunks in zip(spans, groups):
        steps.append([(flip, *span) for flip in range(1, last)])
        steps += [[(last, *chunk)] for chunk in chunks]

    def cross(step, after, cost=SMALL_COST, late=()):
        held = [hold(packed[job], after, cost) if after else packed[job] for job in step]
        held = [hold(piece, late) if late else piece for piece in held]
        return held, [swap_flipped(piece, "tensor", job[0]) for job, piece in zip(step, held)]

    def spread(piece):
        return piece, swap_pairs(piece, "dp", 0), swap_pairs(piece, "dp", 1)

    _, crossed = cross(steps[0], [])
    sent = [spread(packed[(0, 0, head_total)])]
    outs, joined, number = None, None, 0
    for span, chunks in zip(spans, groups):
        for place in range(1 + len(chunks)):
            after = list(sent[-1][1:])
            received, held = crossed, []
            number += 1
            if number < len(steps):
                late = sent[-1][1:] if number > 1 and place == 0 else ()
                cost = between(sent[-1][0], received[0]) if late else SMALL_COST
                held, crossed = cross(steps[number], [received[-1]], cost, late)
            elif outs is not None:
                after.append(outs[0])
            cost = between(sent[-1][0], received[0])
            held.append(sent[-1][0])
            if place == 0:
                joined = spread(hold(join(received, held, cost), after))
                sent.append(joined)
                continue
            piece = spread(hold(hold(received[0], held, cost), after))
            sent.append(piece)
            first_head, count = chunks[place - 1]
            offsets = (first_head, first_head - span[0], 0)
            outs = attend(
                near_ids, list(zip(sent[0], joined, piece)), offsets, outs, first_head, count
            )
    return tuple(outs)


def solution(mesh):
    return jax.shard_map(
        shards,
        mesh=mesh,
        in_specs=(
            P(("dp", "tensor"), None),
            P(("dp", "tensor"), None),
            P(("dp", "tensor"), None),
            P(("dp", "tensor"), None),
            P(),
        ),
        out_specs=(P("dp", "tensor"), P("dp", "tensor"), P("dp", "tensor"), P("dp", "tensor")),
        check_vma=False,
    )
```

```python
import functools
import math

import jax
import jax.numpy as jnp
from jax import lax
from jax.experimental import pallas as pl
from jax.experimental.pallas import tpu as pltpu
from jax.sharding import PartitionSpec as P

HD = 128
SCALE = 1.0 / math.sqrt(HD)
EXP2_SCALE = SCALE * math.log2(math.e)
MASKED = -1e30
GROUPS = ((6,), (6,))
VMEM_LIMIT = 64 * 1024 * 1024 - 256 * 1024
ATTEND_FLOPS = 1_500_000_000
FLOPS_PER_BYTE = 52_000
SMALL_COST = pl.CostEstimate(flops=1, bytes_accessed=1, transcendentals=0)


def split_counts(total, shares):
    whole = sum(shares)
    edges = [round(total * sum(shares[:i]) / whole) for i in range(len(shares) + 1)]
    return [(a, b - a) for a, b in zip(edges[:-1], edges[1:]) if b > a]


def swap_pairs(block, axis, first):
    count = lax.axis_size(axis)
    route = []
    for low in range(first, count - 1, 2):
        route += [(low, low + 1), (low + 1, low)]
    return lax.ppermute(block, axis, route)


def swap_flipped(block, axis, flip):
    return lax.ppermute(block, axis, [(i, i ^ flip) for i in range(lax.axis_size(axis))])


def nearby_ids(image_ids, parts, part_rows):
    shard = lax.axis_index("dp")
    padded = jnp.pad(image_ids[::part_rows], (parts, parts), constant_values=-1)
    odd = lax.rem(shard, 2)

    def ids_of(other):
        return lax.dynamic_slice_in_dim(padded, (other + 1) * parts, parts)

    return jnp.stack((ids_of(shard), ids_of(shard + 1 - 2 * odd), ids_of(shard - 1 + 2 * odd)))


def columns(array, part, stride, first, width):
    start = pl.multiple_of(part * stride + first, HD)
    return array.at[:, pl.ds(start, width)]


def pack_kernel(stride, jobs, *refs):
    arrays, packed, (stage, in_sems, out_sems) = refs[:4], refs[4:-3], refs[-3:]
    me = lax.axis_index("tensor")
    loads, stores = [], []
    for number, (flip, first, count) in enumerate(jobs):
        for index, array in enumerate(arrays):
            load = pltpu.make_async_copy(
                columns(array, me ^ flip, stride, first * HD, count * HD),
                stage.at[flip, index, :, pl.ds(first * HD, count * HD)],
                in_sems.at[number * 4 + index],
            )
            load.start()
            loads.append(load)
    for number, (flip, first, count) in enumerate(jobs):
        for load in loads[number * 4 : number * 4 + 4]:
            load.wait()
        store = pltpu.make_async_copy(
            stage.at[flip, :, :, pl.ds(first * HD, count * HD)],
            packed[number],
            out_sems.at[number],
        )
        store.start()
        stores.append(store)
    for store in stores:
        store.wait()


def pack(arrays, parts, jobs):
    rows, total = arrays[0].shape
    stride = total // parts
    return pl.pallas_call(
        functools.partial(pack_kernel, stride, jobs),
        out_shape=[
            jax.ShapeDtypeStruct((4, rows, count * HD), jnp.bfloat16) for _, _, count in jobs
        ],
        in_specs=[pl.BlockSpec(memory_space=pl.ANY)] * 4,
        out_specs=[pl.BlockSpec(memory_space=pl.ANY)] * len(jobs),
        scratch_shapes=[
            pltpu.VMEM((parts, 4, rows, stride), jnp.bfloat16),
            pltpu.SemaphoreType.DMA((4 * len(jobs),)),
            pltpu.SemaphoreType.DMA((len(jobs),)),
        ],
        compiler_params=pltpu.CompilerParams(vmem_limit_bytes=VMEM_LIMIT),
        cost_estimate=SMALL_COST,
    )(*arrays)


def join_kernel(pieces, *refs):
    received, (joined, stage, in_sems, out_sems) = refs[:pieces], refs[-4:]
    loads, stores = [], []
    for piece in range(pieces):
        load = pltpu.make_async_copy(received[piece], stage.at[piece], in_sems.at[piece])
        load.start()
        loads.append(load)
    for piece in range(pieces):
        loads[piece].wait()
        store = pltpu.make_async_copy(stage.at[piece], joined.at[piece], out_sems.at[piece])
        store.start()
        stores.append(store)
    for store in stores:
        store.wait()


def join(received, after, cost):
    pieces = len(received)
    shape = (pieces,) + received[0].shape
    return pl.pallas_call(
        functools.partial(join_kernel, pieces),
        out_shape=jax.ShapeDtypeStruct(shape, jnp.bfloat16),
        in_specs=[pl.BlockSpec(memory_space=pl.ANY)] * (pieces + len(after)),
        out_specs=pl.BlockSpec(memory_space=pl.ANY),
        scratch_shapes=[
            pltpu.VMEM(shape, jnp.bfloat16),
            pltpu.SemaphoreType.DMA((pieces,)),
            pltpu.SemaphoreType.DMA((pieces,)),
        ],
        compiler_params=pltpu.CompilerParams(vmem_limit_bytes=VMEM_LIMIT),
        cost_estimate=cost,
    )(*received, *after)


def hold(array, after, cost=SMALL_COST):
    return pl.pallas_call(
        lambda *refs: None,
        out_shape=jax.ShapeDtypeStruct(array.shape, array.dtype),
        in_specs=[pl.BlockSpec(memory_space=pl.ANY)] * (1 + len(after)),
        out_specs=pl.BlockSpec(memory_space=pl.ANY),
        input_output_aliases={0: 0},
        compiler_params=pltpu.CompilerParams(vmem_limit_bytes=VMEM_LIMIT),
        cost_estimate=cost,
    )(array, *after)


def dot_nt(a, b):
    return lax.dot_general(a, b, (((1,), (1,)), ((), ())), preferred_element_type=jnp.float32)


def dot_tn(a, b):
    return lax.dot_general(a, b, (((0,), (0,)), ((), ())), preferred_element_type=jnp.float32)


def dot_nn(a, b):
    return jnp.dot(a, b, preferred_element_type=jnp.float32)


def attend_heads(heads, slot_ids, lane_ids, part_rows, rows):
    size = heads[0][0].shape[0]
    slots = size // part_rows

    def per_slot(array):
        return [array[slot * part_rows : (slot + 1) * part_rows] for slot in range(slots)]

    def over_slots(reduce, combine, arrays):
        total = reduce(arrays[0], axis=0, keepdims=True)
        for array in arrays[1:]:
            total = combine(total, reduce(array, axis=0, keepdims=True))
        return total

    def products(head, start):
        queries, keys, values, grads = heads[head]
        tile = slice(start, start + rows)
        return dot_nt(keys, queries[tile]), dot_nt(values, grads[tile])

    def weigh(scores, grad_probs, start):
        lanes = lane_ids[:, start : start + rows]
        scores = [
            part + jnp.where(lanes == slot_id, 0.0, MASKED)
            for part, slot_id in zip(per_slot(scores), slot_ids)
        ]
        row_max = over_slots(jnp.max, jnp.maximum, scores)
        weights = [jnp.exp2((part - row_max) * EXP2_SCALE) for part in scores]
        inverse = 1.0 / over_slots(jnp.sum, jnp.add, weights)
        probs = [part * inverse for part in weights]
        grad_probs = per_slot(grad_probs)
        inner = over_slots(jnp.sum, jnp.add, [p * g for p, g in zip(probs, grad_probs)])
        low = jnp.concatenate([p.astype(jnp.bfloat16) for p in probs])
        grad_scores = [(p * (g - inner)).astype(jnp.bfloat16) for p, g in zip(probs, grad_probs)]
        return low, jnp.concatenate(grad_scores)

    def finish(head, low, grad_scores, start):
        queries, keys, values, grads = heads[head]
        tile = slice(start, start + rows)
        result = results[head]
        if start == 0:
            result[0] = dot_tn(values, low).astype(jnp.bfloat16).T
            result[1] = (dot_tn(keys, grad_scores) * SCALE).astype(jnp.bfloat16).T
            result[2] = result[3] = 0.0
        result[2] += dot_nn(grad_scores[:rows], queries[tile])
        result[3] += dot_nn(low[:rows], grads[tile])

    results = [[None] * 4 for _ in heads]
    work = [(head, start) for head in range(len(heads)) for start in range(0, size, rows)]
    ahead = products(*work[0])
    for number, (head, start) in enumerate(work):
        scores, grad_probs = ahead
        if number + 1 < len(work):
            ahead = products(*work[number + 1])
        finish(head, *weigh(scores, grad_probs, start), start)
    for result in results:
        result[2] = (result[2] * SCALE).astype(jnp.bfloat16)
        result[3] = result[3].astype(jnp.bfloat16)
    return results


def attend_kernel(parts, part_rows, steps, width, offsets, has_outs, *refs):
    image_ids, mine, sides = refs[0], refs[1:4], (refs[4:7], refs[7:10])
    refs = refs[10 + (4 if has_outs else 0) :]
    outs, (window, lane_ids, slot_of, table, sems) = refs[:4], refs[4:]
    rows = parts * part_rows
    most = 3 * rows
    last = parts - 1
    me = lax.axis_index("tensor")
    step = pl.program_id(0)

    def copy_of(group, flip, number, place, sem):
        kind = 0 if flip == 0 else 2 if flip == last else 1
        buffer = lax.rem(number, 2)
        start = pl.multiple_of(place * part_rows, part_rows)
        column = pl.multiple_of(number * width + offsets[kind] * HD, HD)
        source = group[kind].at[flip - 1] if kind == 1 else group[kind]
        return pltpu.make_async_copy(
            source.at[:, :, pl.ds(column, width)],
            window.at[buffer, :, pl.ds(start, part_rows), :],
            sems.at[buffer, sem],
        )

    def copies(number, act):
        for flip in range(parts):
            act(copy_of(mine, flip, number, me ^ flip, flip))
        for source in range(2 * parts):
            slot = slot_of[source]

            @pl.when(slot >= 0)
            def _():
                group = sides[source // parts]
                act(copy_of(group, source % parts, number, parts + slot, parts + source))

    @pl.when(step == 0)
    def _():
        count = jnp.int32(0)
        for slot in range(2 * parts):
            table[slot] = -2
        for source in range(2 * parts):
            side, flip = 1 + source // parts, source % parts
            other_id = image_ids[side, me ^ flip]
            shared = other_id == image_ids[0, 0]
            for part in range(1, parts):
                shared = shared | (other_id == image_ids[0, part])
            slot_of[source] = jnp.where(shared, count, -1)
            table[count] = jnp.where(shared, other_id, -2)
            count = count + shared.astype(jnp.int32)
        table[2 * parts] = count
        window[:, :, rows:] = jnp.zeros((2, 4, most - rows, width), window.dtype)
        copies(0, lambda copy: copy.start())
        place = lax.broadcasted_iota(jnp.int32, (8, most), 1)
        ids = jnp.full((8, most), -2, jnp.int32)
        for slot in range(3 * parts):
            slot_id = image_ids[0, slot] if slot < parts else table[slot - parts]
            inside = (place >= slot * part_rows) & (place < (slot + 1) * part_rows)
            ids = jnp.where(inside, slot_id, ids)
        lane_ids[...] = ids

    @pl.when(step + 1 < steps)
    def _():
        copies(step + 1, lambda copy: copy.start())

    copies(step, lambda copy: copy.wait())
    count = table[2 * parts]
    buffer = lax.rem(step, 2)
    for size in range(rows, most + 1, rows):
        slots = (size - rows) // part_rows

        @pl.when((count <= slots) & (count > slots - parts))
        def _():
            slot_ids = [image_ids[0, slot] for slot in range(parts)]
            slot_ids += [table[slot] for slot in range(slots)]
            spans = [slice(start, start + HD) for start in range(0, width, HD)]
            heads = [[window[buffer, i, :size, span] for i in range(4)] for span in spans]
            results = attend_heads(heads, slot_ids, lane_ids[0:1], part_rows, rows)
            for span, result in zip(spans, results):
                for out, part in zip(outs, result):
                    out[:, span] = part


def attend(image_ids, groups, offsets, outs, first_head, heads):
    _, part_rows, total = groups[0][0].shape
    parts = groups[0][1].shape[0] + 2
    rows = parts * part_rows
    width = HD * math.gcd(2, math.gcd(first_head, heads))
    steps = heads * HD // width
    first_block = first_head * HD // width
    out_spec = pl.BlockSpec((rows, width), lambda s: (0, s + first_block))
    has_outs = outs is not None
    pieces = [piece for group in groups for piece in group]
    aliases = {1 + len(pieces) + i: i for i in range(4)} if has_outs else {}
    return pl.pallas_call(
        functools.partial(
            attend_kernel, parts, part_rows, steps, width, offsets, has_outs
        ),
        grid=(steps,),
        out_shape=[jax.ShapeDtypeStruct((rows, total), jnp.bfloat16)] * 4,
        in_specs=[pl.BlockSpec(memory_space=pltpu.SMEM)]
        + [pl.BlockSpec(memory_space=pl.ANY)] * (len(pieces) + (4 if has_outs else 0)),
        out_specs=[out_spec] * 4,
        scratch_shapes=[
            pltpu.VMEM((2, 4, 3 * rows, width), jnp.bfloat16),
            pltpu.VMEM((8, 3 * rows), jnp.int32),
            pltpu.SMEM((2 * parts,), jnp.int32),
            pltpu.SMEM((2 * parts + 1,), jnp.int32),
            pltpu.SemaphoreType.DMA((2, 3 * parts)),
        ],
        input_output_aliases=aliases,
        compiler_params=pltpu.CompilerParams(
            dimension_semantics=("arbitrary",), vmem_limit_bytes=VMEM_LIMIT
        ),
        cost_estimate=pl.CostEstimate(
            flops=heads * ATTEND_FLOPS, bytes_accessed=1, transcendentals=0
        ),
    )(image_ids, *pieces, *(outs or ()))


def between(sent, received):
    flops = FLOPS_PER_BYTE * (2 * sent.size - received.size)
    return pl.CostEstimate(flops=flops, bytes_accessed=1, transcendentals=0)


def shards(queries, key_vectors, value_vectors, grad_output, image_ids):
    arrays = (queries, key_vectors, value_vectors, grad_output)
    parts = lax.axis_size("tensor")
    part_rows = queries.shape[0]
    head_total = queries.shape[1] // HD // parts
    near_ids = nearby_ids(image_ids, parts, part_rows)
    last = parts - 1
    spans = split_counts(head_total, [sum(shares) for shares in GROUPS])
    groups = []
    for (start, count), shares in zip(spans, GROUPS):
        groups.append([(start + first, size) for first, size in split_counts(count, shares)])

    jobs = []
    for span, chunks in zip(spans, groups):
        jobs += [(flip, *span) for flip in range(last - 1, 0, -1)]
        jobs += [(last, *chunk) for chunk in chunks]
    jobs.insert(last - 1, (0, 0, head_total))
    soon, later = jobs[:last], jobs[last:]
    packed = dict(zip(soon, pack(arrays, parts, soon)))
    packed.update(zip(later, pack(arrays, parts, later)))

    steps = []
    for span, chunks in zip(spans, groups):
        steps.append([(flip, *span) for flip in range(1, last)])
        steps += [[(last, *chunk)] for chunk in chunks]

    def cross(step, after, cost=SMALL_COST, late=()):
        held = [hold(packed[job], after, cost) if after else packed[job] for job in step]
        held = [hold(piece, late) if late else piece for piece in held]
        return held, [swap_flipped(piece, "tensor", job[0]) for job, piece in zip(step, held)]

    def spread(piece):
        return piece, swap_pairs(piece, "dp", 0), swap_pairs(piece, "dp", 1)

    _, crossed = cross(steps[0], [])
    sent = [spread(packed[(0, 0, head_total)])]
    outs, joined, number = None, None, 0
    for span, chunks in zip(spans, groups):
        for place in range(1 + len(chunks)):
            after = list(sent[-1][1 : 3 if place == 0 else 2])
            received, held = crossed, []
            number += 1
            if number < len(steps):
                late = [*sent[-1][1:], sent[-2][2]] if number > 1 and place == 0 else ()
                cost = between(sent[-1][0], received[0]) if late else SMALL_COST
                held, crossed = cross(steps[number], [received[-1]], cost, late)
            elif outs is not None:
                after.append(outs[0])
            cost = between(sent[-1][0], received[0]) if place == 0 else SMALL_COST
            held.append(sent[-1][0])
            if place == 0:
                joined = spread(hold(join(received, held, cost), after))
                sent.append(joined)
                continue
            piece = spread(hold(hold(received[0], held, cost), after))
            sent.append(piece)
            first_head, count = chunks[place - 1]
            offsets = (first_head, first_head - span[0], 0)
            outs = attend(
                near_ids, list(zip(sent[0], joined, piece)), offsets, outs, first_head, count
            )
    return tuple(outs)


def solution(mesh):
    return jax.shard_map(
        shards,
        mesh=mesh,
        in_specs=(
            P(("dp", "tensor"), None),
            P(("dp", "tensor"), None),
            P(("dp", "tensor"), None),
            P(("dp", "tensor"), None),
            P(),
        ),
        out_specs=(P("dp", "tensor"), P("dp", "tensor"), P("dp", "tensor"), P("dp", "tensor")),
        check_vma=False,
    )
```

```python
import functools
import math

import jax
import jax.numpy as jnp
from jax import lax
from jax.experimental import pallas as pl
from jax.experimental.pallas import tpu as pltpu
from jax.sharding import PartitionSpec as P

HD = 128
SCALE = 1.0 / math.sqrt(HD)
EXP2_SCALE = SCALE * math.log2(math.e)
MASKED = -1e30
GROUPS = ((6,), (6,))
VMEM_LIMIT = 64 * 1024 * 1024 - 256 * 1024
ATTEND_FLOPS = 1_500_000_000
FLOPS_PER_BYTE = 52_000
SMALL_COST = pl.CostEstimate(flops=1, bytes_accessed=1, transcendentals=0)


def split_counts(total, shares):
    whole = sum(shares)
    edges = [round(total * sum(shares[:i]) / whole) for i in range(len(shares) + 1)]
    return [(a, b - a) for a, b in zip(edges[:-1], edges[1:]) if b > a]


def swap_pairs(block, axis, first):
    count = lax.axis_size(axis)
    route = []
    for low in range(first, count - 1, 2):
        route += [(low, low + 1), (low + 1, low)]
    return lax.ppermute(block, axis, route)


def swap_flipped(block, axis, flip):
    return lax.ppermute(block, axis, [(i, i ^ flip) for i in range(lax.axis_size(axis))])


def nearby_ids(image_ids, parts, part_rows):
    shard = lax.axis_index("dp")
    padded = jnp.pad(image_ids[::part_rows], (parts, parts), constant_values=-1)
    odd = lax.rem(shard, 2)

    def ids_of(other):
        return lax.dynamic_slice_in_dim(padded, (other + 1) * parts, parts)

    return jnp.stack((ids_of(shard), ids_of(shard + 1 - 2 * odd), ids_of(shard - 1 + 2 * odd)))


def columns(array, part, stride, first, width):
    start = pl.multiple_of(part * stride + first, HD)
    return array.at[:, pl.ds(start, width)]


def pack_kernel(stride, jobs, *refs):
    arrays, packed, (stage, in_sems, out_sems) = refs[:4], refs[4:-3], refs[-3:]
    me = lax.axis_index("tensor")
    loads, stores = [], []
    for number, (flip, first, count) in enumerate(jobs):
        for index, array in enumerate(arrays):
            load = pltpu.make_async_copy(
                columns(array, me ^ flip, stride, first * HD, count * HD),
                stage.at[flip, index, :, pl.ds(first * HD, count * HD)],
                in_sems.at[number * 4 + index],
            )
            load.start()
            loads.append(load)
    for number, (flip, first, count) in enumerate(jobs):
        for load in loads[number * 4 : number * 4 + 4]:
            load.wait()
        store = pltpu.make_async_copy(
            stage.at[flip, :, :, pl.ds(first * HD, count * HD)],
            packed[number],
            out_sems.at[number],
        )
        store.start()
        stores.append(store)
    for store in stores:
        store.wait()


def pack(arrays, parts, jobs):
    rows, total = arrays[0].shape
    stride = total // parts
    return pl.pallas_call(
        functools.partial(pack_kernel, stride, jobs),
        out_shape=[
            jax.ShapeDtypeStruct((4, rows, count * HD), jnp.bfloat16) for _, _, count in jobs
        ],
        in_specs=[pl.BlockSpec(memory_space=pl.ANY)] * 4,
        out_specs=[pl.BlockSpec(memory_space=pl.ANY)] * len(jobs),
        scratch_shapes=[
            pltpu.VMEM((parts, 4, rows, stride), jnp.bfloat16),
            pltpu.SemaphoreType.DMA((4 * len(jobs),)),
            pltpu.SemaphoreType.DMA((len(jobs),)),
        ],
        compiler_params=pltpu.CompilerParams(vmem_limit_bytes=VMEM_LIMIT),
        cost_estimate=SMALL_COST,
    )(*arrays)


def join_kernel(pieces, *refs):
    received, (joined, stage, in_sems, out_sems) = refs[:pieces], refs[-4:]
    loads, stores = [], []
    for piece in range(pieces):
        load = pltpu.make_async_copy(received[piece], stage.at[piece], in_sems.at[piece])
        load.start()
        loads.append(load)
    for piece in range(pieces):
        loads[piece].wait()
        store = pltpu.make_async_copy(stage.at[piece], joined.at[piece], out_sems.at[piece])
        store.start()
        stores.append(store)
    for store in stores:
        store.wait()


def join(received, after, cost):
    pieces = len(received)
    shape = (pieces,) + received[0].shape
    return pl.pallas_call(
        functools.partial(join_kernel, pieces),
        out_shape=jax.ShapeDtypeStruct(shape, jnp.bfloat16),
        in_specs=[pl.BlockSpec(memory_space=pl.ANY)] * (pieces + len(after)),
        out_specs=pl.BlockSpec(memory_space=pl.ANY),
        scratch_shapes=[
            pltpu.VMEM(shape, jnp.bfloat16),
            pltpu.SemaphoreType.DMA((pieces,)),
            pltpu.SemaphoreType.DMA((pieces,)),
        ],
        compiler_params=pltpu.CompilerParams(vmem_limit_bytes=VMEM_LIMIT),
        cost_estimate=cost,
    )(*received, *after)


def hold(array, after, cost=SMALL_COST):
    return pl.pallas_call(
        lambda *refs: None,
        out_shape=jax.ShapeDtypeStruct(array.shape, array.dtype),
        in_specs=[pl.BlockSpec(memory_space=pl.ANY)] * (1 + len(after)),
        out_specs=pl.BlockSpec(memory_space=pl.ANY),
        input_output_aliases={0: 0},
        compiler_params=pltpu.CompilerParams(vmem_limit_bytes=VMEM_LIMIT),
        cost_estimate=cost,
    )(array, *after)


def dot_nt(a, b):
    return lax.dot_general(a, b, (((1,), (1,)), ((), ())), preferred_element_type=jnp.float32)


def dot_tn(a, b):
    return lax.dot_general(a, b, (((0,), (0,)), ((), ())), preferred_element_type=jnp.float32)


def dot_nn(a, b):
    return jnp.dot(a, b, preferred_element_type=jnp.float32)


def attend_heads(heads, slot_ids, lane_ids, part_rows, rows):
    size = heads[0][0].shape[0]
    slots = size // part_rows

    def per_slot(array):
        return [array[slot * part_rows : (slot + 1) * part_rows] for slot in range(slots)]

    def over_slots(reduce, combine, arrays):
        total = reduce(arrays[0], axis=0, keepdims=True)
        for array in arrays[1:]:
            total = combine(total, reduce(array, axis=0, keepdims=True))
        return total

    def products(head, start):
        queries, keys, values, grads = heads[head]
        tile = slice(start, start + rows)
        return dot_nt(keys, queries[tile]), dot_nt(values, grads[tile])

    def weigh(scores, grad_probs, start):
        lanes = lane_ids[:, start : start + rows]
        scores = [
            part + jnp.where(lanes == slot_id, 0.0, MASKED)
            for part, slot_id in zip(per_slot(scores), slot_ids)
        ]
        row_max = over_slots(jnp.max, jnp.maximum, scores)
        weights = [jnp.exp2((part - row_max) * EXP2_SCALE) for part in scores]
        inverse = 1.0 / over_slots(jnp.sum, jnp.add, weights)
        probs = [part * inverse for part in weights]
        grad_probs = per_slot(grad_probs)
        inner = over_slots(jnp.sum, jnp.add, [p * g for p, g in zip(probs, grad_probs)])
        low = jnp.concatenate([p.astype(jnp.bfloat16) for p in probs])
        grad_scores = [(p * (g - inner)).astype(jnp.bfloat16) for p, g in zip(probs, grad_probs)]
        return low, jnp.concatenate(grad_scores)

    def finish(head, low, grad_scores, start):
        queries, keys, values, grads = heads[head]
        tile = slice(start, start + rows)
        result = results[head]
        if start == 0:
            result[0] = dot_tn(values, low).astype(jnp.bfloat16).T
            result[1] = (dot_tn(keys, grad_scores) * SCALE).astype(jnp.bfloat16).T
            result[2] = result[3] = 0.0
        result[2] += dot_nn(grad_scores[:rows], queries[tile])
        result[3] += dot_nn(low[:rows], grads[tile])

    results = [[None] * 4 for _ in heads]
    work = [(head, start) for head in range(len(heads)) for start in range(0, size, rows)]
    ahead = products(*work[0])
    for number, (head, start) in enumerate(work):
        scores, grad_probs = ahead
        if number + 1 < len(work):
            ahead = products(*work[number + 1])
        finish(head, *weigh(scores, grad_probs, start), start)
    for result in results:
        result[2] = (result[2] * SCALE).astype(jnp.bfloat16)
        result[3] = result[3].astype(jnp.bfloat16)
    return results


def attend_kernel(parts, part_rows, steps, width, offsets, has_outs, *refs):
    image_ids, mine, sides = refs[0], refs[1:4], (refs[4:7], refs[7:10])
    refs = refs[10 + (4 if has_outs else 0) :]
    outs, (window, lane_ids, slot_of, table, sems) = refs[:4], refs[4:]
    rows = parts * part_rows
    most = 3 * rows
    last = parts - 1
    me = lax.axis_index("tensor")
    step = pl.program_id(0)

    def copy_of(group, flip, number, place, sem):
        kind = 0 if flip == 0 else 2 if flip == last else 1
        buffer = lax.rem(number, 2)
        start = pl.multiple_of(place * part_rows, part_rows)
        column = pl.multiple_of(number * width + offsets[kind] * HD, HD)
        source = group[kind].at[flip - 1] if kind == 1 else group[kind]
        return pltpu.make_async_copy(
            source.at[:, :, pl.ds(column, width)],
            window.at[buffer, :, pl.ds(start, part_rows), :],
            sems.at[buffer, sem],
        )

    def copies(number, act):
        for flip in range(parts):
            act(copy_of(mine, flip, number, me ^ flip, flip))
        for source in range(2 * parts):
            slot = slot_of[source]

            @pl.when(slot >= 0)
            def _():
                group = sides[source // parts]
                act(copy_of(group, source % parts, number, parts + slot, parts + source))

    @pl.when(step == 0)
    def _():
        count = jnp.int32(0)
        for slot in range(2 * parts):
            table[slot] = -2
        for source in range(2 * parts):
            side, flip = 1 + source // parts, source % parts
            other_id = image_ids[side, me ^ flip]
            shared = other_id == image_ids[0, 0]
            for part in range(1, parts):
                shared = shared | (other_id == image_ids[0, part])
            slot_of[source] = jnp.where(shared, count, -1)
            table[count] = jnp.where(shared, other_id, -2)
            count = count + shared.astype(jnp.int32)
        table[2 * parts] = count
        window[:, :, rows:] = jnp.zeros((2, 4, most - rows, width), window.dtype)
        copies(0, lambda copy: copy.start())
        place = lax.broadcasted_iota(jnp.int32, (8, most), 1)
        ids = jnp.full((8, most), -2, jnp.int32)
        for slot in range(3 * parts):
            slot_id = image_ids[0, slot] if slot < parts else table[slot - parts]
            inside = (place >= slot * part_rows) & (place < (slot + 1) * part_rows)
            ids = jnp.where(inside, slot_id, ids)
        lane_ids[...] = ids

    @pl.when(step + 1 < steps)
    def _():
        copies(step + 1, lambda copy: copy.start())

    copies(step, lambda copy: copy.wait())
    count = table[2 * parts]
    buffer = lax.rem(step, 2)
    for size in range(rows, most + 1, rows):
        slots = (size - rows) // part_rows

        @pl.when((count <= slots) & (count > slots - parts))
        def _():
            slot_ids = [image_ids[0, slot] for slot in range(parts)]
            slot_ids += [table[slot] for slot in range(slots)]
            spans = [slice(start, start + HD) for start in range(0, width, HD)]
            heads = [[window[buffer, i, :size, span] for i in range(4)] for span in spans]
            results = attend_heads(heads, slot_ids, lane_ids[0:1], part_rows, rows)
            for span, result in zip(spans, results):
                for out, part in zip(outs, result):
                    out[:, span] = part


def attend(image_ids, groups, offsets, outs, first_head, heads):
    _, part_rows, total = groups[0][0].shape
    parts = groups[0][1].shape[0] + 2
    rows = parts * part_rows
    width = HD * math.gcd(2, math.gcd(first_head, heads))
    steps = heads * HD // width
    first_block = first_head * HD // width
    out_spec = pl.BlockSpec((rows, width), lambda s: (0, s + first_block))
    has_outs = outs is not None
    pieces = [piece for group in groups for piece in group]
    aliases = {1 + len(pieces) + i: i for i in range(4)} if has_outs else {}
    return pl.pallas_call(
        functools.partial(
            attend_kernel, parts, part_rows, steps, width, offsets, has_outs
        ),
        grid=(steps,),
        out_shape=[jax.ShapeDtypeStruct((rows, total), jnp.bfloat16)] * 4,
        in_specs=[pl.BlockSpec(memory_space=pltpu.SMEM)]
        + [pl.BlockSpec(memory_space=pl.ANY)] * (len(pieces) + (4 if has_outs else 0)),
        out_specs=[out_spec] * 4,
        scratch_shapes=[
            pltpu.VMEM((2, 4, 3 * rows, width), jnp.bfloat16),
            pltpu.VMEM((8, 3 * rows), jnp.int32),
            pltpu.SMEM((2 * parts,), jnp.int32),
            pltpu.SMEM((2 * parts + 1,), jnp.int32),
            pltpu.SemaphoreType.DMA((2, 3 * parts)),
        ],
        input_output_aliases=aliases,
        compiler_params=pltpu.CompilerParams(
            dimension_semantics=("arbitrary",), vmem_limit_bytes=VMEM_LIMIT
        ),
        cost_estimate=pl.CostEstimate(
            flops=heads * ATTEND_FLOPS, bytes_accessed=1, transcendentals=0
        ),
    )(image_ids, *pieces, *(outs or ()))


def between(sent, received):
    flops = FLOPS_PER_BYTE * (2 * sent.size - received.size)
    return pl.CostEstimate(flops=flops, bytes_accessed=1, transcendentals=0)


def shards(queries, key_vectors, value_vectors, grad_output, image_ids):
    arrays = (queries, key_vectors, value_vectors, grad_output)
    parts = lax.axis_size("tensor")
    part_rows = queries.shape[0]
    head_total = queries.shape[1] // HD // parts
    near_ids = nearby_ids(image_ids, parts, part_rows)
    last = parts - 1
    spans = split_counts(head_total, [sum(shares) for shares in GROUPS])
    groups = []
    for (start, count), shares in zip(spans, GROUPS):
        groups.append([(start + first, size) for first, size in split_counts(count, shares)])

    jobs = []
    for span, chunks in zip(spans, groups):
        jobs += [(flip, *span) for flip in range(last - 1, 0, -1)]
        jobs += [(last, *chunk) for chunk in chunks]
    jobs.insert(last - 1, (0, 0, head_total))
    soon, later = jobs[:last], jobs[last:]
    packed = dict(zip(soon, pack(arrays, parts, soon)))
    packed.update(zip(later, pack(arrays, parts, later)))

    steps = []
    for span, chunks in zip(spans, groups):
        steps.append([(flip, *span) for flip in range(1, last)])
        steps += [[(last, *chunk)] for chunk in chunks]

    def cross(step, after, cost=SMALL_COST, late=()):
        held = [hold(packed[job], after, cost) if after else packed[job] for job in step]
        held = [hold(piece, late) if late else piece for piece in held]
        return held, [swap_flipped(piece, "tensor", job[0]) for job, piece in zip(step, held)]

    def spread(piece):
        return piece, swap_pairs(piece, "dp", 0), swap_pairs(piece, "dp", 1)

    _, crossed = cross(steps[0], [])
    sent = [spread(packed[(0, 0, head_total)])]
    outs, joined, number = None, None, 0
    for span, chunks in zip(spans, groups):
        for place in range(1 + len(chunks)):
            after = list(sent[-1][1 : 3 if number + 1 < len(steps) else 2])
            received, held = crossed, []
            number += 1
            if number < len(steps):
                late = sent[-1][1:] if number > 1 and place == 0 else ()
                cost = between(sent[-1][0], received[0]) if late else SMALL_COST
                held, crossed = cross(steps[number], [received[-1]], cost, late)
            elif outs is not None:
                after.append(outs[0])
            cost = between(sent[-1][0], received[0]) if number < len(steps) else SMALL_COST
            held.append(sent[-1][0])
            if place == 0:
                joined = spread(hold(join(received, held, cost), after))
                sent.append(joined)
                continue
            piece = spread(hold(hold(received[0], held, cost), after))
            sent.append(piece)
            first_head, count = chunks[place - 1]
            offsets = (first_head, first_head - span[0], 0)
            outs = attend(
                near_ids, list(zip(sent[0], joined, piece)), offsets, outs, first_head, count
            )
    return tuple(outs)


def solution(mesh):
    return jax.shard_map(
        shards,
        mesh=mesh,
        in_specs=(
            P(("dp", "tensor"), None),
            P(("dp", "tensor"), None),
            P(("dp", "tensor"), None),
            P(("dp", "tensor"), None),
            P(),
        ),
        out_specs=(P("dp", "tensor"), P("dp", "tensor"), P("dp", "tensor"), P("dp", "tensor")),
        check_vma=False,
    )
```

```python
import functools
import math

import jax
import jax.numpy as jnp
from jax import lax
from jax.experimental import pallas as pl
from jax.experimental.pallas import tpu as pltpu
from jax.sharding import PartitionSpec as P

HD = 128
SCALE = 1.0 / math.sqrt(HD)
EXP2_SCALE = SCALE * math.log2(math.e)
MASKED = -1e30
GROUPS = ((6,), (4, 2))
VMEM_LIMIT = 64 * 1024 * 1024 - 256 * 1024
ATTEND_FLOPS = 1_500_000_000
FLOPS_PER_BYTE = 52_000
SMALL_COST = pl.CostEstimate(flops=1, bytes_accessed=1, transcendentals=0)


def split_counts(total, shares):
    whole = sum(shares)
    edges = [round(total * sum(shares[:i]) / whole) for i in range(len(shares) + 1)]
    return [(a, b - a) for a, b in zip(edges[:-1], edges[1:]) if b > a]


def swap_pairs(block, axis, first):
    count = lax.axis_size(axis)
    route = []
    for low in range(first, count - 1, 2):
        route += [(low, low + 1), (low + 1, low)]
    return lax.ppermute(block, axis, route)


def swap_flipped(block, axis, flip):
    return lax.ppermute(block, axis, [(i, i ^ flip) for i in range(lax.axis_size(axis))])


def nearby_ids(image_ids, parts, part_rows):
    shard = lax.axis_index("dp")
    padded = jnp.pad(image_ids[::part_rows], (parts, parts), constant_values=-1)
    odd = lax.rem(shard, 2)

    def ids_of(other):
        return lax.dynamic_slice_in_dim(padded, (other + 1) * parts, parts)

    return jnp.stack((ids_of(shard), ids_of(shard + 1 - 2 * odd), ids_of(shard - 1 + 2 * odd)))


def columns(array, part, stride, first, width):
    start = pl.multiple_of(part * stride + first, HD)
    return array.at[:, pl.ds(start, width)]


def pack_kernel(stride, jobs, *refs):
    arrays, packed, (stage, in_sems, out_sems) = refs[:4], refs[4:-3], refs[-3:]
    me = lax.axis_index("tensor")
    loads, stores = [], []
    for number, (flip, first, count) in enumerate(jobs):
        for index, array in enumerate(arrays):
            load = pltpu.make_async_copy(
                columns(array, me ^ flip, stride, first * HD, count * HD),
                stage.at[flip, index, :, pl.ds(first * HD, count * HD)],
                in_sems.at[number * 4 + index],
            )
            load.start()
            loads.append(load)
    for number, (flip, first, count) in enumerate(jobs):
        for load in loads[number * 4 : number * 4 + 4]:
            load.wait()
        store = pltpu.make_async_copy(
            stage.at[flip, :, :, pl.ds(first * HD, count * HD)],
            packed[number],
            out_sems.at[number],
        )
        store.start()
        stores.append(store)
    for store in stores:
        store.wait()


def pack(arrays, parts, jobs):
    rows, total = arrays[0].shape
    stride = total // parts
    return pl.pallas_call(
        functools.partial(pack_kernel, stride, jobs),
        out_shape=[
            jax.ShapeDtypeStruct((4, rows, count * HD), jnp.bfloat16) for _, _, count in jobs
        ],
        in_specs=[pl.BlockSpec(memory_space=pl.ANY)] * 4,
        out_specs=[pl.BlockSpec(memory_space=pl.ANY)] * len(jobs),
        scratch_shapes=[
            pltpu.VMEM((parts, 4, rows, stride), jnp.bfloat16),
            pltpu.SemaphoreType.DMA((4 * len(jobs),)),
            pltpu.SemaphoreType.DMA((len(jobs),)),
        ],
        compiler_params=pltpu.CompilerParams(vmem_limit_bytes=VMEM_LIMIT),
        cost_estimate=SMALL_COST,
    )(*arrays)


def join_kernel(pieces, *refs):
    received, (joined, stage, in_sems, out_sems) = refs[:pieces], refs[-4:]
    loads, stores = [], []
    for piece in range(pieces):
        load = pltpu.make_async_copy(received[piece], stage.at[piece], in_sems.at[piece])
        load.start()
        loads.append(load)
    for piece in range(pieces):
        loads[piece].wait()
        store = pltpu.make_async_copy(stage.at[piece], joined.at[piece], out_sems.at[piece])
        store.start()
        stores.append(store)
    for store in stores:
        store.wait()


def join(received, after, cost):
    pieces = len(received)
    shape = (pieces,) + received[0].shape
    return pl.pallas_call(
        functools.partial(join_kernel, pieces),
        out_shape=jax.ShapeDtypeStruct(shape, jnp.bfloat16),
        in_specs=[pl.BlockSpec(memory_space=pl.ANY)] * (pieces + len(after)),
        out_specs=pl.BlockSpec(memory_space=pl.ANY),
        scratch_shapes=[
            pltpu.VMEM(shape, jnp.bfloat16),
            pltpu.SemaphoreType.DMA((pieces,)),
            pltpu.SemaphoreType.DMA((pieces,)),
        ],
        compiler_params=pltpu.CompilerParams(vmem_limit_bytes=VMEM_LIMIT),
        cost_estimate=cost,
    )(*received, *after)


def hold(array, after, cost=SMALL_COST):
    return pl.pallas_call(
        lambda *refs: None,
        out_shape=jax.ShapeDtypeStruct(array.shape, array.dtype),
        in_specs=[pl.BlockSpec(memory_space=pl.ANY)] * (1 + len(after)),
        out_specs=pl.BlockSpec(memory_space=pl.ANY),
        input_output_aliases={0: 0},
        compiler_params=pltpu.CompilerParams(vmem_limit_bytes=VMEM_LIMIT),
        cost_estimate=cost,
    )(array, *after)


def dot_nt(a, b):
    return lax.dot_general(a, b, (((1,), (1,)), ((), ())), preferred_element_type=jnp.float32)


def dot_tn(a, b):
    return lax.dot_general(a, b, (((0,), (0,)), ((), ())), preferred_element_type=jnp.float32)


def dot_nn(a, b):
    return jnp.dot(a, b, preferred_element_type=jnp.float32)


def attend_heads(heads, slot_ids, lane_ids, part_rows, rows):
    size = heads[0][0].shape[0]
    slots = size // part_rows

    def per_slot(array):
        return [array[slot * part_rows : (slot + 1) * part_rows] for slot in range(slots)]

    def over_slots(reduce, combine, arrays):
        total = reduce(arrays[0], axis=0, keepdims=True)
        for array in arrays[1:]:
            total = combine(total, reduce(array, axis=0, keepdims=True))
        return total

    def products(head, start):
        queries, keys, values, grads = heads[head]
        tile = slice(start, start + rows)
        return dot_nt(keys, queries[tile]), dot_nt(values, grads[tile])

    def weigh(scores, grad_probs, start):
        lanes = lane_ids[:, start : start + rows]
        scores = [
            part + jnp.where(lanes == slot_id, 0.0, MASKED)
            for part, slot_id in zip(per_slot(scores), slot_ids)
        ]
        row_max = over_slots(jnp.max, jnp.maximum, scores)
        weights = [jnp.exp2((part - row_max) * EXP2_SCALE) for part in scores]
        inverse = 1.0 / over_slots(jnp.sum, jnp.add, weights)
        probs = [part * inverse for part in weights]
        grad_probs = per_slot(grad_probs)
        inner = over_slots(jnp.sum, jnp.add, [p * g for p, g in zip(probs, grad_probs)])
        low = jnp.concatenate([p.astype(jnp.bfloat16) for p in probs])
        grad_scores = [(p * (g - inner)).astype(jnp.bfloat16) for p, g in zip(probs, grad_probs)]
        return low, jnp.concatenate(grad_scores)

    def finish(head, low, grad_scores, start):
        queries, keys, values, grads = heads[head]
        tile = slice(start, start + rows)
        result = results[head]
        if start == 0:
            result[0] = dot_tn(values, low).astype(jnp.bfloat16).T
            result[1] = (dot_tn(keys, grad_scores) * SCALE).astype(jnp.bfloat16).T
            result[2] = result[3] = 0.0
        result[2] += dot_nn(grad_scores[:rows], queries[tile])
        result[3] += dot_nn(low[:rows], grads[tile])

    results = [[None] * 4 for _ in heads]
    work = [(head, start) for head in range(len(heads)) for start in range(0, size, rows)]
    ahead = products(*work[0])
    for number, (head, start) in enumerate(work):
        scores, grad_probs = ahead
        if number + 1 < len(work):
            ahead = products(*work[number + 1])
        finish(head, *weigh(scores, grad_probs, start), start)
    for result in results:
        result[2] = (result[2] * SCALE).astype(jnp.bfloat16)
        result[3] = result[3].astype(jnp.bfloat16)
    return results


def attend_kernel(parts, part_rows, steps, width, offsets, has_outs, *refs):
    image_ids, mine, sides = refs[0], refs[1:4], (refs[4:7], refs[7:10])
    refs = refs[10 + (4 if has_outs else 0) :]
    outs, (window, lane_ids, slot_of, table, sems) = refs[:4], refs[4:]
    rows = parts * part_rows
    most = 3 * rows
    last = parts - 1
    me = lax.axis_index("tensor")
    step = pl.program_id(0)

    def copy_of(group, flip, number, place, sem):
        kind = 0 if flip == 0 else 2 if flip == last else 1
        buffer = lax.rem(number, 2)
        start = pl.multiple_of(place * part_rows, part_rows)
        column = pl.multiple_of(number * width + offsets[kind] * HD, HD)
        source = group[kind].at[flip - 1] if kind == 1 else group[kind]
        return pltpu.make_async_copy(
            source.at[:, :, pl.ds(column, width)],
            window.at[buffer, :, pl.ds(start, part_rows), :],
            sems.at[buffer, sem],
        )

    def copies(number, act):
        for flip in range(parts):
            act(copy_of(mine, flip, number, me ^ flip, flip))
        for source in range(2 * parts):
            slot = slot_of[source]

            @pl.when(slot >= 0)
            def _():
                group = sides[source // parts]
                act(copy_of(group, source % parts, number, parts + slot, parts + source))

    @pl.when(step == 0)
    def _():
        count = jnp.int32(0)
        for slot in range(2 * parts):
            table[slot] = -2
        for source in range(2 * parts):
            side, flip = 1 + source // parts, source % parts
            other_id = image_ids[side, me ^ flip]
            shared = other_id == image_ids[0, 0]
            for part in range(1, parts):
                shared = shared | (other_id == image_ids[0, part])
            slot_of[source] = jnp.where(shared, count, -1)
            table[count] = jnp.where(shared, other_id, -2)
            count = count + shared.astype(jnp.int32)
        table[2 * parts] = count
        window[:, :, rows:] = jnp.zeros((2, 4, most - rows, width), window.dtype)
        copies(0, lambda copy: copy.start())
        place = lax.broadcasted_iota(jnp.int32, (8, most), 1)
        ids = jnp.full((8, most), -2, jnp.int32)
        for slot in range(3 * parts):
            slot_id = image_ids[0, slot] if slot < parts else table[slot - parts]
            inside = (place >= slot * part_rows) & (place < (slot + 1) * part_rows)
            ids = jnp.where(inside, slot_id, ids)
        lane_ids[...] = ids

    @pl.when(step + 1 < steps)
    def _():
        copies(step + 1, lambda copy: copy.start())

    copies(step, lambda copy: copy.wait())
    count = table[2 * parts]
    buffer = lax.rem(step, 2)
    for size in range(rows, most + 1, rows):
        slots = (size - rows) // part_rows

        @pl.when((count <= slots) & (count > slots - parts))
        def _():
            slot_ids = [image_ids[0, slot] for slot in range(parts)]
            slot_ids += [table[slot] for slot in range(slots)]
            spans = [slice(start, start + HD) for start in range(0, width, HD)]
            heads = [[window[buffer, i, :size, span] for i in range(4)] for span in spans]
            results = attend_heads(heads, slot_ids, lane_ids[0:1], part_rows, rows)
            for span, result in zip(spans, results):
                for out, part in zip(outs, result):
                    out[:, span] = part


def attend(image_ids, groups, offsets, outs, first_head, heads):
    _, part_rows, total = groups[0][0].shape
    parts = groups[0][1].shape[0] + 2
    rows = parts * part_rows
    width = HD * math.gcd(2, math.gcd(first_head, heads))
    steps = heads * HD // width
    first_block = first_head * HD // width
    out_spec = pl.BlockSpec((rows, width), lambda s: (0, s + first_block))
    has_outs = outs is not None
    pieces = [piece for group in groups for piece in group]
    aliases = {1 + len(pieces) + i: i for i in range(4)} if has_outs else {}
    return pl.pallas_call(
        functools.partial(
            attend_kernel, parts, part_rows, steps, width, offsets, has_outs
        ),
        grid=(steps,),
        out_shape=[jax.ShapeDtypeStruct((rows, total), jnp.bfloat16)] * 4,
        in_specs=[pl.BlockSpec(memory_space=pltpu.SMEM)]
        + [pl.BlockSpec(memory_space=pl.ANY)] * (len(pieces) + (4 if has_outs else 0)),
        out_specs=[out_spec] * 4,
        scratch_shapes=[
            pltpu.VMEM((2, 4, 3 * rows, width), jnp.bfloat16),
            pltpu.VMEM((8, 3 * rows), jnp.int32),
            pltpu.SMEM((2 * parts,), jnp.int32),
            pltpu.SMEM((2 * parts + 1,), jnp.int32),
            pltpu.SemaphoreType.DMA((2, 3 * parts)),
        ],
        input_output_aliases=aliases,
        compiler_params=pltpu.CompilerParams(
            dimension_semantics=("arbitrary",), vmem_limit_bytes=VMEM_LIMIT
        ),
        cost_estimate=pl.CostEstimate(
            flops=heads * ATTEND_FLOPS, bytes_accessed=1, transcendentals=0
        ),
    )(image_ids, *pieces, *(outs or ()))


def between(sent, received):
    flops = FLOPS_PER_BYTE * (2 * sent.size - received.size)
    return pl.CostEstimate(flops=flops, bytes_accessed=1, transcendentals=0)


def shards(queries, key_vectors, value_vectors, grad_output, image_ids):
    arrays = (queries, key_vectors, value_vectors, grad_output)
    parts = lax.axis_size("tensor")
    part_rows = queries.shape[0]
    head_total = queries.shape[1] // HD // parts
    near_ids = nearby_ids(image_ids, parts, part_rows)
    last = parts - 1
    spans = split_counts(head_total, [sum(shares) for shares in GROUPS])
    groups = []
    for (start, count), shares in zip(spans, GROUPS):
        groups.append([(start + first, size) for first, size in split_counts(count, shares)])

    jobs = []
    for span, chunks in zip(spans, groups):
        jobs += [(flip, *span) for flip in range(last - 1, 0, -1)]
        jobs += [(last, *chunk) for chunk in chunks]
    jobs.insert(last - 1, (0, 0, head_total))
    soon, later = jobs[:last], jobs[last:]
    packed = dict(zip(soon, pack(arrays, parts, soon)))
    packed.update(zip(later, pack(arrays, parts, later)))

    steps = []
    for span, chunks in zip(spans, groups):
        steps.append([(flip, *span) for flip in range(1, last)])
        steps += [[(last, *chunk)] for chunk in chunks]

    def cross(step, after, cost=SMALL_COST, late=()):
        held = [hold(packed[job], after, cost) if after else packed[job] for job in step]
        held = [hold(piece, late) if late else piece for piece in held]
        return held, [swap_flipped(piece, "tensor", job[0]) for job, piece in zip(step, held)]

    def spread(piece):
        return piece, swap_pairs(piece, "dp", 0), swap_pairs(piece, "dp", 1)

    _, crossed = cross(steps[0], [])
    sent = [spread(packed[(0, 0, head_total)])]
    outs, joined, number = None, None, 0
    for span, chunks in zip(spans, groups):
        for place in range(1 + len(chunks)):
            final = place >= 1 and span is spans[-1]
            after = list(sent[-1][1 : 2 if final else 3])
            received, held = crossed, []
            number += 1
            if number < len(steps):
                late = sent[-1][1:] if number > 1 and place == 0 else ()
                cost = between(sent[-1][0], received[0]) if late else SMALL_COST
                held, crossed = cross(steps[number], [received[-1]], cost, late)
            if final and place == 1 and outs is not None:
                after.append(outs[0])
            cost = SMALL_COST if final else between(sent[-1][0], received[0])
            held.append(sent[-1][0])
            if place == 0:
                joined = spread(hold(join(received, held, cost), after))
                sent.append(joined)
                continue
            piece = spread(hold(hold(received[0], held, cost), after))
            sent.append(piece)
            first_head, count = chunks[place - 1]
            offsets = (first_head, first_head - span[0], 0)
            outs = attend(
                near_ids, list(zip(sent[0], joined, piece)), offsets, outs, first_head, count
            )
    return tuple(outs)


def solution(mesh):
    return jax.shard_map(
        shards,
        mesh=mesh,
        in_specs=(
            P(("dp", "tensor"), None),
            P(("dp", "tensor"), None),
            P(("dp", "tensor"), None),
            P(("dp", "tensor"), None),
            P(),
        ),
        out_specs=(P("dp", "tensor"), P("dp", "tensor"), P("dp", "tensor"), P("dp", "tensor")),
        check_vma=False,
    )
```

```python
import functools
import math

import jax
import jax.numpy as jnp
from jax import lax
from jax.experimental import pallas as pl
from jax.experimental.pallas import tpu as pltpu
from jax.sharding import PartitionSpec as P

HD = 128
SCALE = 1.0 / math.sqrt(HD)
EXP2_SCALE = SCALE * math.log2(math.e)
MASKED = -1e30
GROUPS = ((6,), (6,))
VMEM_LIMIT = 64 * 1024 * 1024 - 256 * 1024
ATTEND_FLOPS = 1_500_000_000
FLOPS_PER_BYTE = 52_000
SMALL_COST = pl.CostEstimate(flops=1, bytes_accessed=1, transcendentals=0)


def split_counts(total, shares):
    whole = sum(shares)
    edges = [round(total * sum(shares[:i]) / whole) for i in range(len(shares) + 1)]
    return [(a, b - a) for a, b in zip(edges[:-1], edges[1:]) if b > a]


def swap_pairs(block, axis, first):
    count = lax.axis_size(axis)
    route = []
    for low in range(first, count - 1, 2):
        route += [(low, low + 1), (low + 1, low)]
    return lax.ppermute(block, axis, route)


def swap_flipped(block, axis, flip):
    return lax.ppermute(block, axis, [(i, i ^ flip) for i in range(lax.axis_size(axis))])


def nearby_ids(image_ids, parts, part_rows):
    shard = lax.axis_index("dp")
    padded = jnp.pad(image_ids[::part_rows], (parts, parts), constant_values=-1)
    odd = lax.rem(shard, 2)

    def ids_of(other):
        return lax.dynamic_slice_in_dim(padded, (other + 1) * parts, parts)

    return jnp.stack((ids_of(shard), ids_of(shard + 1 - 2 * odd), ids_of(shard - 1 + 2 * odd)))


def columns(array, part, stride, first, width):
    start = pl.multiple_of(part * stride + first, HD)
    return array.at[:, pl.ds(start, width)]


def pack_kernel(stride, jobs, *refs):
    arrays, packed, (stage, in_sems, out_sems) = refs[:4], refs[4:-3], refs[-3:]
    me = lax.axis_index("tensor")
    loads, stores = [], []
    for number, (flip, first, count) in enumerate(jobs):
        for index, array in enumerate(arrays):
            load = pltpu.make_async_copy(
                columns(array, me ^ flip, stride, first * HD, count * HD),
                stage.at[flip, index, :, pl.ds(first * HD, count * HD)],
                in_sems.at[number * 4 + index],
            )
            load.start()
            loads.append(load)
    for number, (flip, first, count) in enumerate(jobs):
        for load in loads[number * 4 : number * 4 + 4]:
            load.wait()
        store = pltpu.make_async_copy(
            stage.at[flip, :, :, pl.ds(first * HD, count * HD)],
            packed[number],
            out_sems.at[number],
        )
        store.start()
        stores.append(store)
    for store in stores:
        store.wait()


def pack(arrays, parts, jobs):
    rows, total = arrays[0].shape
    stride = total // parts
    return pl.pallas_call(
        functools.partial(pack_kernel, stride, jobs),
        out_shape=[
            jax.ShapeDtypeStruct((4, rows, count * HD), jnp.bfloat16) for _, _, count in jobs
        ],
        in_specs=[pl.BlockSpec(memory_space=pl.ANY)] * 4,
        out_specs=[pl.BlockSpec(memory_space=pl.ANY)] * len(jobs),
        scratch_shapes=[
            pltpu.VMEM((parts, 4, rows, stride), jnp.bfloat16),
            pltpu.SemaphoreType.DMA((4 * len(jobs),)),
            pltpu.SemaphoreType.DMA((len(jobs),)),
        ],
        compiler_params=pltpu.CompilerParams(vmem_limit_bytes=VMEM_LIMIT),
        cost_estimate=SMALL_COST,
    )(*arrays)


def join_kernel(pieces, *refs):
    received, (joined, stage, in_sems, out_sems) = refs[:pieces], refs[-4:]
    loads, stores = [], []
    for piece in range(pieces):
        load = pltpu.make_async_copy(received[piece], stage.at[piece], in_sems.at[piece])
        load.start()
        loads.append(load)
    for piece in range(pieces):
        loads[piece].wait()
        store = pltpu.make_async_copy(stage.at[piece], joined.at[piece], out_sems.at[piece])
        store.start()
        stores.append(store)
    for store in stores:
        store.wait()


def join(received, after, cost):
    pieces = len(received)
    shape = (pieces,) + received[0].shape
    return pl.pallas_call(
        functools.partial(join_kernel, pieces),
        out_shape=jax.ShapeDtypeStruct(shape, jnp.bfloat16),
        in_specs=[pl.BlockSpec(memory_space=pl.ANY)] * (pieces + len(after)),
        out_specs=pl.BlockSpec(memory_space=pl.ANY),
        scratch_shapes=[
            pltpu.VMEM(shape, jnp.bfloat16),
            pltpu.SemaphoreType.DMA((pieces,)),
            pltpu.SemaphoreType.DMA((pieces,)),
        ],
        compiler_params=pltpu.CompilerParams(vmem_limit_bytes=VMEM_LIMIT),
        cost_estimate=cost,
    )(*received, *after)


def hold(array, after, cost=SMALL_COST):
    return pl.pallas_call(
        lambda *refs: None,
        out_shape=jax.ShapeDtypeStruct(array.shape, array.dtype),
        in_specs=[pl.BlockSpec(memory_space=pl.ANY)] * (1 + len(after)),
        out_specs=pl.BlockSpec(memory_space=pl.ANY),
        input_output_aliases={0: 0},
        compiler_params=pltpu.CompilerParams(vmem_limit_bytes=VMEM_LIMIT),
        cost_estimate=cost,
    )(array, *after)


def dot_nt(a, b):
    return lax.dot_general(a, b, (((1,), (1,)), ((), ())), preferred_element_type=jnp.float32)


def dot_tn(a, b):
    return lax.dot_general(a, b, (((0,), (0,)), ((), ())), preferred_element_type=jnp.float32)


def dot_nn(a, b):
    return jnp.dot(a, b, preferred_element_type=jnp.float32)


def attend_heads(heads, slot_ids, lane_ids, part_rows, rows):
    size = heads[0][0].shape[0]
    slots = size // part_rows

    def per_slot(array):
        return [array[slot * part_rows : (slot + 1) * part_rows] for slot in range(slots)]

    def over_slots(reduce, combine, arrays):
        total = reduce(arrays[0], axis=0, keepdims=True)
        for array in arrays[1:]:
            total = combine(total, reduce(array, axis=0, keepdims=True))
        return total

    def products(head, start):
        queries, keys, values, grads = heads[head]
        tile = slice(start, start + rows)
        return dot_nt(keys, queries[tile]), dot_nt(values, grads[tile])

    def weigh(scores, grad_probs, start):
        lanes = lane_ids[:, start : start + rows]
        scores = [
            part + jnp.where(lanes == slot_id, 0.0, MASKED)
            for part, slot_id in zip(per_slot(scores), slot_ids)
        ]
        row_max = over_slots(jnp.max, jnp.maximum, scores)
        weights = [jnp.exp2((part - row_max) * EXP2_SCALE) for part in scores]
        inverse = 1.0 / over_slots(jnp.sum, jnp.add, weights)
        probs = [part * inverse for part in weights]
        grad_probs = per_slot(grad_probs)
        inner = over_slots(jnp.sum, jnp.add, [p * g for p, g in zip(probs, grad_probs)])
        low = jnp.concatenate([p.astype(jnp.bfloat16) for p in probs])
        grad_scores = [(p * (g - inner)).astype(jnp.bfloat16) for p, g in zip(probs, grad_probs)]
        return low, jnp.concatenate(grad_scores)

    def finish(head, low, grad_scores, start):
        queries, keys, values, grads = heads[head]
        tile = slice(start, start + rows)
        result = results[head]
        if start == 0:
            result[0] = dot_tn(values, low).astype(jnp.bfloat16).T
            result[1] = (dot_tn(keys, grad_scores) * SCALE).astype(jnp.bfloat16).T
            result[2] = result[3] = 0.0
        result[2] += dot_nn(grad_scores[:rows], queries[tile])
        result[3] += dot_nn(low[:rows], grads[tile])

    results = [[None] * 4 for _ in heads]
    work = [(head, start) for head in range(len(heads)) for start in range(0, size, rows)]
    ahead, behind = products(*work[0]), None
    for number, (head, start) in enumerate(work):
        scores, grad_probs = ahead
        if number + 1 < len(work):
            ahead = products(*work[number + 1])
        if behind is not None:
            finish(*behind)
        behind = (head, *weigh(scores, grad_probs, start), start)
    finish(*behind)
    for result in results:
        result[2] = (result[2] * SCALE).astype(jnp.bfloat16)
        result[3] = result[3].astype(jnp.bfloat16)
    return results


def attend_kernel(parts, part_rows, steps, width, offsets, has_outs, *refs):
    image_ids, mine, sides = refs[0], refs[1:4], (refs[4:7], refs[7:10])
    refs = refs[10 + (4 if has_outs else 0) :]
    outs, (window, lane_ids, slot_of, table, sems) = refs[:4], refs[4:]
    rows = parts * part_rows
    most = 3 * rows
    last = parts - 1
    me = lax.axis_index("tensor")
    step = pl.program_id(0)

    def copy_of(group, flip, number, place, sem):
        kind = 0 if flip == 0 else 2 if flip == last else 1
        buffer = lax.rem(number, 2)
        start = pl.multiple_of(place * part_rows, part_rows)
        column = pl.multiple_of(number * width + offsets[kind] * HD, HD)
        source = group[kind].at[flip - 1] if kind == 1 else group[kind]
        return pltpu.make_async_copy(
            source.at[:, :, pl.ds(column, width)],
            window.at[buffer, :, pl.ds(start, part_rows), :],
            sems.at[buffer, sem],
        )

    def own_copies(number, act):
        for flip in range(parts):
            act(copy_of(mine, flip, number, me ^ flip, flip))

    def other_copies(number, act):
        for source in range(2 * parts):
            slot = slot_of[source]

            @pl.when(slot >= 0)
            def _():
                group = sides[source // parts]
                act(copy_of(group, source % parts, number, parts + slot, parts + source))

    @pl.when(step == 0)
    def _():
        own_copies(0, lambda copy: copy.start())
        count = jnp.int32(0)
        for slot in range(2 * parts):
            table[slot] = -2
        for source in range(2 * parts):
            side, flip = 1 + source // parts, source % parts
            other_id = image_ids[side, me ^ flip]
            shared = other_id == image_ids[0, 0]
            for part in range(1, parts):
                shared = shared | (other_id == image_ids[0, part])
            slot_of[source] = jnp.where(shared, count, -1)
            table[count] = jnp.where(shared, other_id, -2)
            count = count + shared.astype(jnp.int32)
        table[2 * parts] = count
        other_copies(0, lambda copy: copy.start())
        for slot in range(2 * parts):

            @pl.when((slot >= count) & (slot < (count + parts - 1) // parts * parts))
            def _():
                place = slice(rows + slot * part_rows, rows + (slot + 1) * part_rows)
                window[:, :, place] = jnp.zeros((2, 4, part_rows, width), window.dtype)

        place = lax.broadcasted_iota(jnp.int32, (8, most), 1)
        ids = jnp.full((8, most), -2, jnp.int32)
        for slot in range(3 * parts):
            slot_id = image_ids[0, slot] if slot < parts else table[slot - parts]
            inside = (place >= slot * part_rows) & (place < (slot + 1) * part_rows)
            ids = jnp.where(inside, slot_id, ids)
        lane_ids[...] = ids

    @pl.when(step + 1 < steps)
    def _():
        own_copies(step + 1, lambda copy: copy.start())
        other_copies(step + 1, lambda copy: copy.start())

    own_copies(step, lambda copy: copy.wait())
    other_copies(step, lambda copy: copy.wait())
    count = table[2 * parts]
    buffer = lax.rem(step, 2)
    for size in range(rows, most + 1, rows):
        slots = (size - rows) // part_rows

        @pl.when((count <= slots) & (count > slots - parts))
        def _():
            slot_ids = [image_ids[0, slot] for slot in range(parts)]
            slot_ids += [table[slot] for slot in range(slots)]
            spans = [slice(start, start + HD) for start in range(0, width, HD)]
            heads = [[window[buffer, i, :size, span] for i in range(4)] for span in spans]
            results = attend_heads(heads, slot_ids, lane_ids[0:1], part_rows, rows)
            for span, result in zip(spans, results):
                for out, part in zip(outs, result):
                    out[:, span] = part


def attend(image_ids, groups, offsets, outs, first_head, heads):
    _, part_rows, total = groups[0][0].shape
    parts = groups[0][1].shape[0] + 2
    rows = parts * part_rows
    width = HD * math.gcd(2, math.gcd(first_head, heads))
    steps = heads * HD // width
    first_block = first_head * HD // width
    out_spec = pl.BlockSpec((rows, width), lambda s: (0, s + first_block))
    has_outs = outs is not None
    pieces = [piece for group in groups for piece in group]
    aliases = {1 + len(pieces) + i: i for i in range(4)} if has_outs else {}
    return pl.pallas_call(
        functools.partial(
            attend_kernel, parts, part_rows, steps, width, offsets, has_outs
        ),
        grid=(steps,),
        out_shape=[jax.ShapeDtypeStruct((rows, total), jnp.bfloat16)] * 4,
        in_specs=[pl.BlockSpec(memory_space=pltpu.SMEM)]
        + [pl.BlockSpec(memory_space=pl.ANY)] * (len(pieces) + (4 if has_outs else 0)),
        out_specs=[out_spec] * 4,
        scratch_shapes=[
            pltpu.VMEM((2, 4, 3 * rows, width), jnp.bfloat16),
            pltpu.VMEM((8, 3 * rows), jnp.int32),
            pltpu.SMEM((2 * parts,), jnp.int32),
            pltpu.SMEM((2 * parts + 1,), jnp.int32),
            pltpu.SemaphoreType.DMA((2, 3 * parts)),
        ],
        input_output_aliases=aliases,
        compiler_params=pltpu.CompilerParams(
            dimension_semantics=("arbitrary",), vmem_limit_bytes=VMEM_LIMIT
        ),
        cost_estimate=pl.CostEstimate(
            flops=heads * ATTEND_FLOPS, bytes_accessed=1, transcendentals=0
        ),
    )(image_ids, *pieces, *(outs or ()))


def between(sent, received):
    flops = FLOPS_PER_BYTE * (2 * sent.size - received.size)
    return pl.CostEstimate(flops=flops, bytes_accessed=1, transcendentals=0)


def shards(queries, key_vectors, value_vectors, grad_output, image_ids):
    arrays = (queries, key_vectors, value_vectors, grad_output)
    parts = lax.axis_size("tensor")
    part_rows = queries.shape[0]
    head_total = queries.shape[1] // HD // parts
    near_ids = nearby_ids(image_ids, parts, part_rows)
    last = parts - 1
    spans = split_counts(head_total, [sum(shares) for shares in GROUPS])
    groups = []
    for (start, count), shares in zip(spans, GROUPS):
        groups.append([(start + first, size) for first, size in split_counts(count, shares)])

    jobs = []
    for span, chunks in zip(spans, groups):
        jobs += [(flip, *span) for flip in range(last - 1, 0, -1)]
        jobs += [(last, *chunk) for chunk in chunks]
    jobs.insert(last - 1, (0, 0, head_total))
    soon, later = jobs[:last], jobs[last:]
    packed = dict(zip(soon, pack(arrays, parts, soon)))
    packed.update(zip(later, pack(arrays, parts, later)))

    steps = []
    for span, chunks in zip(spans, groups):
        steps.append([(flip, *span) for flip in range(1, last)])
        steps += [[(last, *chunk)] for chunk in chunks]

    def cross(step, after, cost=SMALL_COST, late=()):
        held = [hold(packed[job], after, cost) if after else packed[job] for job in step]
        held = [hold(piece, late) if late else piece for piece in held]
        return held, [swap_flipped(piece, "tensor", job[0]) for job, piece in zip(step, held)]

    def spread(piece):
        return piece, swap_pairs(piece, "dp", 0), swap_pairs(piece, "dp", 1)

    _, crossed = cross(steps[0], [])
    sent = [spread(packed[(0, 0, head_total)])]
    outs, joined, number = None, None, 0
    for span, chunks in zip(spans, groups):
        for place in range(1 + len(chunks)):
            after = list(sent[-1][1 : 3 if number + 1 < len(steps) else 2])
            received, held = crossed, []
            number += 1
            if number < len(steps):
                late = sent[-1][1:] if number > 1 and place == 0 else ()
                cost = between(sent[-1][0], received[0]) if late else SMALL_COST
                held, crossed = cross(steps[number], [received[-1]], cost, late)
            elif outs is not None:
                after.append(outs[0])
            cost = between(sent[-1][0], received[0]) if number < len(steps) else SMALL_COST
            held.append(sent[-1][0])
            if place == 0:
                joined = spread(hold(join(received, held, cost), after))
                sent.append(joined)
                continue
            piece = spread(hold(hold(received[0], held, cost), after))
            sent.append(piece)
            first_head, count = chunks[place - 1]
            offsets = (first_head, first_head - span[0], 0)
            outs = attend(
                near_ids, list(zip(sent[0], joined, piece)), offsets, outs, first_head, count
            )
    return tuple(outs)


def solution(mesh):
    return jax.shard_map(
        shards,
        mesh=mesh,
        in_specs=(
            P(("dp", "tensor"), None),
            P(("dp", "tensor"), None),
            P(("dp", "tensor"), None),
            P(("dp", "tensor"), None),
            P(),
        ),
        out_specs=(P("dp", "tensor"), P("dp", "tensor"), P("dp", "tensor"), P("dp", "tensor")),
        check_vma=False,
    )
```

```python
import functools
import math

import jax
import jax.numpy as jnp
from jax import lax
from jax.experimental import pallas as pl
from jax.experimental.pallas import tpu as pltpu
from jax.sharding import PartitionSpec as P

HD = 128
SCALE = 1.0 / math.sqrt(HD)
EXP2_SCALE = SCALE * math.log2(math.e)
MASKED = -1e30
GROUPS = ((6,), (6,))
VMEM_LIMIT = 64 * 1024 * 1024 - 256 * 1024
ATTEND_FLOPS = 1_500_000_000
FLOPS_PER_BYTE = 52_000
SMALL_COST = pl.CostEstimate(flops=1, bytes_accessed=1, transcendentals=0)


def split_counts(total, shares):
    whole = sum(shares)
    edges = [round(total * sum(shares[:i]) / whole) for i in range(len(shares) + 1)]
    return [(a, b - a) for a, b in zip(edges[:-1], edges[1:]) if b > a]


def swap_pairs(block, axis, first):
    count = lax.axis_size(axis)
    route = []
    for low in range(first, count - 1, 2):
        route += [(low, low + 1), (low + 1, low)]
    return lax.ppermute(block, axis, route)


def swap_flipped(block, axis, flip):
    return lax.ppermute(block, axis, [(i, i ^ flip) for i in range(lax.axis_size(axis))])


def nearby_ids(image_ids, parts, part_rows):
    shard = lax.axis_index("dp")
    padded = jnp.pad(image_ids[::part_rows], (parts, parts), constant_values=-1)
    odd = lax.rem(shard, 2)

    def ids_of(other):
        return lax.dynamic_slice_in_dim(padded, (other + 1) * parts, parts)

    return jnp.stack((ids_of(shard), ids_of(shard + 1 - 2 * odd), ids_of(shard - 1 + 2 * odd)))


def columns(array, part, stride, first, width):
    start = pl.multiple_of(part * stride + first, HD)
    return array.at[:, pl.ds(start, width)]


def pack_kernel(stride, jobs, *refs):
    arrays, packed, (stage, in_sems, out_sems) = refs[:4], refs[4:-3], refs[-3:]
    me = lax.axis_index("tensor")
    loads, stores = [], []
    for number, (flip, first, count) in enumerate(jobs):
        for index, array in enumerate(arrays):
            load = pltpu.make_async_copy(
                columns(array, me ^ flip, stride, first * HD, count * HD),
                stage.at[flip, index, :, pl.ds(first * HD, count * HD)],
                in_sems.at[number * 4 + index],
            )
            load.start()
            loads.append(load)
    for number, (flip, first, count) in enumerate(jobs):
        for load in loads[number * 4 : number * 4 + 4]:
            load.wait()
        store = pltpu.make_async_copy(
            stage.at[flip, :, :, pl.ds(first * HD, count * HD)],
            packed[number],
            out_sems.at[number],
        )
        store.start()
        stores.append(store)
    for store in stores:
        store.wait()


def pack(arrays, parts, jobs):
    rows, total = arrays[0].shape
    stride = total // parts
    return pl.pallas_call(
        functools.partial(pack_kernel, stride, jobs),
        out_shape=[
            jax.ShapeDtypeStruct((4, rows, count * HD), jnp.bfloat16) for _, _, count in jobs
        ],
        in_specs=[pl.BlockSpec(memory_space=pl.ANY)] * 4,
        out_specs=[pl.BlockSpec(memory_space=pl.ANY)] * len(jobs),
        scratch_shapes=[
            pltpu.VMEM((parts, 4, rows, stride), jnp.bfloat16),
            pltpu.SemaphoreType.DMA((4 * len(jobs),)),
            pltpu.SemaphoreType.DMA((len(jobs),)),
        ],
        compiler_params=pltpu.CompilerParams(vmem_limit_bytes=VMEM_LIMIT),
        cost_estimate=SMALL_COST,
    )(*arrays)


def join_kernel(pieces, *refs):
    received, (joined, stage, in_sems, out_sems) = refs[:pieces], refs[-4:]
    places = [(piece, index) for piece in range(pieces) for index in range(4)]
    loads, stores = [], []
    for piece, index in places:
        load = pltpu.make_async_copy(
            received[piece].at[index], stage.at[piece, index], in_sems.at[piece * 4 + index]
        )
        load.start()
        loads.append(load)
    for load, (piece, index) in zip(loads, places):
        load.wait()
        store = pltpu.make_async_copy(
            stage.at[piece, index], joined.at[piece, index], out_sems.at[piece * 4 + index]
        )
        store.start()
        stores.append(store)
    for store in stores:
        store.wait()


def join(received, after, cost):
    pieces = len(received)
    shape = (pieces,) + received[0].shape
    return pl.pallas_call(
        functools.partial(join_kernel, pieces),
        out_shape=jax.ShapeDtypeStruct(shape, jnp.bfloat16),
        in_specs=[pl.BlockSpec(memory_space=pl.ANY)] * (pieces + len(after)),
        out_specs=pl.BlockSpec(memory_space=pl.ANY),
        scratch_shapes=[
            pltpu.VMEM(shape, jnp.bfloat16),
            pltpu.SemaphoreType.DMA((pieces * 4,)),
            pltpu.SemaphoreType.DMA((pieces * 4,)),
        ],
        compiler_params=pltpu.CompilerParams(vmem_limit_bytes=VMEM_LIMIT),
        cost_estimate=cost,
    )(*received, *after)


def hold(array, after, cost=SMALL_COST):
    return pl.pallas_call(
        lambda *refs: None,
        out_shape=jax.ShapeDtypeStruct(array.shape, array.dtype),
        in_specs=[pl.BlockSpec(memory_space=pl.ANY)] * (1 + len(after)),
        out_specs=pl.BlockSpec(memory_space=pl.ANY),
        input_output_aliases={0: 0},
        compiler_params=pltpu.CompilerParams(vmem_limit_bytes=VMEM_LIMIT),
        cost_estimate=cost,
    )(array, *after)


def dot_nt(a, b):
    return lax.dot_general(a, b, (((1,), (1,)), ((), ())), preferred_element_type=jnp.float32)


def dot_tn(a, b):
    return lax.dot_general(a, b, (((0,), (0,)), ((), ())), preferred_element_type=jnp.float32)


def dot_nn(a, b):
    return jnp.dot(a, b, preferred_element_type=jnp.float32)


def attend_heads(heads, slot_ids, lane_ids, part_rows, rows):
    size = heads[0][0].shape[0]
    slots = size // part_rows

    def per_slot(array):
        return [array[slot * part_rows : (slot + 1) * part_rows] for slot in range(slots)]

    def over_slots(reduce, combine, arrays):
        total = reduce(arrays[0], axis=0, keepdims=True)
        for array in arrays[1:]:
            total = combine(total, reduce(array, axis=0, keepdims=True))
        return total

    def products(head, start):
        queries, keys, values, grads = heads[head]
        tile = slice(start, start + rows)
        return dot_nt(keys, queries[tile]), dot_nt(values, grads[tile])

    def weigh(scores, grad_probs, start):
        lanes = lane_ids[:, start : start + rows]
        scores = [
            part + jnp.where(lanes == slot_id, 0.0, MASKED)
            for part, slot_id in zip(per_slot(scores), slot_ids)
        ]
        row_max = over_slots(jnp.max, jnp.maximum, scores)
        weights = [jnp.exp2((part - row_max) * EXP2_SCALE) for part in scores]
        inverse = 1.0 / over_slots(jnp.sum, jnp.add, weights)
        probs = [part * inverse for part in weights]
        grad_probs = per_slot(grad_probs)
        inner = over_slots(jnp.sum, jnp.add, [p * g for p, g in zip(probs, grad_probs)])
        low = jnp.concatenate([p.astype(jnp.bfloat16) for p in probs])
        grad_scores = [(p * (g - inner)).astype(jnp.bfloat16) for p, g in zip(probs, grad_probs)]
        return low, jnp.concatenate(grad_scores)

    def finish(head, low, grad_scores, start):
        queries, keys, values, grads = heads[head]
        tile = slice(start, start + rows)
        result = results[head]
        if start == 0:
            result[0] = dot_tn(values, low).astype(jnp.bfloat16).T
            result[1] = (dot_tn(keys, grad_scores) * SCALE).astype(jnp.bfloat16).T
            result[2] = result[3] = 0.0
        result[2] += dot_nn(grad_scores[:rows], queries[tile])
        result[3] += dot_nn(low[:rows], grads[tile])

    results = [[None] * 4 for _ in heads]
    work = [(head, start) for head in range(len(heads)) for start in range(0, size, rows)]
    ahead, behind = products(*work[0]), None
    for number, (head, start) in enumerate(work):
        scores, grad_probs = ahead
        if number + 1 < len(work):
            ahead = products(*work[number + 1])
        if behind is not None:
            finish(*behind)
        behind = (head, *weigh(scores, grad_probs, start), start)
    finish(*behind)
    for result in results:
        result[2] = (result[2] * SCALE).astype(jnp.bfloat16)
        result[3] = result[3].astype(jnp.bfloat16)
    return results


def attend_kernel(parts, part_rows, steps, width, offsets, has_outs, *refs):
    image_ids, mine, sides = refs[0], refs[1:4], (refs[4:7], refs[7:10])
    refs = refs[10 + (4 if has_outs else 0) :]
    outs, (window, lane_ids, slot_of, table, sems) = refs[:4], refs[4:]
    rows = parts * part_rows
    most = 3 * rows
    last = parts - 1
    me = lax.axis_index("tensor")
    step = pl.program_id(0)

    def copy_of(group, flip, number, place, sem):
        kind = 0 if flip == 0 else 2 if flip == last else 1
        buffer = lax.rem(number, 2)
        start = pl.multiple_of(place * part_rows, part_rows)
        column = pl.multiple_of(number * width + offsets[kind] * HD, HD)
        source = group[kind].at[flip - 1] if kind == 1 else group[kind]
        return pltpu.make_async_copy(
            source.at[:, :, pl.ds(column, width)],
            window.at[buffer, :, pl.ds(start, part_rows), :],
            sems.at[buffer, sem],
        )

    def own_copies(number, act):
        for flip in range(parts):
            act(copy_of(mine, flip, number, me ^ flip, flip))

    def other_copies(number, act):
        for source in range(2 * parts):
            slot = slot_of[source]

            @pl.when(slot >= 0)
            def _():
                group = sides[source // parts]
                act(copy_of(group, source % parts, number, parts + slot, parts + source))

    @pl.when(step == 0)
    def _():
        own_copies(0, lambda copy: copy.start())
        count = jnp.int32(0)
        for slot in range(2 * parts):
            table[slot] = -2
        for source in range(2 * parts):
            side, flip = 1 + source // parts, source % parts
            other_id = image_ids[side, me ^ flip]
            shared = other_id == image_ids[0, 0]
            for part in range(1, parts):
                shared = shared | (other_id == image_ids[0, part])
            slot_of[source] = jnp.where(shared, count, -1)
            table[count] = jnp.where(shared, other_id, -2)
            count = count + shared.astype(jnp.int32)
        table[2 * parts] = count
        other_copies(0, lambda copy: copy.start())
        for slot in range(2 * parts):

            @pl.when((slot >= count) & (slot < (count + parts - 1) // parts * parts))
            def _():
                place = slice(rows + slot * part_rows, rows + (slot + 1) * part_rows)
                window[:, :, place] = jnp.zeros((2, 4, part_rows, width), window.dtype)

        place = lax.broadcasted_iota(jnp.int32, (8, most), 1)
        ids = jnp.full((8, most), -2, jnp.int32)
        for slot in range(3 * parts):
            slot_id = image_ids[0, slot] if slot < parts else table[slot - parts]
            inside = (place >= slot * part_rows) & (place < (slot + 1) * part_rows)
            ids = jnp.where(inside, slot_id, ids)
        lane_ids[...] = ids

    @pl.when(step + 1 < steps)
    def _():
        own_copies(step + 1, lambda copy: copy.start())
        other_copies(step + 1, lambda copy: copy.start())

    own_copies(step, lambda copy: copy.wait())
    other_copies(step, lambda copy: copy.wait())
    count = table[2 * parts]
    buffer = lax.rem(step, 2)
    for size in range(rows, most + 1, rows):
        slots = (size - rows) // part_rows

        @pl.when((count <= slots) & (count > slots - parts))
        def _():
            slot_ids = [image_ids[0, slot] for slot in range(parts)]
            slot_ids += [table[slot] for slot in range(slots)]
            spans = [slice(start, start + HD) for start in range(0, width, HD)]
            heads = [[window[buffer, i, :size, span] for i in range(4)] for span in spans]
            results = attend_heads(heads, slot_ids, lane_ids[0:1], part_rows, rows)
            for span, result in zip(spans, results):
                for out, part in zip(outs, result):
                    out[:, span] = part


def attend(image_ids, groups, offsets, outs, first_head, heads):
    _, part_rows, total = groups[0][0].shape
    parts = groups[0][1].shape[0] + 2
    rows = parts * part_rows
    width = HD * math.gcd(2, math.gcd(first_head, heads))
    steps = heads * HD // width
    first_block = first_head * HD // width
    out_spec = pl.BlockSpec((rows, width), lambda s: (0, s + first_block))
    has_outs = outs is not None
    pieces = [piece for group in groups for piece in group]
    aliases = {1 + len(pieces) + i: i for i in range(4)} if has_outs else {}
    return pl.pallas_call(
        functools.partial(
            attend_kernel, parts, part_rows, steps, width, offsets, has_outs
        ),
        grid=(steps,),
        out_shape=[jax.ShapeDtypeStruct((rows, total), jnp.bfloat16)] * 4,
        in_specs=[pl.BlockSpec(memory_space=pltpu.SMEM)]
        + [pl.BlockSpec(memory_space=pl.ANY)] * (len(pieces) + (4 if has_outs else 0)),
        out_specs=[out_spec] * 4,
        scratch_shapes=[
            pltpu.VMEM((2, 4, 3 * rows, width), jnp.bfloat16),
            pltpu.VMEM((8, 3 * rows), jnp.int32),
            pltpu.SMEM((2 * parts,), jnp.int32),
            pltpu.SMEM((2 * parts + 1,), jnp.int32),
            pltpu.SemaphoreType.DMA((2, 3 * parts)),
        ],
        input_output_aliases=aliases,
        compiler_params=pltpu.CompilerParams(
            dimension_semantics=("arbitrary",), vmem_limit_bytes=VMEM_LIMIT
        ),
        cost_estimate=pl.CostEstimate(
            flops=heads * ATTEND_FLOPS, bytes_accessed=1, transcendentals=0
        ),
    )(image_ids, *pieces, *(outs or ()))


def between(sent, received):
    flops = FLOPS_PER_BYTE * (2 * sent.size - received.size)
    return pl.CostEstimate(flops=flops, bytes_accessed=1, transcendentals=0)


def shards(queries, key_vectors, value_vectors, grad_output, image_ids):
    arrays = (queries, key_vectors, value_vectors, grad_output)
    parts = lax.axis_size("tensor")
    part_rows = queries.shape[0]
    head_total = queries.shape[1] // HD // parts
    near_ids = nearby_ids(image_ids, parts, part_rows)
    last = parts - 1
    spans = split_counts(head_total, [sum(shares) for shares in GROUPS])
    groups = []
    for (start, count), shares in zip(spans, GROUPS):
        groups.append([(start + first, size) for first, size in split_counts(count, shares)])

    jobs = []
    for span, chunks in zip(spans, groups):
        jobs += [(flip, *span) for flip in range(last - 1, 0, -1)]
        jobs += [(last, *chunk) for chunk in chunks]
    jobs.insert(last - 1, (0, 0, head_total))
    soon, later = jobs[:last], jobs[last:]
    packed = dict(zip(soon, pack(arrays, parts, soon)))
    packed.update(zip(later, pack(arrays, parts, later)))

    steps = []
    for span, chunks in zip(spans, groups):
        steps.append([(flip, *span) for flip in range(1, last)])
        steps += [[(last, *chunk)] for chunk in chunks]

    def cross(step, after, cost=SMALL_COST, late=()):
        held = [hold(packed[job], after, cost) if after else packed[job] for job in step]
        held = [hold(piece, late) if late else piece for piece in held]
        return held, [swap_flipped(piece, "tensor", job[0]) for job, piece in zip(step, held)]

    def spread(piece):
        return piece, swap_pairs(piece, "dp", 0), swap_pairs(piece, "dp", 1)

    _, crossed = cross(steps[0], [])
    sent = [spread(packed[(0, 0, head_total)])]
    outs, joined, number = None, None, 0
    for span, chunks in zip(spans, groups):
        for place in range(1 + len(chunks)):
            after = list(sent[-1][1 : 3 if number + 1 < len(steps) else 2])
            received, held = crossed, []
            number += 1
            if number < len(steps):
                late = sent[-1][1:] if number > 1 and place == 0 else ()
                cost = between(sent[-1][0], received[0]) if late else SMALL_COST
                held, crossed = cross(steps[number], [received[-1]], cost, late)
            elif outs is not None:
                after.append(outs[0])
            cost = between(sent[-1][0], received[0]) if number < len(steps) else SMALL_COST
            held.append(sent[-1][0])
            if place == 0:
                joined = spread(hold(join(received, held, cost), after))
                sent.append(joined)
                continue
            piece = spread(hold(hold(received[0], held, cost), after))
            sent.append(piece)
            first_head, count = chunks[place - 1]
            offsets = (first_head, first_head - span[0], 0)
            outs = attend(
                near_ids, list(zip(sent[0], joined, piece)), offsets, outs, first_head, count
            )
    return tuple(outs)


def solution(mesh):
    return jax.shard_map(
        shards,
        mesh=mesh,
        in_specs=(
            P(("dp", "tensor"), None),
            P(("dp", "tensor"), None),
            P(("dp", "tensor"), None),
            P(("dp", "tensor"), None),
            P(),
        ),
        out_specs=(P("dp", "tensor"), P("dp", "tensor"), P("dp", "tensor"), P("dp", "tensor")),
        check_vma=False,
    )
```

```python
import functools
import math

import jax
import jax.numpy as jnp
from jax import lax
from jax.experimental import pallas as pl
from jax.experimental.pallas import tpu as pltpu
from jax.sharding import PartitionSpec as P

HD = 128
SCALE = 1.0 / math.sqrt(HD)
EXP2_SCALE = SCALE * math.log2(math.e)
MASKED = -1e30
GROUPS = ((6,), (6,))
VMEM_LIMIT = 64 * 1024 * 1024 - 256 * 1024
ATTEND_FLOPS = 1_500_000_000
FLOPS_PER_BYTE = 52_000
SMALL_COST = pl.CostEstimate(flops=1, bytes_accessed=1, transcendentals=0)


def split_counts(total, shares):
    whole = sum(shares)
    edges = [round(total * sum(shares[:i]) / whole) for i in range(len(shares) + 1)]
    return [(a, b - a) for a, b in zip(edges[:-1], edges[1:]) if b > a]


def swap_pairs(block, axis, first):
    count = lax.axis_size(axis)
    route = []
    for low in range(first, count - 1, 2):
        route += [(low, low + 1), (low + 1, low)]
    return lax.ppermute(block, axis, route)


def swap_flipped(block, axis, flip):
    return lax.ppermute(block, axis, [(i, i ^ flip) for i in range(lax.axis_size(axis))])


def nearby_ids(image_ids, parts, part_rows):
    shard = lax.axis_index("dp")
    padded = jnp.pad(image_ids[::part_rows], (parts, parts), constant_values=-1)
    odd = lax.rem(shard, 2)

    def ids_of(other):
        return lax.dynamic_slice_in_dim(padded, (other + 1) * parts, parts)

    return jnp.stack((ids_of(shard), ids_of(shard + 1 - 2 * odd), ids_of(shard - 1 + 2 * odd)))


def columns(array, part, stride, first, width):
    start = pl.multiple_of(part * stride + first, HD)
    return array.at[:, pl.ds(start, width)]


def pack_kernel(stride, jobs, *refs):
    arrays, packed, (stage, in_sems, out_sems) = refs[:4], refs[4:-3], refs[-3:]
    me = lax.axis_index("tensor")
    loads, stores = [], []
    for number, (flip, first, count) in enumerate(jobs):
        for index, array in enumerate(arrays):
            load = pltpu.make_async_copy(
                columns(array, me ^ flip, stride, first * HD, count * HD),
                stage.at[flip, index, :, pl.ds(first * HD, count * HD)],
                in_sems.at[number * 4 + index],
            )
            load.start()
            loads.append(load)
    for number, (flip, first, count) in enumerate(jobs):
        for load in loads[number * 4 : number * 4 + 4]:
            load.wait()
        store = pltpu.make_async_copy(
            stage.at[flip, :, :, pl.ds(first * HD, count * HD)],
            packed[number],
            out_sems.at[number],
        )
        store.start()
        stores.append(store)
    for store in stores:
        store.wait()


def pack(arrays, parts, jobs):
    rows, total = arrays[0].shape
    stride = total // parts
    return pl.pallas_call(
        functools.partial(pack_kernel, stride, jobs),
        out_shape=[
            jax.ShapeDtypeStruct((4, rows, count * HD), jnp.bfloat16) for _, _, count in jobs
        ],
        in_specs=[pl.BlockSpec(memory_space=pl.ANY)] * 4,
        out_specs=[pl.BlockSpec(memory_space=pl.ANY)] * len(jobs),
        scratch_shapes=[
            pltpu.VMEM((parts, 4, rows, stride), jnp.bfloat16),
            pltpu.SemaphoreType.DMA((4 * len(jobs),)),
            pltpu.SemaphoreType.DMA((len(jobs),)),
        ],
        compiler_params=pltpu.CompilerParams(vmem_limit_bytes=VMEM_LIMIT),
        cost_estimate=SMALL_COST,
    )(*arrays)


def join_kernel(pieces, *refs):
    received, (joined, stage, in_sems, out_sems) = refs[:pieces], refs[-4:]
    loads, stores = [], []
    for piece in range(pieces):
        load = pltpu.make_async_copy(received[piece], stage.at[piece], in_sems.at[piece])
        load.start()
        loads.append(load)
    for piece in range(pieces):
        loads[piece].wait()
        store = pltpu.make_async_copy(stage.at[piece], joined.at[piece], out_sems.at[piece])
        store.start()
        stores.append(store)
    for store in stores:
        store.wait()


def join(received, after, cost):
    pieces = len(received)
    shape = (pieces,) + received[0].shape
    return pl.pallas_call(
        functools.partial(join_kernel, pieces),
        out_shape=jax.ShapeDtypeStruct(shape, jnp.bfloat16),
        in_specs=[pl.BlockSpec(memory_space=pl.ANY)] * (pieces + len(after)),
        out_specs=pl.BlockSpec(memory_space=pl.ANY),
        scratch_shapes=[
            pltpu.VMEM(shape, jnp.bfloat16),
            pltpu.SemaphoreType.DMA((pieces,)),
            pltpu.SemaphoreType.DMA((pieces,)),
        ],
        compiler_params=pltpu.CompilerParams(vmem_limit_bytes=VMEM_LIMIT),
        cost_estimate=cost,
    )(*received, *after)


def hold(array, after, cost=SMALL_COST):
    return pl.pallas_call(
        lambda *refs: None,
        out_shape=jax.ShapeDtypeStruct(array.shape, array.dtype),
        in_specs=[pl.BlockSpec(memory_space=pl.ANY)] * (1 + len(after)),
        out_specs=pl.BlockSpec(memory_space=pl.ANY),
        input_output_aliases={0: 0},
        compiler_params=pltpu.CompilerParams(vmem_limit_bytes=VMEM_LIMIT),
        cost_estimate=cost,
    )(array, *after)


def dot_nt(a, b):
    return lax.dot_general(a, b, (((1,), (1,)), ((), ())), preferred_element_type=jnp.float32)


def dot_tn(a, b):
    return lax.dot_general(a, b, (((0,), (0,)), ((), ())), preferred_element_type=jnp.float32)


def dot_nn(a, b):
    return jnp.dot(a, b, preferred_element_type=jnp.float32)


def attend_heads(heads, slot_ids, lane_ids, part_rows, rows):
    size = heads[0][0].shape[0]
    slots = size // part_rows

    def per_slot(array):
        return [array[slot * part_rows : (slot + 1) * part_rows] for slot in range(slots)]

    def over_slots(reduce, combine, arrays):
        total = reduce(arrays[0], axis=0, keepdims=True)
        for array in arrays[1:]:
            total = combine(total, reduce(array, axis=0, keepdims=True))
        return total

    def products(head, start):
        queries, keys, values, grads = heads[head]
        tile = slice(start, start + rows)
        return dot_nt(keys, queries[tile]), dot_nt(values, grads[tile])

    def weigh(scores, grad_probs, start):
        lanes = lane_ids[:, start : start + rows]
        scores = [
            part + jnp.where(lanes == slot_id, 0.0, MASKED)
            for part, slot_id in zip(per_slot(scores), slot_ids)
        ]
        row_max = over_slots(jnp.max, jnp.maximum, scores)
        weights = [jnp.exp2((part - row_max) * EXP2_SCALE) for part in scores]
        inverse = 1.0 / over_slots(jnp.sum, jnp.add, weights)
        probs = [part * inverse for part in weights]
        grad_probs = per_slot(grad_probs)
        inner = over_slots(jnp.sum, jnp.add, [p * g for p, g in zip(probs, grad_probs)])
        low = jnp.concatenate([p.astype(jnp.bfloat16) for p in probs])
        grad_scores = [(p * (g - inner)).astype(jnp.bfloat16) for p, g in zip(probs, grad_probs)]
        return low, jnp.concatenate(grad_scores)

    def finish(head, low, grad_scores, start):
        queries, keys, values, grads = heads[head]
        tile = slice(start, start + rows)
        result = results[head]
        if start == 0:
            result[0] = dot_tn(values, low).astype(jnp.bfloat16).T
            result[1] = (dot_tn(keys, grad_scores) * SCALE).astype(jnp.bfloat16).T
            result[2] = result[3] = 0.0
        result[2] += dot_nn(grad_scores[:rows], queries[tile])
        result[3] += dot_nn(low[:rows], grads[tile])

    results = [[None] * 4 for _ in heads]
    work = [(head, start) for head in range(len(heads)) for start in range(0, size, rows)]
    ahead, behind = products(*work[0]), None
    for number, (head, start) in enumerate(work):
        scores, grad_probs = ahead
        if number + 1 < len(work):
            ahead = products(*work[number + 1])
        if behind is not None:
            finish(*behind)
        behind = (head, *weigh(scores, grad_probs, start), start)
    finish(*behind)
    for result in results:
        result[2] = (result[2] * SCALE).astype(jnp.bfloat16)
        result[3] = result[3].astype(jnp.bfloat16)
    return results


def attend_kernel(parts, part_rows, steps, width, offsets, has_outs, *refs):
    image_ids, mine, sides = refs[0], refs[1:4], (refs[4:7], refs[7:10])
    refs = refs[10 + (4 if has_outs else 0) :]
    outs, (window, lane_ids, slot_of, table, sems) = refs[:4], refs[4:]
    rows = parts * part_rows
    most = 3 * rows
    last = parts - 1
    me = lax.axis_index("tensor")
    step = pl.program_id(0)

    def copy_of(group, flip, number, place, sem):
        kind = 0 if flip == 0 else 2 if flip == last else 1
        buffer = lax.rem(number, 2)
        start = pl.multiple_of(place * part_rows, part_rows)
        column = pl.multiple_of(number * width + offsets[kind] * HD, HD)
        source = group[kind].at[flip - 1] if kind == 1 else group[kind]
        return pltpu.make_async_copy(
            source.at[:, :, pl.ds(column, width)],
            window.at[buffer, :, pl.ds(start, part_rows), :],
            sems.at[buffer, sem],
        )

    def own_copies(number, act):
        for flip in range(parts):
            act(copy_of(mine, flip, number, me ^ flip, flip))

    def other_copies(number, act):
        for source in range(2 * parts):
            slot = slot_of[source]

            @pl.when(slot >= 0)
            def _():
                group = sides[source // parts]
                act(copy_of(group, source % parts, number, parts + slot, parts + source))

    @pl.when(step == 0)
    def _():
        own_copies(0, lambda copy: copy.start())
        count = jnp.int32(0)
        for slot in range(2 * parts):
            table[slot] = -2
        for source in range(2 * parts):
            side, flip = 1 + source // parts, source % parts
            other_id = image_ids[side, me ^ flip]
            shared = other_id == image_ids[0, 0]
            for part in range(1, parts):
                shared = shared | (other_id == image_ids[0, part])
            slot_of[source] = jnp.where(shared, count, -1)
            table[count] = jnp.where(shared, other_id, -2)
            count = count + shared.astype(jnp.int32)
        table[2 * parts] = count
        other_copies(0, lambda copy: copy.start())
        for slot in range(2 * parts):

            @pl.when((slot >= count) & (slot < (count + parts - 1) // parts * parts))
            def _():
                place = slice(rows + slot * part_rows, rows + (slot + 1) * part_rows)
                window[:, :, place] = jnp.zeros((2, 4, part_rows, width), window.dtype)

        place = lax.broadcasted_iota(jnp.int32, (8, most), 1)
        ids = jnp.full((8, most), -2, jnp.int32)
        for slot in range(3 * parts):
            slot_id = image_ids[0, slot] if slot < parts else table[slot - parts]
            inside = (place >= slot * part_rows) & (place < (slot + 1) * part_rows)
            ids = jnp.where(inside, slot_id, ids)
        lane_ids[...] = ids

    @pl.when(step + 1 < steps)
    def _():
        own_copies(step + 1, lambda copy: copy.start())
        other_copies(step + 1, lambda copy: copy.start())

    own_copies(step, lambda copy: copy.wait())
    other_copies(step, lambda copy: copy.wait())
    count = table[2 * parts]
    buffer = lax.rem(step, 2)
    for size in range(rows, most + 1, rows):
        slots = (size - rows) // part_rows

        @pl.when((count <= slots) & (count > slots - parts))
        def _():
            slot_ids = [image_ids[0, slot] for slot in range(parts)]
            slot_ids += [table[slot] for slot in range(slots)]
            spans = [slice(start, start + HD) for start in range(0, width, HD)]
            heads = [[window[buffer, i, :size, span] for i in range(4)] for span in spans]
            results = attend_heads(heads, slot_ids, lane_ids[0:1], part_rows, rows)
            for span, result in zip(spans, results):
                for out, part in zip(outs, result):
                    out[:, span] = part


def attend(image_ids, groups, offsets, outs, first_head, heads):
    _, part_rows, total = groups[0][0].shape
    parts = groups[0][1].shape[0] + 2
    rows = parts * part_rows
    width = HD * math.gcd(2, math.gcd(first_head, heads))
    steps = heads * HD // width
    first_block = first_head * HD // width
    out_spec = pl.BlockSpec((rows, width), lambda s: (0, s + first_block))
    has_outs = outs is not None
    pieces = [piece for group in groups for piece in group]
    aliases = {1 + len(pieces) + i: i for i in range(4)} if has_outs else {}
    return pl.pallas_call(
        functools.partial(
            attend_kernel, parts, part_rows, steps, width, offsets, has_outs
        ),
        grid=(steps,),
        out_shape=[jax.ShapeDtypeStruct((rows, total), jnp.bfloat16)] * 4,
        in_specs=[pl.BlockSpec(memory_space=pltpu.SMEM)]
        + [pl.BlockSpec(memory_space=pl.ANY)] * (len(pieces) + (4 if has_outs else 0)),
        out_specs=[out_spec] * 4,
        scratch_shapes=[
            pltpu.VMEM((2, 4, 3 * rows, width), jnp.bfloat16),
            pltpu.VMEM((8, 3 * rows), jnp.int32),
            pltpu.SMEM((2 * parts,), jnp.int32),
            pltpu.SMEM((2 * parts + 1,), jnp.int32),
            pltpu.SemaphoreType.DMA((2, 3 * parts)),
        ],
        input_output_aliases=aliases,
        compiler_params=pltpu.CompilerParams(
            dimension_semantics=("arbitrary",), vmem_limit_bytes=VMEM_LIMIT
        ),
        cost_estimate=pl.CostEstimate(
            flops=heads * ATTEND_FLOPS, bytes_accessed=1, transcendentals=0
        ),
    )(image_ids, *pieces, *(outs or ()))


def between(sent, received):
    flops = FLOPS_PER_BYTE * (2 * sent.size - received.size)
    return pl.CostEstimate(flops=flops, bytes_accessed=1, transcendentals=0)


def shards(queries, key_vectors, value_vectors, grad_output, image_ids):
    arrays = (queries, key_vectors, value_vectors, grad_output)
    parts = lax.axis_size("tensor")
    part_rows = queries.shape[0]
    head_total = queries.shape[1] // HD // parts
    near_ids = nearby_ids(image_ids, parts, part_rows)
    last = parts - 1
    spans = split_counts(head_total, [sum(shares) for shares in GROUPS])
    groups = []
    for (start, count), shares in zip(spans, GROUPS):
        groups.append([(start + first, size) for first, size in split_counts(count, shares)])

    jobs = []
    for span, chunks in zip(spans, groups):
        jobs += [(flip, *span) for flip in range(last - 1, 0, -1)]
        jobs += [(last, *chunk) for chunk in chunks]
    jobs.insert(last - 1, (0, 0, head_total))
    soon, later = jobs[:last], jobs[last:]
    packed = dict(zip(soon, pack(arrays, parts, soon)))
    packed.update(zip(later, pack(arrays, parts, later)))

    steps = []
    for span, chunks in zip(spans, groups):
        steps.append([(flip, *span) for flip in range(1, last)])
        steps += [[(last, *chunk)] for chunk in chunks]

    def cross(step, after, cost=SMALL_COST, late=()):
        held = [hold(packed[job], after, cost) if after else packed[job] for job in step]
        held = [hold(piece, late) if late else piece for piece in held]
        order = list(zip(step, held))
        order = order[::-1] if after else order
        crossed = [swap_flipped(piece, "tensor", job[0]) for job, piece in order]
        return held, crossed[::-1] if after else crossed

    def spread(piece):
        return piece, swap_pairs(piece, "dp", 0), swap_pairs(piece, "dp", 1)

    _, crossed = cross(steps[0], [])
    sent = [spread(packed[(0, 0, head_total)])]
    outs, joined, number = None, None, 0
    for span, chunks in zip(spans, groups):
        for place in range(1 + len(chunks)):
            after = list(sent[-1][1 : 3 if number + 1 < len(steps) else 2])
            received, held = crossed, []
            number += 1
            if number < len(steps):
                late = sent[-1][1:] if number > 1 and place == 0 else ()
                cost = between(sent[-1][0], received[0]) if late else SMALL_COST
                held, crossed = cross(steps[number], [received[-1]], cost, late)
            elif outs is not None:
                after.append(outs[0])
            cost = between(sent[-1][0], received[0]) if number < len(steps) else SMALL_COST
            held.append(sent[-1][0])
            if place == 0:
                joined = spread(hold(join(received, held, cost), after))
                sent.append(joined)
                continue
            piece = spread(hold(hold(received[0], held, cost), after))
            sent.append(piece)
            first_head, count = chunks[place - 1]
            offsets = (first_head, first_head - span[0], 0)
            outs = attend(
                near_ids, list(zip(sent[0], joined, piece)), offsets, outs, first_head, count
            )
    return tuple(outs)


def solution(mesh):
    return jax.shard_map(
        shards,
        mesh=mesh,
        in_specs=(
            P(("dp", "tensor"), None),
            P(("dp", "tensor"), None),
            P(("dp", "tensor"), None),
            P(("dp", "tensor"), None),
            P(),
        ),
        out_specs=(P("dp", "tensor"), P("dp", "tensor"), P("dp", "tensor"), P("dp", "tensor")),
        check_vma=False,
    )
```

```python
import functools
import math

import jax
import jax.numpy as jnp
from jax import lax
from jax.experimental import pallas as pl
from jax.experimental.pallas import tpu as pltpu
from jax.sharding import PartitionSpec as P

HD = 128
SCALE = 1.0 / math.sqrt(HD)
EXP2_SCALE = SCALE * math.log2(math.e)
MASKED = -1e30
GROUPS = ((6,), (6,))
VMEM_LIMIT = 64 * 1024 * 1024 - 256 * 1024
ATTEND_FLOPS = 1_500_000_000
FLOPS_PER_BYTE = 52_000
SMALL_COST = pl.CostEstimate(flops=1, bytes_accessed=1, transcendentals=0)


def split_counts(total, shares):
    whole = sum(shares)
    edges = [round(total * sum(shares[:i]) / whole) for i in range(len(shares) + 1)]
    return [(a, b - a) for a, b in zip(edges[:-1], edges[1:]) if b > a]


def swap_pairs(block, axis, first):
    count = lax.axis_size(axis)
    route = []
    for low in range(first, count - 1, 2):
        route += [(low, low + 1), (low + 1, low)]
    return lax.ppermute(block, axis, route)


def swap_flipped(block, axis, flip):
    return lax.ppermute(block, axis, [(i, i ^ flip) for i in range(lax.axis_size(axis))])


def nearby_ids(image_ids, parts, part_rows):
    shard = lax.axis_index("dp")
    padded = jnp.pad(image_ids[::part_rows], (parts, parts), constant_values=-1)
    odd = lax.rem(shard, 2)

    def ids_of(other):
        return lax.dynamic_slice_in_dim(padded, (other + 1) * parts, parts)

    return jnp.stack((ids_of(shard), ids_of(shard + 1 - 2 * odd), ids_of(shard - 1 + 2 * odd)))


def columns(array, part, stride, first, width):
    start = pl.multiple_of(part * stride + first, HD)
    return array.at[:, pl.ds(start, width)]


def pack_kernel(stride, jobs, *refs):
    arrays, packed, (stage, in_sems, out_sems) = refs[:4], refs[4:-3], refs[-3:]
    me = lax.axis_index("tensor")
    loads, stores = [], []
    for number, (flip, first, count) in enumerate(jobs):
        for index, array in enumerate(arrays):
            load = pltpu.make_async_copy(
                columns(array, me ^ flip, stride, first * HD, count * HD),
                stage.at[flip, index, :, pl.ds(first * HD, count * HD)],
                in_sems.at[number * 4 + index],
            )
            load.start()
            loads.append(load)
    for number, (flip, first, count) in enumerate(jobs):
        for load in loads[number * 4 : number * 4 + 4]:
            load.wait()
        store = pltpu.make_async_copy(
            stage.at[flip, :, :, pl.ds(first * HD, count * HD)],
            packed[number],
            out_sems.at[number],
        )
        store.start()
        stores.append(store)
    for store in stores:
        store.wait()


def pack(arrays, parts, jobs):
    rows, total = arrays[0].shape
    stride = total // parts
    return pl.pallas_call(
        functools.partial(pack_kernel, stride, jobs),
        out_shape=[
            jax.ShapeDtypeStruct((4, rows, count * HD), jnp.bfloat16) for _, _, count in jobs
        ],
        in_specs=[pl.BlockSpec(memory_space=pl.ANY)] * 4,
        out_specs=[pl.BlockSpec(memory_space=pl.ANY)] * len(jobs),
        scratch_shapes=[
            pltpu.VMEM((parts, 4, rows, stride), jnp.bfloat16),
            pltpu.SemaphoreType.DMA((4 * len(jobs),)),
            pltpu.SemaphoreType.DMA((len(jobs),)),
        ],
        compiler_params=pltpu.CompilerParams(vmem_limit_bytes=VMEM_LIMIT),
        cost_estimate=SMALL_COST,
    )(*arrays)


def join_kernel(pieces, *refs):
    received, (joined, stage, in_sems, out_sems) = refs[:pieces], refs[-4:]
    loads, stores = [], []
    for piece in range(pieces):
        load = pltpu.make_async_copy(received[piece], stage.at[piece], in_sems.at[piece])
        load.start()
        loads.append(load)
    for piece in range(pieces):
        loads[piece].wait()
        store = pltpu.make_async_copy(stage.at[piece], joined.at[piece], out_sems.at[piece])
        store.start()
        stores.append(store)
    for store in stores:
        store.wait()


def join(received, after, cost):
    pieces = len(received)
    shape = (pieces,) + received[0].shape
    return pl.pallas_call(
        functools.partial(join_kernel, pieces),
        out_shape=jax.ShapeDtypeStruct(shape, jnp.bfloat16),
        in_specs=[pl.BlockSpec(memory_space=pl.ANY)] * (pieces + len(after)),
        out_specs=pl.BlockSpec(memory_space=pl.ANY),
        scratch_shapes=[
            pltpu.VMEM(shape, jnp.bfloat16),
            pltpu.SemaphoreType.DMA((pieces,)),
            pltpu.SemaphoreType.DMA((pieces,)),
        ],
        compiler_params=pltpu.CompilerParams(vmem_limit_bytes=VMEM_LIMIT),
        cost_estimate=cost,
    )(*received, *after)


def hold(array, after, cost=SMALL_COST):
    return pl.pallas_call(
        lambda *refs: None,
        out_shape=jax.ShapeDtypeStruct(array.shape, array.dtype),
        in_specs=[pl.BlockSpec(memory_space=pl.ANY)] * (1 + len(after)),
        out_specs=pl.BlockSpec(memory_space=pl.ANY),
        input_output_aliases={0: 0},
        compiler_params=pltpu.CompilerParams(vmem_limit_bytes=VMEM_LIMIT),
        cost_estimate=cost,
    )(array, *after)


def dot_nt(a, b):
    return lax.dot_general(a, b, (((1,), (1,)), ((), ())), preferred_element_type=jnp.float32)


def dot_tn(a, b):
    return lax.dot_general(a, b, (((0,), (0,)), ((), ())), preferred_element_type=jnp.float32)


def dot_nn(a, b):
    return jnp.dot(a, b, preferred_element_type=jnp.float32)


def attend_heads(heads, slot_ids, lane_ids, part_rows, rows):
    size = heads[0][0].shape[0]
    slots = size // part_rows

    def per_slot(array):
        return [array[slot * part_rows : (slot + 1) * part_rows] for slot in range(slots)]

    def over_slots(reduce, combine, arrays):
        total = reduce(arrays[0], axis=0, keepdims=True)
        for array in arrays[1:]:
            total = combine(total, reduce(array, axis=0, keepdims=True))
        return total

    def products(head, start):
        queries, keys, values, grads = heads[head]
        tile = slice(start, start + rows)
        return dot_nt(keys, queries[tile]), dot_nt(values, grads[tile])

    def weigh(scores, grad_probs, start):
        lanes = lane_ids[:, start : start + rows]
        scores = [
            part + jnp.where(lanes == slot_id, 0.0, MASKED)
            for part, slot_id in zip(per_slot(scores), slot_ids)
        ]
        row_max = over_slots(jnp.max, jnp.maximum, scores)
        weights = [jnp.exp2((part - row_max) * EXP2_SCALE) for part in scores]
        inverse = 1.0 / over_slots(jnp.sum, jnp.add, weights)
        probs = [part * inverse for part in weights]
        grad_probs = per_slot(grad_probs)
        inner = over_slots(jnp.sum, jnp.add, [p * g for p, g in zip(probs, grad_probs)])
        low = jnp.concatenate([p.astype(jnp.bfloat16) for p in probs])
        grad_scores = [(p * (g - inner)).astype(jnp.bfloat16) for p, g in zip(probs, grad_probs)]
        return low, jnp.concatenate(grad_scores)

    def finish(head, low, grad_scores, start):
        queries, keys, values, grads = heads[head]
        tile = slice(start, start + rows)
        result = results[head]
        if start == 0:
            result[0] = dot_tn(values, low).astype(jnp.bfloat16).T
            result[1] = (dot_tn(keys, grad_scores) * SCALE).astype(jnp.bfloat16).T
            result[2] = result[3] = 0.0
        result[2] += dot_nn(grad_scores[:rows], queries[tile])
        result[3] += dot_nn(low[:rows], grads[tile])

    results = [[None] * 4 for _ in heads]
    work = [(head, start) for head in range(len(heads)) for start in range(0, size, rows)]
    ahead, behind = products(*work[0]), None
    for number, (head, start) in enumerate(work):
        scores, grad_probs = ahead
        if number + 1 < len(work):
            ahead = products(*work[number + 1])
        if behind is not None:
            finish(*behind)
        behind = (head, *weigh(scores, grad_probs, start), start)
    finish(*behind)
    for result in results:
        result[2] = (result[2] * SCALE).astype(jnp.bfloat16)
        result[3] = result[3].astype(jnp.bfloat16)
    return results


def attend_kernel(parts, part_rows, steps, width, offsets, has_outs, *refs):
    image_ids, mine, sides = refs[0], refs[1:4], (refs[4:7], refs[7:10])
    refs = refs[10 + (4 if has_outs else 0) :]
    outs, (window, lane_ids, slot_of, table, sems) = refs[:4], refs[4:]
    rows = parts * part_rows
    most = 3 * rows
    last = parts - 1
    me = lax.axis_index("tensor")
    step = pl.program_id(0)

    def copy_of(group, flip, number, place, sem):
        kind = 0 if flip == 0 else 2 if flip == last else 1
        buffer = lax.rem(number, 2)
        start = pl.multiple_of(place * part_rows, part_rows)
        column = pl.multiple_of(number * width + offsets[kind] * HD, HD)
        source = group[kind].at[flip - 1] if kind == 1 else group[kind]
        return pltpu.make_async_copy(
            source.at[:, :, pl.ds(column, width)],
            window.at[buffer, :, pl.ds(start, part_rows), :],
            sems.at[buffer, sem],
        )

    def own_copies(number, act):
        for flip in range(parts):
            act(copy_of(mine, flip, number, me ^ flip, flip))

    def other_copies(number, act):
        for source in range(2 * parts):
            slot = slot_of[source]

            @pl.when(slot >= 0)
            def _():
                group = sides[source // parts]
                act(copy_of(group, source % parts, number, parts + slot, parts + source))

    @pl.when(step == 0)
    def _():
        own_copies(0, lambda copy: copy.start())
        count = jnp.int32(0)
        for slot in range(2 * parts):
            table[slot] = -2
        for source in range(2 * parts):
            side, flip = 1 + source // parts, source % parts
            other_id = image_ids[side, me ^ flip]
            shared = other_id == image_ids[0, 0]
            for part in range(1, parts):
                shared = shared | (other_id == image_ids[0, part])
            slot_of[source] = jnp.where(shared, count, -1)
            table[count] = jnp.where(shared, other_id, -2)
            count = count + shared.astype(jnp.int32)
        table[2 * parts] = count
        other_copies(0, lambda copy: copy.start())
        for slot in range(2 * parts):

            @pl.when((slot >= count) & (slot < (count + parts - 1) // parts * parts))
            def _():
                place = slice(rows + slot * part_rows, rows + (slot + 1) * part_rows)
                window[:, :, place] = jnp.zeros((2, 4, part_rows, width), window.dtype)

        place = lax.broadcasted_iota(jnp.int32, (8, most), 1)
        ids = jnp.full((8, most), -2, jnp.int32)
        for slot in range(3 * parts):
            slot_id = image_ids[0, slot] if slot < parts else table[slot - parts]
            inside = (place >= slot * part_rows) & (place < (slot + 1) * part_rows)
            ids = jnp.where(inside, slot_id, ids)
        lane_ids[...] = ids

    @pl.when(step + 1 < steps)
    def _():
        own_copies(step + 1, lambda copy: copy.start())
        other_copies(step + 1, lambda copy: copy.start())

    own_copies(step, lambda copy: copy.wait())
    other_copies(step, lambda copy: copy.wait())
    count = table[2 * parts]
    buffer = lax.rem(step, 2)
    for size in range(rows, most + 1, rows):
        slots = (size - rows) // part_rows

        @pl.when((count <= slots) & (count > slots - parts))
        def _():
            slot_ids = [image_ids[0, slot] for slot in range(parts)]
            slot_ids += [table[slot] for slot in range(slots)]
            spans = [slice(start, start + HD) for start in range(0, width, HD)]
            heads = [[window[buffer, i, :size, span] for i in range(4)] for span in spans]
            results = attend_heads(heads, slot_ids, lane_ids[0:1], part_rows, rows)
            for span, result in zip(spans, results):
                for out, part in zip(outs, result):
                    out[:, span] = part


def attend(image_ids, groups, offsets, outs, first_head, heads):
    _, part_rows, total = groups[0][0].shape
    parts = groups[0][1].shape[0] + 2
    rows = parts * part_rows
    shared = math.gcd(first_head, heads)
    width = HD * next(count for count in (3, 2, 1) if shared % count == 0)
    steps = heads * HD // width
    first_block = first_head * HD // width
    out_spec = pl.BlockSpec((rows, width), lambda s: (0, s + first_block))
    has_outs = outs is not None
    pieces = [piece for group in groups for piece in group]
    aliases = {1 + len(pieces) + i: i for i in range(4)} if has_outs else {}
    return pl.pallas_call(
        functools.partial(
            attend_kernel, parts, part_rows, steps, width, offsets, has_outs
        ),
        grid=(steps,),
        out_shape=[jax.ShapeDtypeStruct((rows, total), jnp.bfloat16)] * 4,
        in_specs=[pl.BlockSpec(memory_space=pltpu.SMEM)]
        + [pl.BlockSpec(memory_space=pl.ANY)] * (len(pieces) + (4 if has_outs else 0)),
        out_specs=[out_spec] * 4,
        scratch_shapes=[
            pltpu.VMEM((2, 4, 3 * rows, width), jnp.bfloat16),
            pltpu.VMEM((8, 3 * rows), jnp.int32),
            pltpu.SMEM((2 * parts,), jnp.int32),
            pltpu.SMEM((2 * parts + 1,), jnp.int32),
            pltpu.SemaphoreType.DMA((2, 3 * parts)),
        ],
        input_output_aliases=aliases,
        compiler_params=pltpu.CompilerParams(
            dimension_semantics=("arbitrary",), vmem_limit_bytes=VMEM_LIMIT
        ),
        cost_estimate=pl.CostEstimate(
            flops=heads * ATTEND_FLOPS, bytes_accessed=1, transcendentals=0
        ),
    )(image_ids, *pieces, *(outs or ()))


def between(sent, received):
    flops = FLOPS_PER_BYTE * (2 * sent.size - received.size)
    return pl.CostEstimate(flops=flops, bytes_accessed=1, transcendentals=0)


def shards(queries, key_vectors, value_vectors, grad_output, image_ids):
    arrays = (queries, key_vectors, value_vectors, grad_output)
    parts = lax.axis_size("tensor")
    part_rows = queries.shape[0]
    head_total = queries.shape[1] // HD // parts
    near_ids = nearby_ids(image_ids, parts, part_rows)
    last = parts - 1
    spans = split_counts(head_total, [sum(shares) for shares in GROUPS])
    groups = []
    for (start, count), shares in zip(spans, GROUPS):
        groups.append([(start + first, size) for first, size in split_counts(count, shares)])

    jobs = []
    for span, chunks in zip(spans, groups):
        jobs += [(flip, *span) for flip in range(last - 1, 0, -1)]
        jobs += [(last, *chunk) for chunk in chunks]
    jobs.insert(last - 1, (0, 0, head_total))
    soon, later = jobs[:last], jobs[last:]
    packed = dict(zip(soon, pack(arrays, parts, soon)))
    packed.update(zip(later, pack(arrays, parts, later)))

    steps = []
    for span, chunks in zip(spans, groups):
        steps.append([(flip, *span) for flip in range(1, last)])
        steps += [[(last, *chunk)] for chunk in chunks]

    def cross(step, after, cost=SMALL_COST, late=()):
        held = [hold(packed[job], after, cost) if after else packed[job] for job in step]
        held = [hold(piece, late) if late else piece for piece in held]
        return held, [swap_flipped(piece, "tensor", job[0]) for job, piece in zip(step, held)]

    def spread(piece):
        return piece, swap_pairs(piece, "dp", 0), swap_pairs(piece, "dp", 1)

    _, crossed = cross(steps[0], [])
    sent = [spread(packed[(0, 0, head_total)])]
    outs, joined, number = None, None, 0
    for span, chunks in zip(spans, groups):
        for place in range(1 + len(chunks)):
            after = list(sent[-1][1 : 3 if number + 1 < len(steps) else 2])
            received, held = crossed, []
            number += 1
            if number < len(steps):
                late = sent[-1][1:] if number > 1 and place == 0 else ()
                cost = between(sent[-1][0], received[0]) if late else SMALL_COST
                held, crossed = cross(steps[number], [received[-1]], cost, late)
            elif outs is not None:
                after.append(outs[0])
            cost = between(sent[-1][0], received[0]) if number < len(steps) else SMALL_COST
            held.append(sent[-1][0])
            if place == 0:
                joined = spread(hold(join(received, held, cost), after))
                sent.append(joined)
                continue
            piece = spread(hold(hold(received[0], held, cost), after))
            sent.append(piece)
            first_head, count = chunks[place - 1]
            offsets = (first_head, first_head - span[0], 0)
            outs = attend(
                near_ids, list(zip(sent[0], joined, piece)), offsets, outs, first_head, count
            )
    return tuple(outs)


def solution(mesh):
    return jax.shard_map(
        shards,
        mesh=mesh,
        in_specs=(
            P(("dp", "tensor"), None),
            P(("dp", "tensor"), None),
            P(("dp", "tensor"), None),
            P(("dp", "tensor"), None),
            P(),
        ),
        out_specs=(P("dp", "tensor"), P("dp", "tensor"), P("dp", "tensor"), P("dp", "tensor")),
        check_vma=False,
    )
```
